32 devices in a mesh: shard: 4 (over y, x), rep: 8 (over z, core).
Axes of the slice: x: 2, y: 2, z: 4, core: 2. Of those that a mesh axis runs over, the one named last changes fastest.
Arguments:
- tokens: bfloat16 [16384, 960], P(('rep', 'shard')), may hold values from -6 to 6
- cotangent: bfloat16 [16384, 960], P(('rep', 'shard')), may hold values from -6 to 6
- lengths: int32 [8, 4], P('rep'), may hold values from 1 to 1792, 2048 in all within a row
- qkv_copy: bfloat16 [960, 1600], P('shard'), may hold values from -0.1875 to 0.1875
- qkv_master: float32 [960, 1600], P('shard'), may hold values from -0.1875 to 0.1875
- qkv_first: float32 [960, 1600], P('shard'), may hold values from -448 to 448
- qkv_second: float32 [960, 1600], P('shard'), may hold values from 3932.16 to 15728.64
- proj_copy: bfloat16 [960, 960], P('shard'), may hold values from -3 to 3
- proj_master: float32 [960, 960], P('shard'), may hold values from -3 to 3
- proj_first: float32 [960, 960], P('shard'), may hold values from -56 to 56
- proj_second: float32 [960, 960], P('shard'), may hold values from 54.0672 to 212.992
- gateup_copy: bfloat16 [960, 5120], P('shard'), may hold values from -0.1875 to 0.1875
- gateup_master: float32 [960, 5120], P('shard'), may hold values from -0.1875 to 0.1875
- gateup_first: float32 [960, 5120], P('shard'), may hold values from -384 to 384
- gateup_second: float32 [960, 5120], P('shard'), may hold values from 2736.128 to 10928.128
- down_copy: bfloat16 [2560, 960], P('shard'), may hold values from -0.125 to 0.125
- down_master: float32 [2560, 960], P('shard'), may hold values from -0.125 to 0.125
- down_first: float32 [2560, 960], P('shard'), may hold values from -384 to 384
- down_second: float32 [2560, 960], P('shard'), may hold values from 2736.128 to 10928.128
- gain_copy: bfloat16 [2, 960], P(None, 'shard'), may hold values from 0.5 to 1.5
- gain_master: float32 [2, 960], P(None, 'shard'), may hold values from 0.5 to 1.5
- gain_first: float32 [2, 960], P(None, 'shard'), may hold values from -640 to 640
- gain_second: float32 [2, 960], P(None, 'shard'), may hold values from 6995.968 to 28016.64
Outputs:
- output: bfloat16 [16384, 960], P(('rep', 'shard'))
- input_grad: float32 [16384, 960], P(('rep', 'shard'))
- qkv_grad: float32 [960, 1600], P('shard')
- qkv_master_new: float32 [960, 1600], P('shard')
- qkv_copy_new: bfloat16 [960, 1600], P('shard')
- qkv_first_new: float32 [960, 1600], P('shard')
- qkv_second_new: float32 [960, 1600], P('shard')
- proj_grad: float32 [960, 960], P('shard')
- proj_master_new: float32 [960, 960], P('shard')
- proj_copy_new: bfloat16 [960, 960], P('shard')
- proj_first_new: float32 [960, 960], P('shard')
- proj_second_new: float32 [960, 960], P('shard')
- gateup_grad: float32 [960, 5120], P('shard')
- gateup_master_new: float32 [960, 5120], P('shard')
- gateup_copy_new: bfloat16 [960, 5120], P('shard')
- gateup_first_new: float32 [960, 5120], P('shard')
- gateup_second_new: float32 [960, 5120], P('shard')
- down_grad: float32 [2560, 960], P('shard')
- down_master_new: float32 [2560, 960], P('shard')
- down_copy_new: bfloat16 [2560, 960], P('shard')
- down_first_new: float32 [2560, 960], P('shard')
- down_second_new: float32 [2560, 960], P('shard')
- gain_grad: float32 [2, 960], P(None, 'shard')
- gain_master_new: float32 [2, 960], P(None, 'shard')
- gain_copy_new: bfloat16 [2, 960], P(None, 'shard')
- gain_first_new: float32 [2, 960], P(None, 'shard')
- gain_second_new: float32 [2, 960], P(None, 'shard')
The draws below stay inside these ranges and needn't reach their ends.
Inputs may be any that keep to these rules, and one draw needn't show every extreme that they name: In each row the 4 lengths sum to 2048, and the longest is exactly 1792 tokens.
All inputs are finite; a program needn't handle non-finite values.
Results may differ from the reference program's by a relative error of at most 0.014.
Values may be sent and summed in bfloat16 or wider, within the bound.
No kernel may reach another device: no remote copies, remote signals or barrier semaphores. Data moves between devices by JAX's collectives and lax.ppermute only.
A program may use at most 256 MiB of HBM per device.

```python
import math
import jax
import jax.numpy as jnp
import numpy as np
from jax import lax

D = 960
FF = 2560
HEADS = 15
KV_HEADS = 5
HEAD_DIM = 64
TOK_DEV = 512
DOCS = 4
BLOCK = 256
STEP = 10
QKV = 1600
ROW = 2048
ROWS = 8
TOKENS = 16384


def steps_of(own_key, dims, shards, smallest, top_value):
    level = 1.0
    for axis_at, shards_of in shards:
        heights = jax.random.uniform(jax.random.fold_in(jax.random.fold_in(own_key, 6), axis_at), (shards_of,), jnp.float32, smallest / len(shards), top_value / len(shards))
        level = level * jnp.repeat(jnp.exp(heights), dims[axis_at] // shards_of).reshape((-1,) + (1,) * (len(dims) - 1 - axis_at))
    return level


def length_profile(count, total, reach, slope):
    loads = [(1 << 20) // math.isqrt(rank ** slope) + 1 for rank in range(2, count + 1)]
    surplus, counts = total - reach - (count - 1), [1] * (count - 1)
    while surplus > 0:
        free = [i for i in range(count - 1) if counts[i] < reach]
        pool, budget = sum([loads[i] for i in free]), surplus
        for i in free:
            extra = min(reach - counts[i], max(1, budget * loads[i] // pool), surplus)
            counts[i] = counts[i] + extra
            surplus = surplus - extra
    return np.array([reach] + counts)


def uneven_parts(key, count, total, limit, slope):
    if count == 2:
        one = jax.random.randint(key, (), max(1, total - limit), min(limit, total - 1) + 1)
        return jnp.stack([one, total - one])
    tallies = jnp.asarray(length_profile(count, total, limit, slope), jnp.int32)
    pairs = (count - 1) // 2
    source_of, receiver = tallies[1:1 + 2 * pairs:2], tallies[2:2 + 2 * pairs:2]
    slack = jnp.minimum(source_of - 1, limit - receiver)
    moved = jax.random.randint(jax.random.fold_in(key, 1), (pairs,), 0, 1 << 20) % (slack + 1)
    tallies = tallies.at[1:1 + 2 * pairs:2].set(source_of - moved).at[2:2 + 2 * pairs:2].set(receiver + moved)
    return tallies[jax.random.permutation(jax.random.fold_in(key, 2), count)]


def centred(key, shape, spread, most, cuts=(), held_as=jnp.bfloat16):
    level = steps_of(key, shape, cuts, -0.22, 0.18) if cuts else 1.0
    values = jax.random.normal(key, shape, jnp.float32) * spread * level
    return jnp.minimum(jnp.maximum(values, -most), most).astype(held_as)


def setup_inputs(seed: int = 0) -> dict:
    key_of = jax.random.split(jax.random.key(seed), 24)
    tokens = centred(key_of[0], (TOKENS, D), 1.0, 6.0, ((0, 32),))
    cotangent = centred(key_of[1], (TOKENS, D), 1.0, 6.0, ((0, 32),))
    lengths = jax.vmap(lambda own: uneven_parts(own, DOCS, ROW, ROW - TOK_DEV // 2, 2))(jax.random.split(key_of[2], ROWS)).reshape((ROWS, DOCS)).astype(jnp.int32)
    qkv_copy = centred(key_of[3], (D, QKV), D ** -0.5, 0.1875, ((0, 4),))
    qkv_master = centred(key_of[4], (D, QKV), D ** -0.5, 0.1875, ((0, 4),), jnp.float32)
    qkv_first = centred(key_of[5], (D, QKV), (0.6 * TOKENS ** 0.5), 448.0, ((0, 4),), jnp.float32)
    qkv_second = jnp.clip(jnp.exp(math.log(15728.64) - 1.3862944 * jax.random.uniform(key_of[6], (D, QKV), jnp.float32) ** steps_of(key_of[6], (D, QKV), ((0, 4),), -0.2, 0.2)), 3932.16, 15728.64)
    proj_copy = centred(key_of[7], (D, D), (max(HEAD_DIM // 16, 1)) ** -0.5, 3.0, ((0, 4),))
    proj_master = centred(key_of[8], (D, D), (max(HEAD_DIM // 16, 1)) ** -0.5, 3.0, ((0, 4),), jnp.float32)
    proj_first = centred(key_of[9], (D, D), (0.07 * TOKENS ** 0.5), 56.0, ((0, 4),), jnp.float32)
    proj_second = jnp.clip(jnp.exp(math.log(212.992) - 1.3710269 * jax.random.uniform(key_of[10], (D, D), jnp.float32) ** steps_of(key_of[10], (D, D), ((0, 4),), -0.2, 0.2)), 54.0672, 212.992)
    gateup_copy = centred(key_of[11], (D, 2 * FF), D ** -0.5, 0.1875, ((0, 4),))
    gateup_master = centred(key_of[12], (D, 2 * FF), D ** -0.5, 0.1875, ((0, 4),), jnp.float32)
    gateup_first = centred(key_of[13], (D, 2 * FF), (0.5 * TOKENS ** 0.5), 384.0, ((0, 4),), jnp.float32)
    gateup_second = jnp.clip(jnp.exp(math.log(10928.128) - 1.3847963 * jax.random.uniform(key_of[14], (D, 2 * FF), jnp.float32) ** steps_of(key_of[14], (D, 2 * FF), ((0, 4),), -0.2, 0.2)), 2736.128, 10928.128)
    down_copy = centred(key_of[15], (FF, D), FF ** -0.5, 0.125, ((0, 4),))
    down_master = centred(key_of[16], (FF, D), FF ** -0.5, 0.125, ((0, 4),), jnp.float32)
    down_first = centred(key_of[17], (FF, D), (0.5 * TOKENS ** 0.5), 384.0, ((0, 4),), jnp.float32)
    down_second = jnp.clip(jnp.exp(math.log(10928.128) - 1.3847963 * jax.random.uniform(key_of[18], (FF, D), jnp.float32) ** steps_of(key_of[18], (FF, D), ((0, 4),), -0.2, 0.2)), 2736.128, 10928.128)
    gain_copy = jnp.clip(1.0 + 0.1 * jax.random.normal(key_of[19], (2, D), jnp.float32), 0.5, 1.5).astype(jnp.bfloat16)
    gain_master = jnp.clip(1.0 + 0.1 * jax.random.normal(key_of[20], (2, D), jnp.float32), 0.5, 1.5)
    gain_first = centred(key_of[21], (2, D), (0.8 * TOKENS ** 0.5), 640.0, ((1, 4),), jnp.float32)
    gain_second = jnp.clip(jnp.exp(math.log(28016.64) - 1.3874647 * jax.random.uniform(key_of[22], (2, D), jnp.float32) ** steps_of(key_of[22], (2, D), ((1, 4),), -0.2, 0.2)), 6995.968, 28016.64)
    return dict(tokens=tokens, cotangent=cotangent, lengths=lengths, qkv_copy=qkv_copy, qkv_master=qkv_master, qkv_first=qkv_first, qkv_second=qkv_second, proj_copy=proj_copy, proj_master=proj_master, proj_first=proj_first, proj_second=proj_second, gateup_copy=gateup_copy, gateup_master=gateup_master, gateup_first=gateup_first, gateup_second=gateup_second, down_copy=down_copy, down_master=down_master, down_first=down_first, down_second=down_second, gain_copy=gain_copy, gain_master=gain_master, gain_first=gain_first, gain_second=gain_second)


NORM_EPSILON = 1e-05
ROPE_THETA = 100000.0
MASKED_SCORE = -1e+30
BETA_FIRST = 0.5
BETA_SECOND = 0.6
ADAM_EPSILON = 1e-08
DECAY_RATE = 0.1

@jax.custom_vjp
def low(v):
    return lax.optimization_barrier(v.astype(jnp.bfloat16)).astype(jnp.float32)

@jax.custom_vjp
def low_back(v):
    return v

def low_keep(v):
    return (low(v), None)

def low_pass(kept, grad):
    return (grad,)

def back_keep(v):
    return (v, None)

def back_low(kept, grad):
    return (low(grad),)
low.defvjp(low_keep, low_pass)
low_back.defvjp(back_keep, back_low)

def product(left, right):
    return jnp.dot(left, right, precision=lax.Precision.HIGHEST, preferred_element_type=jnp.float32)

def row_layout(doc_lengths, token_count):
    doc_end = jnp.cumsum(doc_lengths, dtype=jnp.int32)
    starts = doc_end - doc_lengths
    places = jnp.arange(token_count, dtype=jnp.int32)
    inside = (places[:, None] >= starts[None, :]) & (places[:, None] < doc_end[None, :])
    doc_start = lax.optimization_barrier(jnp.sum(jnp.where(inside, starts[None, :], 0), axis=1, dtype=jnp.int32))
    return (doc_start, places - doc_start)

def rope_tables(position):
    half_dim = HEAD_DIM // 2
    frequency = ROPE_THETA ** (-2.0 * jnp.arange(half_dim, dtype=jnp.float32) / HEAD_DIM)
    angles = position.astype(jnp.float32)[:, None] * frequency[None, :]
    return (jnp.cos(angles), jnp.sin(angles))

def rotate(values, cosine_table, sine_table, head_count):
    shaped = values.reshape(values.shape[0], head_count, 2, HEAD_DIM // 2)
    first_half = shaped[:, :, 0]
    second = shaped[:, :, 1]
    cosine = cosine_table[:, None, :]
    sine = sine_table[:, None, :]
    turned = jnp.stack([first_half * cosine - second * sine, second * cosine + first_half * sine], axis=2)
    return turned.reshape(values.shape)

def attend(queries, key_rows, value_rows, allowed):
    token_count = queries.shape[0]
    group_size = HEADS // KV_HEADS
    query_groups = queries.reshape(token_count, KV_HEADS, group_size, HEAD_DIM).transpose(1, 2, 0, 3)
    key_groups = key_rows.reshape(token_count, KV_HEADS, HEAD_DIM).transpose(1, 0, 2)
    value_groups = value_rows.reshape(token_count, KV_HEADS, HEAD_DIM).transpose(1, 0, 2)

    def one_group(members):
        products = jnp.einsum('hqd,kd->hqk', members[0], members[1], precision=lax.Precision.HIGHEST)
        scores = jnp.where(allowed[None], low_back(products * HEAD_DIM ** (-0.5)), MASKED_SCORE)
        row_max = lax.optimization_barrier(jnp.max(scores, axis=-1, keepdims=True))
        log_total = row_max + jnp.log(lax.optimization_barrier(jnp.sum(jnp.exp(scores - row_max), axis=-1, keepdims=True)))
        weights = low(jnp.exp(scores - log_total))
        return jnp.einsum('hqk,kd->hqd', weights, members[2], precision=lax.Precision.HIGHEST)
    mixed_groups = lax.map(jax.checkpoint(one_group), (query_groups, key_groups, value_groups))
    return mixed_groups.transpose(2, 0, 1, 3).reshape(token_count, HEADS * HEAD_DIM)

def block_layer(x_float, w_qkv, w_proj, w_gateup, w_down, gains, doc_start, position):
    cosine_table, sine_table = rope_tables(position)
    block_index = position // BLOCK
    allowed = (doc_start[:, None] == doc_start[None, :]) & (block_index[None, :] <= block_index[:, None])
    query_width = HEADS * HEAD_DIM
    key_width = KV_HEADS * HEAD_DIM
    scale_one = lax.rsqrt(lax.optimization_barrier(jnp.mean(x_float * x_float, axis=-1, keepdims=True)) + NORM_EPSILON)
    normed_one = low(x_float * scale_one * gains[0])
    joined = low_back(product(normed_one, w_qkv))
    queries = low(rotate(joined[:, :query_width], cosine_table, sine_table, HEADS))
    key_rows = low(rotate(joined[:, query_width:query_width + key_width], cosine_table, sine_table, KV_HEADS))
    value_rows = low(joined[:, query_width + key_width:])
    mixed_heads = low_back(low(attend(queries, key_rows, value_rows, allowed)))
    residual = x_float + low_back(product(mixed_heads, w_proj))
    scale_two = lax.rsqrt(lax.optimization_barrier(jnp.mean(residual * residual, axis=-1, keepdims=True)) + NORM_EPSILON)
    normed_two = low(residual * scale_two * gains[1])
    gate_up = low_back(product(normed_two, w_gateup))
    activated = low(jax.nn.silu(gate_up[:, :FF]) * gate_up[:, FF:])
    return residual + low_back(product(activated, w_down))

def adamw_step(grad_sum, master, first, second, rate, decay):
    first_new = BETA_FIRST * first + (1.0 - BETA_FIRST) * grad_sum
    second_new = BETA_SECOND * second + (1.0 - BETA_SECOND) * grad_sum * grad_sum
    corrected = first_new / (1.0 - BETA_FIRST ** STEP) / (jnp.sqrt(second_new / (1.0 - BETA_SECOND ** STEP)) + ADAM_EPSILON)
    master_new = master - rate * (corrected + decay * master)
    return (master_new, master_new.astype(jnp.bfloat16), first_new, second_new)

def reference(tokens, cotangent, lengths, qkv_copy, qkv_master, qkv_first, qkv_second, proj_copy, proj_master, proj_first, proj_second, gateup_copy, gateup_master, gateup_first, gateup_second, down_copy, down_master, down_first, down_second, gain_copy, gain_master, gain_first, gain_second):
    weights_float = (qkv_copy.astype(jnp.float32), proj_copy.astype(jnp.float32), gateup_copy.astype(jnp.float32), down_copy.astype(jnp.float32), gain_copy.astype(jnp.float32))
    token_rows = tokens.reshape(ROWS, ROW, D)
    cotangent_rows = cotangent.reshape(ROWS, ROW, D)

    def per_row(running, members):
        doc_start, position = row_layout(members[2], ROW)

        def forward(x_float, w_qkv, w_proj, w_gateup, w_down, gains):
            return block_layer(x_float, w_qkv, w_proj, w_gateup, w_down, gains, doc_start, position)
        result, pull_back = jax.vjp(forward, members[0].astype(jnp.float32), weights_float[0], weights_float[1], weights_float[2], weights_float[3], weights_float[4])
        grads = pull_back(members[1].astype(jnp.float32))
        running = tuple((total_grad + row_grad for total_grad, row_grad in zip(running, grads[1:])))
        return (running, (result.astype(jnp.bfloat16), grads[0]))
    zero_grads = tuple((jnp.zeros(matrix.shape, jnp.float32) for matrix in weights_float))
    summed, (outputs, input_grads) = lax.scan(per_row, zero_grads, (token_rows, cotangent_rows, lengths))
    qkv_grad, proj_grad, gateup_grad, down_grad, gain_grad = summed
    qkv_new = adamw_step(qkv_grad, qkv_master, qkv_first, qkv_second, D ** (-0.5), DECAY_RATE)
    proj_new = adamw_step(proj_grad, proj_master, proj_first, proj_second, max(HEAD_DIM // 16, 1) ** (-0.5), DECAY_RATE)
    gateup_new = adamw_step(gateup_grad, gateup_master, gateup_first, gateup_second, D ** (-0.5), DECAY_RATE)
    down_new = adamw_step(down_grad, down_master, down_first, down_second, FF ** (-0.5), DECAY_RATE)
    gain_new = adamw_step(gain_grad, gain_master, gain_first, gain_second, 0.5, 0.0)
    return (outputs.reshape(TOKENS, D), input_grads.reshape(TOKENS, D), qkv_grad, qkv_new[0], qkv_new[1], qkv_new[2], qkv_new[3], proj_grad, proj_new[0], proj_new[1], proj_new[2], proj_new[3], gateup_grad, gateup_new[0], gateup_new[1], gateup_new[2], gateup_new[3], down_grad, down_new[0], down_new[1], down_new[2], down_new[3], gain_grad, gain_new[0], gain_new[1], gain_new[2], gain_new[3])
```

```python
import functools

import jax
import jax.numpy as jnp
from jax import lax
from jax.experimental import pallas as pl
from jax.experimental.pallas import tpu as pltpu
from jax.sharding import Mesh, PartitionSpec as P

D = 960
FF = 2560
HEADS = 15
KV_HEADS = 5
GROUP = 3
HEAD_DIM = 64
BLOCK = 256
STEP = 10
QKV = 1600

NORM_EPSILON = 1e-05
ROPE_THETA = 100000.0
BETA_FIRST = 0.5
BETA_SECOND = 0.6
ADAM_EPSILON = 1e-08
DECAY_RATE = 0.1

LOG2E = 1.4426950408889634
LN2 = 0.6931471805599453
QC = 256
KT = 256
NORM_ROWS = 16
SAFE = 60.0
LANE_LOG = 125
LANE_INNER = 61

F32 = jnp.float32
BF = jnp.bfloat16
NT = (((1,), (1,)), ((), ()))
TN = (((0,), (0,)), ((), ()))
VMEM_BYTES = 58 << 20
ANY = pl.BlockSpec(memory_space=pl.ANY)
WHOLE = pl.BlockSpec(memory_space=pltpu.VMEM)
SCALARS = pl.BlockSpec(memory_space=pltpu.SMEM)


def params():
    return pltpu.CompilerParams(vmem_limit_bytes=VMEM_BYTES)


def cost(flops, moved):
    return pl.CostEstimate(flops=int(flops), bytes_accessed=int(moved), transcendentals=0)


def lanes():
    return lax.broadcasted_iota(jnp.int32, (1, 128), 1)


def split3(value):
    high = value.astype(BF)
    rest = value - high.astype(F32)
    mid = rest.astype(BF)
    return high, mid, (rest - mid.astype(F32)).astype(BF)


def start_all(copies):
    for one in copies:
        one.start()


def wait_all(copies):
    for one in copies:
        one.wait()


def row_halves_plan(refs, target, meta, sems, width):
    if len(refs) == 1:
        return [pltpu.make_async_copy(refs[0], target, sems.at[0])], [], []
    own = refs[0]
    rows = own.shape[0]
    piece = refs[1].shape[0]
    me, core, zpar = meta[0], meta[1], meta[2]
    first = rows - piece
    common = [
        pltpu.make_async_copy(
            own, target.at[pl.ds(pl.multiple_of(me * rows, 16), rows), :], sems.at[0]
        )
    ]
    by_core = ([], [])
    for k, rel in enumerate((1 + zpar, 2 - zpar, 3)):
        base = (me ^ rel) * rows
        low = target.at[pl.ds(pl.multiple_of(base, 16), first), :]
        high = target.at[pl.ds(pl.multiple_of(base + first, 16), piece), :]
        mine, other = refs[1 + k], refs[4 + k]
        for c in range(2):
            low_src, high_src = (mine, other) if c == 0 else (other, mine)
            by_core[c].append(
                pltpu.make_async_copy(low_src.at[pl.ds(0, first), :], low, sems.at[1 + k])
            )
            by_core[c].append(pltpu.make_async_copy(high_src, high, sems.at[4 + k]))
    return common, by_core[0], by_core[1]


def plan_start(plan, meta):
    common, zero, one = plan
    start_all(common)
    if zero:
        pl.when(meta[1] == 0)(lambda: start_all(zero))
        pl.when(meta[1] == 1)(lambda: start_all(one))


def plan_wait(plan, meta):
    common, zero, one = plan
    wait_all(common)
    if zero:
        pl.when(meta[1] == 0)(lambda: wait_all(zero))
        pl.when(meta[1] == 1)(lambda: wait_all(one))


def gateup_copies(refs, target, meta, sems):
    if len(refs) == 1:
        return [
            pltpu.make_async_copy(refs[0].at[:, pl.ds(i * FF, FF)], target.at[i], sems.at[i])
            for i in range(2)
        ]
    me, core, zpar = meta[0], meta[1], meta[2]
    rows = refs[0].shape[0]
    own_rows = pl.ds(pl.multiple_of(me * rows, 16), rows)
    out = [
        pltpu.make_async_copy(
            refs[0].at[:, pl.ds(i * FF, FF)], target.at[i, own_rows, :], sems.at[6 + i]
        )
        for i in range(2)
    ]
    for k, rel in enumerate((1 + zpar, 2 - zpar, 3)):
        at = pl.ds(pl.multiple_of((me ^ rel) * rows, 16), rows)
        out.append(pltpu.make_async_copy(refs[1 + k], target.at[core, at, :], sems.at[k]))
        out.append(pltpu.make_async_copy(refs[4 + k], target.at[1 - core, at, :], sems.at[3 + k]))
    return out


def rope_tile(tile, cosine, sine):
    low = (lanes() % 64) < 32
    swapped = jnp.where(low, pltpu.roll(tile, 96, 1), pltpu.roll(tile, 32, 1))
    return tile * cosine + swapped * sine


def qkv_body(nw, meta, x_ref, gain_ref, cos_ref, sin_ref, *refs):
    w_refs = refs[:nw]
    q_ref, kv_ref, blocks_ref, qn_ref, w_scr, n_scr, j_scr, sems = refs[nw:]
    plan = row_halves_plan(w_refs, w_scr, meta, sems, QKV)
    plan_start(plan, meta)
    x = x_ref[...].astype(F32)
    scale = lax.rsqrt(jnp.mean(x * x, axis=1, keepdims=True) + NORM_EPSILON)
    n_scr[...] = (x * scale * gain_ref[0:1, :].astype(F32)).astype(BF)
    put_blocks(n_scr, blocks_ref)
    plan_wait(plan, meta)
    tokens = x_ref.shape[0]
    j_scr[...] = jnp.dot(n_scr[...], w_scr[...], preferred_element_type=F32)
    lane = lanes()
    cosine = cos_ref[...]
    sine = sin_ref[...]
    top_q = jnp.zeros((tokens, 1), F32)
    kv_ref[tokens:, :] = jnp.zeros((NORM_ROWS, KV_HEADS * 128), BF)
    keys = {}
    for t in range(10):
        tile = rope_tile(j_scr[:, 128 * t : 128 * (t + 1)], cosine, sine)
        turned = pltpu.roll(tile, 64, 1)
        for half in range(2):
            part = tile if half == 0 else turned
            head = 2 * t + half
            if head < HEADS:
                part = jnp.where(lane < 64, part * (LOG2E * 0.125), 0.0).astype(BF)
                q_ref[head] = part
                part = part.astype(F32)
                top_q = jnp.maximum(top_q, jnp.sum(part * part, axis=1, keepdims=True))
            else:
                keys[head - HEADS] = part
    qn_ref[...] = jnp.broadcast_to(jnp.max(top_q, axis=0, keepdims=True) * 1.02, (8, 128))
    for g in range(KV_HEADS):
        t = 10 + g // 2
        if t == 12:
            last = j_scr[:, 1536:1600]
            value = jnp.concatenate([last, last], axis=1)
        else:
            value = j_scr[:, 128 * t : 128 * (t + 1)]
            if g % 2 == 0:
                value = pltpu.roll(value, 64, 1)
        both = jnp.where(lane < 64, keys[g], value).astype(BF)
        kv_ref[:tokens, 128 * g : 128 * (g + 1)] = both
        key = jnp.where(lane < 64, both.astype(F32), 0.0)
        top = jnp.max(jnp.sum(key * key, axis=1, keepdims=True), axis=0, keepdims=True)
        kv_ref[tokens:, 128 * g : 128 * (g + 1)] = jnp.broadcast_to(
            top * 1.02, (NORM_ROWS, 128)
        ).astype(BF)


def put_blocks(n_ref, blocks_ref):
    shards = blocks_ref.shape[1]
    width = D // shards
    first = width - 128
    for b in range(shards):
        for c in range(2):
            at = b * width + c * first
            blocks_ref[c, b] = n_ref[:, at : at + 128]


def qkv_call(meta, x, gains, cosine, sine, weights, shards):
    tokens = x.shape[0]
    nw = len(weights)
    return pl.pallas_call(
        functools.partial(qkv_body, nw),
        in_specs=[SCALARS] + [WHOLE] * 4 + [ANY] * nw,
        out_specs=[WHOLE] * 4,
        out_shape=[
            jax.ShapeDtypeStruct((HEADS, tokens, 128), BF),
            jax.ShapeDtypeStruct((tokens + NORM_ROWS, KV_HEADS * 128), BF),
            jax.ShapeDtypeStruct((2, 4, tokens, 128), BF),
            jax.ShapeDtypeStruct((8, 128), F32),
        ],
        scratch_shapes=[
            pltpu.VMEM((D, QKV), BF),
            pltpu.VMEM((tokens, D), BF),
            pltpu.VMEM((tokens, QKV), F32),
            pltpu.SemaphoreType.DMA((8,)),
        ],
        compiler_params=params(),
        cost_estimate=cost(2 * tokens * D * QKV, 10 << 20),
        name="qkv_project",
    )(meta, x, gains, cosine, sine, *weights)


def load_pieces(shards, tokens, me, pieces, kv_scr, sem, nrm_scr=None, nsem=None):
    copies = []
    for j in range(shards):
        row = pl.multiple_of((me ^ j) * tokens, tokens)
        for h in range(KV_HEADS):
            copies.append(
                pltpu.make_async_copy(
                    pieces[j].at[pl.ds(0, tokens), pl.ds(h * 128, 128)],
                    kv_scr.at[h, pl.ds(row, tokens), :],
                    sem.at[j, h],
                )
            )
        if nrm_scr is not None:
            copies.append(
                pltpu.make_async_copy(
                    pieces[j].at[pl.ds(tokens, NORM_ROWS), :], nrm_scr.at[j], nsem.at[j]
                )
            )
    start_all(copies)
    wait_all(copies)


def pair_range(meta, c):
    t_lo = meta[3 + 2 * c]
    t_hi = meta[4 + 2 * c]
    odd = (t_hi - t_lo) & 1
    start = jnp.where((odd == 1) & (t_lo > 0), t_lo - 1, t_lo)
    return start, (t_hi - t_lo + odd) // 2


def attend_forward_body(shards, tokens, meta, q_ref, qm_ref, qn_ref, aug_ref, *refs):
    pieces = refs[:shards]
    o_ref, q2_ref, kv_scr, acc_scr, m_scr, nrm_scr, sem, nsem = refs[shards:]
    g = pl.program_id(0)
    c = pl.program_id(1)

    @pl.when((g == 0) & (c == 0))
    def _():
        load_pieces(shards, tokens, meta[0], pieces, kv_scr, sem, nrm_scr, nsem)

    lane = lanes()
    qm = qm_ref[...]
    rows_all = GROUP * QC
    acc_scr[...] = jnp.zeros_like(acc_scr)
    q2_ref[...] = jnp.where(lane < 64, q_ref[...], qm[None])
    safe = jnp.max(qn_ref[...]) * jnp.max(nrm_scr[...].astype(F32)) < SAFE * SAFE
    start, pairs = pair_range(meta, c)

    def tiles(u):
        rows = pl.ds(pl.multiple_of((start + 2 * u) * KT, KT), 2 * KT)
        kv = kv_scr[g, rows, :]
        return (
            jnp.where(lane < 64, kv, aug_ref[rows, :]),
            jnp.where(lane < 64, jnp.ones_like(kv), kv),
        )

    @pl.when(safe)
    def _():
        def step(u, carry):
            keys, values = tiles(u)
            scores = lax.dot_general(
                q2_ref[...].reshape(rows_all, 128), keys, NT, preferred_element_type=F32
            )
            weights = jnp.exp2(scores).astype(BF)
            acc_scr[...] += jnp.dot(weights, values, preferred_element_type=F32)
            return carry

        lax.fori_loop(0, pairs, step, 0)
        m_scr[...] = jnp.zeros_like(m_scr)

    @pl.when(jnp.logical_not(safe))
    def _():
        m_scr[...] = jnp.full_like(m_scr, -1e30)

        def step(u, carry):
            keys, values = tiles(u)

            def head(h, carry):
                scores = lax.dot_general(q2_ref[h], keys, NT, preferred_element_type=F32)
                rows = pl.ds(pl.multiple_of(h * QC, QC), QC)
                old = m_scr[rows, :1]
                new = jnp.maximum(old, jnp.max(scores, axis=1, keepdims=True))
                weights = jnp.exp2(scores - new).astype(BF)
                acc_scr[rows, :] = acc_scr[rows, :] * jnp.exp2(old - new) + jnp.dot(
                    weights, values, preferred_element_type=F32
                )
                m_scr[rows, :] = jnp.broadcast_to(new, (QC, 128))
                return carry

            return lax.fori_loop(0, GROUP, head, carry)

        lax.fori_loop(0, pairs, step, 0)

    def finish(h, carry):
        rows = pl.ds(pl.multiple_of(h * QC, QC), QC)
        acc = acc_scr[rows, :]
        other = pltpu.roll(acc, 64, 1)
        o_ref[h] = jnp.where(lane < 64, 0.0, acc / jnp.where(lane < 64, 1.0, other)).astype(BF)
        total = jnp.where(lane < 64, acc, other)
        high, mid, low = split3(-(m_scr[rows, :] + jnp.log2(total)))
        with_log = jnp.where(lane == LANE_LOG + 2, low, q2_ref[h])
        with_log = jnp.where(lane == LANE_LOG + 1, mid, with_log)
        q2_ref[h] = jnp.where(lane == LANE_LOG, high, with_log)
        return carry

    lax.fori_loop(0, GROUP, finish, 0)


def attend_forward(meta, q, qm, qn, aug, pieces):
    shards = len(pieces)
    tokens = pieces[0].shape[0] - NORM_ROWS
    row = shards * tokens
    block = pl.BlockSpec((GROUP, QC, 128), lambda g, c, m: (g, c, 0))
    return pl.pallas_call(
        functools.partial(attend_forward_body, shards, tokens),
        grid_spec=pltpu.PrefetchScalarGridSpec(
            num_scalar_prefetch=1,
            grid=(KV_HEADS, tokens // QC),
            in_specs=[
                block,
                pl.BlockSpec((QC, 128), lambda g, c, m: (c, 0)),
                pl.BlockSpec((8, 128), lambda g, c, m: (0, 0)),
                pl.BlockSpec((row, 128), lambda g, c, m: (0, 0)),
            ]
            + [ANY] * shards,
            out_specs=[block, block],
            scratch_shapes=[
                pltpu.VMEM((KV_HEADS, row, 128), BF),
                pltpu.VMEM((GROUP * QC, 128), F32),
                pltpu.VMEM((GROUP * QC, 128), F32),
                pltpu.VMEM((shards, NORM_ROWS, KV_HEADS * 128), BF),
                pltpu.SemaphoreType.DMA((shards, KV_HEADS)),
                pltpu.SemaphoreType.DMA((shards,)),
            ],
        ),
        out_shape=[jax.ShapeDtypeStruct((HEADS, tokens, 128), BF)] * 2,
        compiler_params=params(),
        cost_estimate=cost(16 * HEADS * tokens * row * 128, 10 << 20),
        name="attend_forward",
    )(meta, q, qm, qn, aug, *pieces)


def attend_backward_body(shards, tokens, meta, q_ref, do_ref, aug_ref, *refs):
    pieces = refs[:shards]
    dq_ref = refs[shards]
    outs = refs[shards + 1 : 2 * shards + 1]
    kv_scr, dkv_scr, ob_scr, dq_scr, qt_scr, sem, osem = refs[2 * shards + 1 :]
    g = pl.program_id(0)
    c = pl.program_id(1)
    me = meta[0]

    @pl.when((g == 0) & (c == 0))
    def _():
        load_pieces(shards, tokens, me, pieces, kv_scr, sem)

    @pl.when(c == 0)
    def _():
        dkv_scr[...] = jnp.zeros_like(dkv_scr)

    lane = lanes()
    rows_all = GROUP * QC
    dq_scr[...] = jnp.zeros_like(dq_scr)
    qt_scr[...] = jnp.transpose(
        jnp.where(lane < 64, q_ref[...], do_ref[...]).reshape(rows_all, 128)
    )
    start, pairs = pair_range(meta, c)

    def step(u, carry):
        tile = start + 2 * u
        rows = pl.ds(pl.multiple_of(tile * KT, KT), 2 * KT)
        kv = kv_scr[g, rows, :]
        ones = jnp.where(lane >= LANE_INNER, jnp.ones_like(kv), jnp.zeros_like(kv))
        keys = jnp.where(lane < 64, kv, aug_ref[rows, :])
        values = jnp.where(lane < 64, ones, kv)
        queries = q_ref[...].reshape(rows_all, 128)
        grads = do_ref[...].reshape(rows_all, 128)
        weights = jnp.exp2(lax.dot_general(queries, keys, NT, preferred_element_type=F32))
        inner = lax.dot_general(grads, values, NT, preferred_element_type=F32)
        grad_scores = (weights * inner).astype(BF)
        weights = weights.astype(BF)
        dq_scr[...] += jnp.dot(grad_scores, keys, preferred_element_type=F32)
        for i in range(2):
            part = slice(i * KT, (i + 1) * KT)
            dkv_scr[tile + i, :64] += jnp.dot(
                qt_scr[:64], grad_scores[:, part], preferred_element_type=F32
            )
            dkv_scr[tile + i, 64:] += jnp.dot(
                qt_scr[64:], weights[:, part], preferred_element_type=F32
            )
        return carry

    lax.fori_loop(0, pairs, step, 0)
    dq_ref[...] = dq_scr[...].reshape(GROUP, QC, 128) * 0.125

    @pl.when(c == pl.num_programs(1) - 1)
    def _():
        for t in range(shards * tokens // KT):
            both = dkv_scr[t]
            both = jnp.concatenate([both[:64] * LN2, both[64:]], axis=0)
            ob_scr[t * KT : (t + 1) * KT, :] = jnp.transpose(both).astype(BF)
        copies = []
        for j in range(shards):
            row = pl.multiple_of((me ^ j) * tokens, tokens)
            copies.append(
                pltpu.make_async_copy(
                    ob_scr.at[pl.ds(row, tokens), :],
                    outs[j].at[:, pl.ds(pl.multiple_of(g * 128, 128), 128)],
                    osem.at[j],
                )
            )
        start_all(copies)
        wait_all(copies)


def attend_backward(meta, q2, do, aug, pieces):
    shards = len(pieces)
    tokens = pieces[0].shape[0] - NORM_ROWS
    row = shards * tokens
    rows_all = GROUP * QC
    block = pl.BlockSpec((GROUP, QC, 128), lambda g, c, m: (g, c, 0))
    return pl.pallas_call(
        functools.partial(attend_backward_body, shards, tokens),
        grid_spec=pltpu.PrefetchScalarGridSpec(
            num_scalar_prefetch=1,
            grid=(KV_HEADS, tokens // QC),
            in_specs=[block, block, pl.BlockSpec((row, 128), lambda g, c, m: (0, 0))]
            + [ANY] * shards,
            out_specs=[block] + [ANY] * shards,
            scratch_shapes=[
                pltpu.VMEM((KV_HEADS, row, 128), BF),
                pltpu.VMEM((row // KT, 128, KT), F32),
                pltpu.VMEM((row, 128), BF),
                pltpu.VMEM((rows_all, 128), F32),
                pltpu.VMEM((128, rows_all), BF),
                pltpu.SemaphoreType.DMA((shards, KV_HEADS)),
                pltpu.SemaphoreType.DMA((shards,)),
            ],
        ),
        out_shape=[jax.ShapeDtypeStruct((HEADS, tokens, 128), F32)]
        + [jax.ShapeDtypeStruct((tokens, KV_HEADS * 128), BF)] * shards,
        compiler_params=params(),
        cost_estimate=cost(30 * HEADS * tokens * row * 128, 16 << 20),
        name="attend_backward",
    )(meta, q2, do, aug, *pieces)


MLP_TILE = 640


def mlp_body(counts, meta, x_ref, o_ref, cot_ref, gain_ref, *refs):
    n_proj, n_gu, n_down = counts
    proj_refs = refs[:n_proj]
    gu_refs = refs[n_proj : n_proj + n_gu]
    down_refs = refs[n_proj + n_gu : n_proj + n_gu + n_down]
    (
        out_ref,
        gres_ref,
        gb_ref,
        mixed_ref,
        n2b_ref,
        act_ref,
        dgu_mine_ref,
        dgu_send_ref,
        do_ref,
        gain_out_ref,
        proj_scr,
        gu_scr,
        down_scr,
        mix_scr,
        n2_scr,
        acc_scr,
        dn_scr,
        act_scr,
        dgu_scr,
        proj_sems,
        gu_sems,
        down_sems,
        out_sems,
    ) = refs[n_proj + n_gu + n_down :]
    proj_plan = row_halves_plan(proj_refs, proj_scr, meta, proj_sems, D)
    down_plan = row_halves_plan(down_refs, down_scr, meta, down_sems, D)
    gu_copies = gateup_copies(gu_refs, gu_scr, meta, gu_sems)
    plan_start(proj_plan, meta)
    start_all(gu_copies)
    plan_start(down_plan, meta)
    lane = lanes()
    for t in range(8):
        low = pltpu.roll(o_ref[2 * t].astype(F32), 64, 1)
        if t < 7:
            tile = jnp.where(lane < 64, low, o_ref[2 * t + 1].astype(F32)).astype(BF)
            mix_scr[:, 128 * t : 128 * (t + 1)] = tile
        else:
            mix_scr[:, 896:960] = low[:, :64].astype(BF)
    put_blocks(mix_scr, mixed_ref)
    plan_wait(proj_plan, meta)
    residual = x_ref[...].astype(F32) + jnp.dot(
        mix_scr[...], proj_scr[...], preferred_element_type=F32
    )
    gres_ref[...] = residual
    scale = lax.rsqrt(jnp.mean(residual * residual, axis=1, keepdims=True) + NORM_EPSILON)
    gain = gain_ref[1:2, :].astype(F32)
    n2_scr[...] = (residual * scale * gain).astype(BF)
    width = n2b_ref.shape[2]
    for b in range(n2b_ref.shape[0]):
        n2b_ref[b] = n2_scr[:, b * width : (b + 1) * width]
    wait_all(gu_copies)
    plan_wait(down_plan, meta)
    tiles = FF // MLP_TILE
    core = meta[1]
    out_copies = []
    for f in range(tiles):
        cols = slice(f * MLP_TILE, (f + 1) * MLP_TILE)
        normed = n2_scr[...]
        gate = jnp.dot(normed, gu_scr[0, :, cols], preferred_element_type=F32)
        up = jnp.dot(normed, gu_scr[1, :, cols], preferred_element_type=F32)
        grad_act = lax.dot_general(
            cot_ref[...], down_scr[cols, :], NT, preferred_element_type=F32
        )
        gated = 1.0 / (1.0 + jnp.exp(-gate))
        silu = gate * gated
        act = (silu * up).astype(BF)
        grad_gate = (grad_act * up * gated * (1.0 + gate * (1.0 - gated))).astype(BF)
        grad_up = (grad_act * silu).astype(BF)
        half = MLP_TILE // 2
        act_scr[0, f] = act[:, :half]
        act_scr[1, f] = act[:, half:]
        dgu_scr[0, :, cols] = grad_gate
        dgu_scr[1, :, cols] = grad_up
        add_out = jnp.dot(act, down_scr[cols, :], preferred_element_type=F32)
        add_dn = lax.dot_general(
            grad_gate, gu_scr[0, :, cols], NT, preferred_element_type=F32
        ) + lax.dot_general(grad_up, gu_scr[1, :, cols], NT, preferred_element_type=F32)
        if f == 0:
            acc_scr[...] = add_out
            dn_scr[...] = add_dn
        else:
            acc_scr[...] += add_out
            dn_scr[...] += add_dn
        copies = [
            pltpu.make_async_copy(act_scr.at[i, f], act_ref.at[i, f], out_sems.at[f, i])
            for i in range(2)
        ]
        for i, ref in enumerate((dgu_mine_ref, dgu_send_ref)):
            copies.append(
                pltpu.make_async_copy(
                    dgu_scr.at[core if i == 0 else 1 - core, :, pl.ds(f * MLP_TILE, MLP_TILE)],
                    ref.at[:, pl.ds(f * MLP_TILE, MLP_TILE)],
                    out_sems.at[f, 2 + i],
                )
            )
        start_all(copies)
        out_copies += copies
    residual = gres_ref[...]
    out_ref[...] = (residual + acc_scr[...]).astype(BF)
    grad = dn_scr[...]
    gain_out_ref[...] = jnp.broadcast_to(
        jnp.sum(grad * residual * scale, axis=0, keepdims=True), (8, D)
    )
    scaled = grad * gain
    mean = jnp.mean(scaled * residual, axis=1, keepdims=True)
    grad_residual = (
        cot_ref[...].astype(F32) + scale * scaled - residual * (scale * scale * scale * mean)
    )
    gres_ref[...] = grad_residual
    gb_ref[...] = grad_residual.astype(BF)
    dn_scr[...] = lax.dot_general(gb_ref[...], proj_scr[...], NT, preferred_element_type=F32)
    ones = (
        (lax.broadcasted_iota(jnp.int32, (128, 128), 0) < 64)
        == (lax.broadcasted_iota(jnp.int32, (128, 128), 1) < 64)
    ).astype(BF)
    for t in range(8):
        if t < 7:
            gm = dn_scr[:, 128 * t : 128 * (t + 1)].astype(BF)
            mixed = mix_scr[:, 128 * t : 128 * (t + 1)]
        else:
            gm = dn_scr[:, 896:960].astype(BF)
            gm = jnp.concatenate([gm, jnp.zeros_like(gm)], axis=1)
            mixed = mix_scr[:, 896:960]
            mixed = jnp.concatenate([mixed, jnp.zeros_like(mixed)], axis=1)
        gm = gm.astype(F32)
        high, mid, low = split3(gm * mixed.astype(F32))
        inner = jnp.dot(high, ones, preferred_element_type=F32) + (
            jnp.dot(mid, ones, preferred_element_type=F32)
            + jnp.dot(low, ones, preferred_element_type=F32)
        )
        turned = pltpu.roll(gm, 64, 1)
        turned_inner = pltpu.roll(inner, 64, 1)
        for half in range(2):
            head = 2 * t + half
            if head >= HEADS:
                continue
            grads = turned if half == 0 else gm
            high, mid, low = split3(-(inner if half == 0 else turned_inner))
            tile = jnp.where(lane < 64, 0.0, grads).astype(BF)
            tile = jnp.where(lane == LANE_INNER + 2, low, tile)
            tile = jnp.where(lane == LANE_INNER + 1, mid, tile)
            do_ref[head] = jnp.where(lane == LANE_INNER, high, tile)
    wait_all(out_copies)


def mlp_call(meta, x, o, cot, gains, proj, gateup, down, shards):
    tokens = x.shape[0]
    counts = (len(proj), len(gateup), len(down))
    tiles = FF // MLP_TILE
    return pl.pallas_call(
        functools.partial(mlp_body, counts),
        in_specs=[SCALARS] + [WHOLE] * 4 + [ANY] * sum(counts),
        out_specs=[WHOLE] * 5 + [ANY] * 3 + [WHOLE] * 2,
        out_shape=[
            jax.ShapeDtypeStruct((tokens, D), BF),
            jax.ShapeDtypeStruct((tokens, D), F32),
            jax.ShapeDtypeStruct((tokens, D), BF),
            jax.ShapeDtypeStruct((2, 4, tokens, 128), BF),
            jax.ShapeDtypeStruct((4, tokens, D // 4), BF),
            jax.ShapeDtypeStruct((2, tiles, tokens, MLP_TILE // 2), BF),
            jax.ShapeDtypeStruct((tokens, FF), BF),
            jax.ShapeDtypeStruct((tokens, FF), BF),
            jax.ShapeDtypeStruct((HEADS, tokens, 128), BF),
            jax.ShapeDtypeStruct((8, D), F32),
        ],
        scratch_shapes=[
            pltpu.VMEM((D, D), BF),
            pltpu.VMEM((2, D, FF), BF),
            pltpu.VMEM((FF, D), BF),
            pltpu.VMEM((tokens, D), BF),
            pltpu.VMEM((tokens, D), BF),
            pltpu.VMEM((tokens, D), F32),
            pltpu.VMEM((tokens, D), F32),
            pltpu.VMEM((2, tiles, tokens, MLP_TILE // 2), BF),
            pltpu.VMEM((2, tokens, FF), BF),
            pltpu.SemaphoreType.DMA((8,)),
            pltpu.SemaphoreType.DMA((8,)),
            pltpu.SemaphoreType.DMA((8,)),
            pltpu.SemaphoreType.DMA((tiles, 4)),
        ],
        compiler_params=params(),
        cost_estimate=cost(2 * tokens * D * (6 * FF + 2 * D), 40 << 20),
        name="feed_forward",
    )(meta, x, o, cot, gains, *proj, *gateup, *down)


def joined_body(nw, shards, meta, dq_ref, cos_ref, sin_ref, x_ref, gain_ref, gres_ref, *refs):
    dkv_refs = refs[:shards]
    w_refs = refs[shards : shards + nw]
    gj_ref, ig_ref, gain_out_ref, w_scr, g_scr, sems = refs[shards + nw :]
    plan = row_halves_plan(w_refs, w_scr, meta, sems, QKV)
    plan_start(plan, meta)
    lane = lanes()
    cosine = cos_ref[...]
    sine = -sin_ref[...]
    heads = {}

    def dkv(g):
        if g not in heads:
            total = dkv_refs[0][:, 128 * g : 128 * (g + 1)].astype(F32)
            for ref in dkv_refs[1:]:
                total = total + ref[:, 128 * g : 128 * (g + 1)].astype(F32)
            heads[g] = (total, pltpu.roll(total, 64, 1))
        return heads[g]

    def low_half(h):
        if h < HEADS:
            return dq_ref[h]
        if h < HEADS + KV_HEADS:
            return dkv(h - HEADS)[0]
        return dkv(h - HEADS - KV_HEADS)[1]

    def high_half(h):
        if h < HEADS:
            return pltpu.roll(dq_ref[h], 64, 1)
        if h < HEADS + KV_HEADS:
            return dkv(h - HEADS)[1]
        return dkv(h - HEADS - KV_HEADS)[0]

    for t in range(13):
        if t == 12:
            gj_ref[:, 1536:1600] = low_half(24)[:, :64].astype(BF)
            continue
        tile = jnp.where(lane < 64, low_half(2 * t), high_half(2 * t + 1))
        if t < 10:
            tile = rope_tile(tile, cosine, sine)
        gj_ref[:, 128 * t : 128 * (t + 1)] = tile.astype(BF)
    plan_wait(plan, meta)
    g_scr[...] = lax.dot_general(gj_ref[...], w_scr[...], NT, preferred_element_type=F32)
    grad = g_scr[...]
    x = x_ref[...].astype(F32)
    scale = lax.rsqrt(jnp.mean(x * x, axis=1, keepdims=True) + NORM_EPSILON)
    gain_out_ref[...] = jnp.broadcast_to(
        jnp.sum(grad * x * scale, axis=0, keepdims=True), (8, D)
    )
    scaled = grad * gain_ref[0:1, :].astype(F32)
    mean = jnp.mean(scaled * x, axis=1, keepdims=True)
    ig_ref[...] = gres_ref[...] + scale * scaled - x * (scale * scale * scale * mean)


def joined_call(meta, dq, cosine, sine, x, gains, gres, dkvs, weights):
    tokens = x.shape[0]
    nw = len(weights)
    shards = len(dkvs)
    return pl.pallas_call(
        functools.partial(joined_body, nw, shards),
        in_specs=[SCALARS] + [WHOLE] * (6 + shards) + [ANY] * nw,
        out_specs=[WHOLE] * 3,
        out_shape=[
            jax.ShapeDtypeStruct((tokens, QKV), BF),
            jax.ShapeDtypeStruct((tokens, D), F32),
            jax.ShapeDtypeStruct((8, D), F32),
        ],
        scratch_shapes=[
            pltpu.VMEM((D, QKV), BF),
            pltpu.VMEM((tokens, D), F32),
            pltpu.SemaphoreType.DMA((8,)),
        ],
        compiler_params=params(),
        cost_estimate=cost(2 * tokens * D * QKV, 16 << 20),
        name="joined_backward",
    )(meta, dq, cosine, sine, x, gains, gres, *dkvs, *weights)


def wgrad_body(count, meta, *refs):
    a_refs = refs[:count]
    b_refs = refs[count : 2 * count]
    outs = refs[2 * count :]
    me = meta[0]
    for j, out in enumerate(outs):
        block = me ^ j
        total = lax.dot_general(a_refs[0][block], b_refs[0][...], TN, preferred_element_type=F32)
        for a_ref, b_ref in zip(a_refs[1:], b_refs[1:]):
            total = total + lax.dot_general(
                a_ref[block], b_ref[...], TN, preferred_element_type=F32
            )
        out[...] = total.astype(BF)


def wgrad_call(meta, lefts, rights, tile, name):
    count = len(lefts)
    blocks, tokens, m = lefts[0].shape
    n = rights[0].shape[1]
    return pl.pallas_call(
        functools.partial(wgrad_body, count),
        grid_spec=pltpu.PrefetchScalarGridSpec(
            num_scalar_prefetch=1,
            grid=(n // tile,),
            in_specs=[pl.BlockSpec((blocks, tokens, m), lambda i, s: (0, 0, 0))] * count
            + [pl.BlockSpec((tokens, tile), lambda i, s: (0, i))] * count,
            out_specs=[pl.BlockSpec((m, tile), lambda i, s: (0, i))] * blocks,
        ),
        out_shape=[jax.ShapeDtypeStruct((m, n), BF)] * blocks,
        compiler_params=params(),
        cost_estimate=cost(2 * count * blocks * tokens * m * n, 12 << 20),
        name=name,
    )(meta, *lefts, *rights)


def adamw_step(grad_sum, master, first, second, rate, decay):
    first_new = BETA_FIRST * first + (1.0 - BETA_FIRST) * grad_sum
    second_new = BETA_SECOND * second + (1.0 - BETA_SECOND) * grad_sum * grad_sum
    corrected = (
        first_new
        / (1.0 - BETA_FIRST**STEP)
        / (jnp.sqrt(second_new / (1.0 - BETA_SECOND**STEP)) + ADAM_EPSILON)
    )
    master_new = master - rate * (corrected + decay * master)
    return (master_new, master_new.astype(jnp.bfloat16), first_new, second_new)


def row_tables(doc_lengths, row, offset, tokens):
    ends = jnp.cumsum(doc_lengths, dtype=jnp.int32)
    starts = ends - doc_lengths
    blocks = (doc_lengths + BLOCK - 1) // BLOCK
    bases = jnp.cumsum(blocks, dtype=jnp.int32) - blocks
    places = jnp.arange(row, dtype=jnp.int32)
    inside = (places[:, None] >= starts[None, :]) & (places[:, None] < ends[None, :])

    def pick(values):
        return jnp.sum(jnp.where(inside, values[None, :], 0), axis=1, dtype=jnp.int32)

    doc_start, doc_end, base = pick(starts), pick(ends), pick(bases)
    position = places - doc_start
    segment = base + position // BLOCK
    reach = jnp.minimum(doc_end, doc_start + BLOCK * (position // BLOCK + 1))
    lane = jnp.arange(128, dtype=jnp.int32)
    aug = ((lane[None, :] == segment[:, None] + 64) | (lane[None, :] >= LANE_LOG)).astype(BF)

    def own(values):
        return lax.dynamic_slice_in_dim(values, offset, tokens)

    doc_start, reach, base, segment = own(doc_start), own(reach), own(base), own(segment)
    seen = (lane[None, :] >= base[:, None] + 64) & (lane[None, :] <= segment[:, None] + 64)
    open_lane = seen | (lane[None, :] >= LANE_LOG) | (lane[None, :] < 64)
    qmask = jnp.where(open_lane, 0.0, -1e30).astype(BF)
    chunks = tokens // QC
    low = jnp.min(doc_start.reshape(chunks, QC), axis=1) // KT
    high = (jnp.max(reach.reshape(chunks, QC), axis=1) + KT - 1) // KT
    ranges = jnp.stack([low, high], axis=1).reshape(-1).astype(jnp.int32)
    half = HEAD_DIM // 2
    frequency = ROPE_THETA ** (-2.0 * jnp.arange(half, dtype=F32) / HEAD_DIM)
    angles = own(position).astype(F32)[:, None] * frequency[None, :]
    cosine, sine = jnp.cos(angles), jnp.sin(angles)
    cosine = jnp.concatenate([cosine] * 4, axis=1)
    sine = jnp.concatenate([-sine, sine, -sine, sine], axis=1)
    return aug, qmask, ranges, cosine, sine


def early_gradients(meta, core, over_core, down_in, gateup_in, proj_in, n1_blocks):
    def both(mine, send):
        return (mine, over_core(send))

    def of_core(values, which):
        return lax.dynamic_index_in_dim(values, which, axis=0, keepdims=False)

    def halves(values):
        return both(of_core(values, core), of_core(values, 1 - core))

    act, cotangent = down_in
    n2_blocks, dgu_mine, dgu_send = gateup_in
    mixed_blocks, grad_branch = proj_in
    n1_pair = halves(n1_blocks)
    down_g = wgrad_call(meta, halves(act), both(cotangent, cotangent), D, "down_gradient")
    gateup_g = wgrad_call(
        meta, both(n2_blocks, n2_blocks), both(dgu_mine, dgu_send), 640, "gateup_gradient"
    )
    proj_g = wgrad_call(
        meta, halves(mixed_blocks), both(grad_branch, grad_branch), D, "proj_gradient"
    )
    return down_g, gateup_g, proj_g, n1_pair, both


def local(
    shards,
    depth,
    tokens,
    cotangent,
    lengths,
    qkv_copy,
    qkv_master,
    qkv_first,
    qkv_second,
    proj_copy,
    proj_master,
    proj_first,
    proj_second,
    gateup_copy,
    gateup_master,
    gateup_first,
    gateup_second,
    down_copy,
    down_master,
    down_first,
    down_second,
    gain_copy,
    gain_master,
    gain_first,
    gain_second,
):
    fast = shards == 4 and depth == 4
    me = lax.axis_index("shard")
    z = lax.axis_index("deep")
    core = lax.axis_index("core")
    count = tokens.shape[0]

    def over_shard(value, flip):
        return lax.ppermute(value, "shard", [(s, s ^ flip) for s in range(shards)])

    def over_core(value):
        return lax.ppermute(value, "core", [(0, 1), (1, 0)])

    def over_deep(value, flip):
        return lax.ppermute(value, "deep", [(s, s ^ flip) for s in range(depth)])

    def hop(value, flips):
        pairs = [
            (s * depth + d, (s ^ flips[d % 2]) * depth + d)
            for s in range(shards)
            for d in range(depth)
        ]
        return lax.ppermute(value, ("shard", "deep"), pairs)

    def gather(piece):
        one = hop(piece, (1, 2))
        two = over_deep(one, 1)
        three = hop(one, (2, 1))
        return one, two, three, over_core(one), over_core(two), over_core(three)

    aug, qmask, ranges, cosine, sine = row_tables(
        lengths[0], count * shards, me * count, count
    )
    meta = jnp.concatenate([jnp.stack([me, core, z % 2]).astype(jnp.int32), ranges])

    if fast:
        pad = (qkv_copy.shape[0] - 128)
        qkv_w = (qkv_copy,) + gather(lax.dynamic_slice_in_dim(qkv_copy, core * pad, 128))
        proj_w = (proj_copy,) + gather(lax.dynamic_slice_in_dim(proj_copy, core * pad, 128))
        gateup_w = (gateup_copy,) + gather(
            lax.dynamic_slice_in_dim(gateup_copy, core * FF, FF, axis=1)
        )
        half = down_copy.shape[0] // 2
        down_w = (down_copy,) + gather(lax.dynamic_slice_in_dim(down_copy, core * half, half))
        parts = jnp.stack([gain_copy] + [over_shard(gain_copy, j) for j in range(1, 4)])
        order = jnp.arange(4) ^ me
        gains = jnp.take(parts, order, axis=0).transpose(1, 0, 2).reshape(2, D)
    else:
        qkv_w, proj_w, gateup_w, down_w = (
            (lax.all_gather(w, "shard", axis=0, tiled=True),)
            for w in (qkv_copy, proj_copy, gateup_copy, down_copy)
        )
        gains = lax.all_gather(gain_copy, "shard", axis=1, tiled=True)

    q, kv, n1_blocks, qn = qkv_call(meta, tokens, gains, cosine, sine, qkv_w, shards)
    pieces = [kv] + [over_shard(kv, j) for j in range(1, shards)]
    o, q2 = attend_forward(meta, q, qmask, qn, aug, pieces)
    (
        output,
        grad_residual,
        grad_branch,
        mixed_blocks,
        n2_blocks,
        act,
        dgu_mine,
        dgu_send,
        do,
        gain_two,
    ) = mlp_call(meta, tokens, o, cotangent, gains, proj_w, gateup_w, down_w, shards)

    if fast:
        down_g, gateup_g, proj_g, n1_pair, both = early_gradients(
            meta,
            core,
            over_core,
            (act, cotangent),
            (n2_blocks, dgu_mine, dgu_send),
            (mixed_blocks, grad_branch),
            n1_blocks,
        )

    back = attend_backward(meta, q2, do, aug, pieces)
    dkvs = [back[1]] + [over_shard(back[1 + j], j) for j in range(1, shards)]
    grad_joined, input_grad, gain_one = joined_call(
        meta, back[0], cosine, sine, tokens, gains, grad_residual, dkvs, qkv_w
    )
    if fast:
        joined_pair = both(grad_joined, grad_joined)
        qkv_g = wgrad_call(meta, n1_pair, joined_pair, QKV, "qkv_gradient")

    def reduce_shard(blocks, first, then):
        far = over_shard(blocks[3], first)
        near = over_shard(blocks[first], first)
        passed = (blocks[then].astype(F32) + far.astype(F32)).astype(BF)
        last = over_shard(passed, then)
        return (blocks[0].astype(F32) + near.astype(F32) + last.astype(F32)).astype(BF)

    def reduce_deep(value, axis):
        size = value.shape[axis] // 4

        def take(block, at, length):
            return lax.dynamic_slice_in_dim(block, at, length, axis=axis)

        low, high = z % 2, (z // 2) % 2
        near = over_deep(take(value, (1 - low) * 2 * size, 2 * size), 1)
        kept = (take(value, low * 2 * size, 2 * size).astype(F32) + near.astype(F32)).astype(BF)
        far = over_deep(take(kept, (1 - high) * size, size), 2)
        kept = (take(kept, high * size, size).astype(F32) + far.astype(F32)).astype(BF)
        other = over_deep(kept, 2)

        def order(mine, theirs, bit):
            return jnp.concatenate(
                [jnp.where(bit == 0, mine, theirs), jnp.where(bit == 0, theirs, mine)], axis=axis
            )

        kept = order(kept, other, high)
        other = over_deep(kept, 1)
        return order(kept, other, low)

    def by_core(mine):
        theirs = over_core(mine)
        return jnp.where(core == 0, mine, theirs), jnp.where(core == 0, theirs, mine)

    gain_sum = jnp.concatenate([gain_one[:1], gain_two[:1]], axis=0)
    if fast:
        low, high = by_core(reduce_deep(reduce_shard(down_g, 2, 1), 0))
        down_grad = jnp.concatenate([low, high], axis=0).astype(F32)
        low, high = by_core(reduce_deep(reduce_shard(gateup_g, 1, 2), 1))
        gateup_grad = jnp.concatenate([low, high], axis=1).astype(F32)
        cut = D // shards // 2
        low, high = by_core(reduce_deep(reduce_shard(proj_g, 2, 1), 0))
        proj_grad = jnp.concatenate([low[:cut], high[128 - cut :]], axis=0).astype(F32)
        low, high = by_core(reduce_deep(reduce_shard(qkv_g, 2, 1), 0))
        qkv_grad = jnp.concatenate([low[:cut], high[128 - cut :]], axis=0).astype(F32)
        for flip in (1, 2):
            gain_sum = gain_sum + over_shard(gain_sum, flip)
        gain_sum = gain_sum + over_core(gain_sum)
        for flip in (1, 2):
            gain_sum = gain_sum + over_deep(gain_sum, flip)
    else:
        everyone = ("shard", "deep", "core")

        def owned(left, right):
            whole = jnp.einsum("ta,tb->ab", left, right, preferred_element_type=F32)
            mine = lax.psum_scatter(whole, "shard", scatter_dimension=0, tiled=True)
            return lax.psum(mine, ("deep", "core"))

        def plain(blocks):
            parts = jnp.concatenate([blocks[0][..., : D // 4 - 128], blocks[1]], axis=-1)
            return parts.transpose(1, 0, 2).reshape(count, D)

        grad_gate = jnp.where(core == 0, dgu_mine, dgu_send)
        grad_up = jnp.where(core == 0, dgu_send, dgu_mine)
        down_grad = owned(act.transpose(2, 1, 0, 3).reshape(count, FF), cotangent)
        gateup_grad = owned(
            n2_blocks.transpose(1, 0, 2).reshape(count, D),
            jnp.concatenate([grad_gate, grad_up], axis=1),
        )
        proj_grad = owned(plain(mixed_blocks), grad_branch)
        qkv_grad = owned(plain(n1_blocks), grad_joined)
        gain_sum = lax.psum(gain_sum, everyone)
    width = D // shards
    gain_grad = lax.dynamic_slice_in_dim(gain_sum, me * width, width, axis=1)

    down_new = adamw_step(down_grad, down_master, down_first, down_second, FF ** (-0.5), DECAY_RATE)
    gateup_new = adamw_step(
        gateup_grad, gateup_master, gateup_first, gateup_second, D ** (-0.5), DECAY_RATE
    )
    proj_new = adamw_step(
        proj_grad,
        proj_master,
        proj_first,
        proj_second,
        max(HEAD_DIM // 16, 1) ** (-0.5),
        DECAY_RATE,
    )
    qkv_new = adamw_step(qkv_grad, qkv_master, qkv_first, qkv_second, D ** (-0.5), DECAY_RATE)
    gain_new = adamw_step(gain_grad, gain_master, gain_first, gain_second, 0.5, 0.0)
    return (
        (output, input_grad)
        + (qkv_grad,) + qkv_new
        + (proj_grad,) + proj_new
        + (gateup_grad,) + gateup_new
        + (down_grad,) + down_new
        + (gain_grad,) + gain_new
    )


def solution(mesh):
    shards, rep = mesh.shape["shard"], mesh.shape["rep"]
    depth = rep // 2
    fine = Mesh(mesh.devices.reshape(shards, depth, 2), ("shard", "deep", "core"))
    by_token = P(("deep", "core", "shard"), None)
    by_row = P("shard", None)
    by_column = P(None, "shard")
    return jax.shard_map(
        functools.partial(local, shards, depth),
        mesh=fine,
        in_specs=(by_token, by_token, P(("deep", "core"), None)) + (by_row,) * 16 + (by_column,) * 4,
        out_specs=(by_token,) * 2 + (by_row,) * 20 + (by_column,) * 5,
        check_vma=False,
    )
```

```python
import functools

import jax
import jax.numpy as jnp
from jax import lax
from jax.experimental import pallas as pl
from jax.experimental.pallas import tpu as pltpu
from jax.sharding import Mesh, PartitionSpec as P

D = 960
FF = 2560
HEADS = 15
KV_HEADS = 5
GROUP = 3
HEAD_DIM = 64
BLOCK = 256
STEP = 10
QKV = 1600

NORM_EPSILON = 1e-05
ROPE_THETA = 100000.0
BETA_FIRST = 0.5
BETA_SECOND = 0.6
ADAM_EPSILON = 1e-08
DECAY_RATE = 0.1

LOG2E = 1.4426950408889634
LN2 = 0.6931471805599453
QC = 256
FIRST = 3
KT = 256
NORM_ROWS = 16
SAFE = 60.0
LANE_LOG = 125
LANE_INNER = 61

F32 = jnp.float32
BF = jnp.bfloat16
NT = (((1,), (1,)), ((), ()))
TN = (((0,), (0,)), ((), ()))
VMEM_BYTES = 58 << 20
ANY = pl.BlockSpec(memory_space=pl.ANY)
WHOLE = pl.BlockSpec(memory_space=pltpu.VMEM)
SCALARS = pl.BlockSpec(memory_space=pltpu.SMEM)


def params():
    return pltpu.CompilerParams(vmem_limit_bytes=VMEM_BYTES)


def cost(flops, moved):
    del flops, moved
    return pl.CostEstimate(flops=1, bytes_accessed=1, transcendentals=0)


def after_body(*refs):
    del refs


def after(values, deps):
    values, deps = tuple(values), tuple(deps)
    return pl.pallas_call(
        after_body,
        in_specs=[ANY] * (len(values) + len(deps)),
        out_specs=[ANY] * len(values),
        out_shape=[jax.ShapeDtypeStruct(one.shape, one.dtype) for one in values],
        input_output_aliases={i: i for i in range(len(values))},
        compiler_params=params(),
        cost_estimate=cost(1, 1),
        name="after",
    )(*values, *deps)


def transposed(value):
    rows = value.shape[0]
    pad = -rows % 128
    if pad:
        value = jnp.concatenate([value, jnp.zeros((pad, value.shape[1]), value.dtype)], axis=0)
    return jnp.transpose(value)[:, :rows]


def transposed_back(value):
    columns = value.shape[1]
    pad = -columns % 128
    if pad:
        value = jnp.concatenate([value, jnp.zeros((value.shape[0], pad), value.dtype)], axis=1)
    return jnp.transpose(value)[:columns, :]


def lanes():
    return lax.broadcasted_iota(jnp.int32, (1, 128), 1)


def split3(value):
    high = value.astype(BF)
    rest = value - high.astype(F32)
    mid = rest.astype(BF)
    return high, mid, (rest - mid.astype(F32)).astype(BF)


def start_all(copies):
    for one in copies:
        one.start()


def wait_all(copies):
    for one in copies:
        one.wait()


PIECE = 128
PIECE_ROWS = 144
GP_ROWS = 304


def qkv_plan(refs, target, meta, sems):
    if len(refs) == 1:
        return [pltpu.make_async_copy(refs[0], target, sems.at[0])], [], []
    rows = refs[0].shape[0]
    me, zpar = meta[0], meta[2]
    first = rows - PIECE
    own = target.at[pl.ds(pl.multiple_of(me * rows, 16), rows), :]
    common = [pltpu.make_async_copy(refs[0], own, sems.at[0])]
    by_core = ([], [])
    for k, rel in enumerate((1 + zpar, 2 - zpar, 3)):
        base = (me ^ rel) * rows
        low = target.at[pl.ds(pl.multiple_of(base, 16), first), :]
        high = target.at[pl.ds(pl.multiple_of(base + first, 16), PIECE), :]
        mine, other = refs[1 + k], refs[4 + k]
        for c in range(2):
            low_src, high_src = (mine, other) if c == 0 else (other, mine)
            by_core[c].append(
                pltpu.make_async_copy(low_src.at[pl.ds(0, first), :], low, sems.at[1 + k])
            )
            by_core[c].append(
                pltpu.make_async_copy(high_src.at[pl.ds(0, PIECE), :], high, sems.at[4 + k])
            )
    return common, by_core[0], by_core[1]


def proj_plan_of(refs, target, meta, sems):
    if len(refs) == 1:
        return [pltpu.make_async_copy(refs[0], target, sems.at[0])], [], []
    rows = refs[0].shape[0]
    me, zpar = meta[0], meta[2]
    first = rows - PIECE
    own = target.at[pl.ds(pl.multiple_of(me * rows, 16), rows), :]
    common = [pltpu.make_async_copy(refs[0], own, sems.at[0])]
    by_core = ([], [])
    top = GP_ROWS - 64
    for k, rel in enumerate((1 + zpar, 2 - zpar, 3)):
        base = (me ^ rel) * rows
        mine, other = refs[1 + k], refs[4 + k]
        for c in range(2):
            low_src, high_src = (mine, other) if c == 0 else (other, mine)
            jobs = (
                (low_src, 0, 64, 0),
                (low_src, 1, first - 64, 64),
                (high_src, 0, 64, first),
                (high_src, 1, 64, first + 64),
            )
            for n, (src, side, count, at) in enumerate(jobs):
                by_core[c].append(
                    pltpu.make_async_copy(
                        src.at[pl.ds(top, count), pl.ds(side * 1024, 1024)],
                        target.at[pl.ds(pl.multiple_of(base + at, 16), count), :],
                        sems.at[1 + 4 * k + n],
                    )
                )
    return common, by_core[0], by_core[1]


def plan_start(plan, meta):
    common, zero, one = plan
    start_all(common)
    if zero:
        pl.when(meta[1] == 0)(lambda: start_all(zero))
        pl.when(meta[1] == 1)(lambda: start_all(one))


def plan_wait(plan, meta):
    common, zero, one = plan
    wait_all(common)
    if zero:
        pl.when(meta[1] == 0)(lambda: wait_all(zero))
        pl.when(meta[1] == 1)(lambda: wait_all(one))


def gateup_copies(refs, target, meta, sems, tile):
    me, core, zpar = meta[0], meta[1], meta[2]
    rows = refs[0].shape[0]
    out = []
    for f in range(FF // tile):
        cols = pl.ds(f * tile, tile)
        own_rows = pl.ds(pl.multiple_of(me * rows, 16), rows)
        if len(refs) == 1:
            own_rows = pl.ds(0, rows)
        copies = [
            pltpu.make_async_copy(
                refs[0].at[:, pl.ds(i * FF + f * tile, tile)],
                target.at[i, own_rows, cols],
                sems.at[f, i],
            )
            for i in range(2)
        ]
        if len(refs) > 1:
            for k, rel in enumerate((1 + zpar, 2 - zpar, 3)):
                at = pl.ds(pl.multiple_of((me ^ rel) * rows, 16), rows)
                for n, (half, ref) in enumerate(((core, refs[1 + k]), (1 - core, refs[4 + k]))):
                    copies.append(
                        pltpu.make_async_copy(
                            ref.at[pl.ds(0, rows), cols],
                            target.at[half, at, cols],
                            sems.at[f, 2 + 2 * k + n],
                        )
                    )
        out.append(copies)
    return out


def down_copies(refs, target, meta, sems):
    if len(refs) == 1:
        return [pltpu.make_async_copy(refs[0], target, sems.at[0])]
    me, core, zpar = meta[0], meta[1], meta[2]
    width = refs[0].shape[1]
    rows = refs[1].shape[0]

    def columns(rel):
        return pl.ds(pl.multiple_of((me ^ rel) * width, 128), width)

    out = [pltpu.make_async_copy(refs[0], target.at[:, columns(0)], sems.at[6])]
    for k, rel in enumerate((1 + zpar, 2 - zpar, 3)):
        for which, ref in ((core, refs[1 + k]), (1 - core, refs[4 + k])):
            at = pl.ds(pl.multiple_of(which * rows, 16), rows)
            out.append(
                pltpu.make_async_copy(ref, target.at[at, columns(rel)], sems.at[len(out) - 1])
            )
    return out


def cut_body(meta, gateup_ref, proj_ref, dep_ref, gp_out, proj_out):
    rows = gateup_ref.shape[0]
    gp_out[:rows] = gateup_ref[...]
    gp_out[rows:] = jnp.zeros((GP_ROWS - rows, FF), BF)
    half = proj_ref[pl.ds(pl.multiple_of(meta[1] * (rows - PIECE), 16), PIECE), :]
    gp_out[rows:, :D] = half[:64]
    gp_out[rows:, 1024 : 1024 + D] = half[64:]
    proj_out[:, 896:] = jnp.zeros((rows, 128), BF)
    proj_out[:, :D] = proj_ref[...]


def cut_call(meta, gateup, proj, dep):
    rows = gateup.shape[0]
    return pl.pallas_call(
        cut_body,
        grid_spec=pltpu.PrefetchScalarGridSpec(
            num_scalar_prefetch=1,
            grid=(1,),
            in_specs=[
                pl.BlockSpec((rows, FF), lambda i, m: (0, m[1])),
                pl.BlockSpec(proj.shape, lambda i, m: (0, 0)),
                ANY,
            ],
            out_specs=[
                pl.BlockSpec((GP_ROWS, FF), lambda i, m: (0, 0)),
                pl.BlockSpec((rows, 1024), lambda i, m: (0, 0)),
            ],
        ),
        out_shape=[
            jax.ShapeDtypeStruct((GP_ROWS, FF), BF),
            jax.ShapeDtypeStruct((rows, 1024), BF),
        ],
        compiler_params=params(),
        cost_estimate=cost(0, 8 << 20),
        name="cut_weights",
    )(meta, gateup, proj, dep)


def rope_tile(tile, cosine, sine):
    low = (lanes() % 64) < 32
    swapped = jnp.where(low, pltpu.roll(tile, 96, 1), pltpu.roll(tile, 32, 1))
    return tile * cosine + swapped * sine


def first_norm_body(x_ref, cot_ref, *refs):
    x_out, cot_out, scaled_ref = refs[-3:]
    x = transposed(x_ref[...])
    x_out[...] = x
    cot_out[...] = transposed(cot_ref[...])
    x = x.astype(F32)
    scale = lax.rsqrt(jnp.mean(x * x, axis=1, keepdims=True) + NORM_EPSILON)
    scaled_ref[...] = x * scale


def first_norm_call(x, cot, deps):
    tokens = x.shape[1]
    return pl.pallas_call(
        first_norm_body,
        in_specs=[WHOLE] * 2 + [ANY] * len(deps),
        out_specs=[WHOLE] * 3,
        out_shape=[jax.ShapeDtypeStruct((tokens, D), BF)] * 2
        + [jax.ShapeDtypeStruct((tokens, D), F32)],
        compiler_params=params(),
        cost_estimate=cost(0, 5 << 20),
        name="first_norm",
    )(x, cot, *deps)


def kv_body(nw, shards, meta, scaled_ref, gain_ref, cos_ref, sin_ref, *refs):
    w_refs = refs[:nw]
    n_ref, gains_out, kva_out, kvb_ref, w_scr, j_scr, kva_ref, g_scr, sems, gsems = refs[nw:]
    plan = qkv_plan(w_refs, w_scr, meta, sems)
    if nw > 1:
        gain_copies = [
            pltpu.make_async_copy(
                w_refs[1 + k].at[pl.ds(PIECE, 16), pl.ds(0, 256)], g_scr.at[k], gsems.at[k]
            )
            for k in range(3)
        ]
        start_all(gain_copies)
        plan_start(plan, meta)
        wait_all(gain_copies)
        me, zpar = meta[0], meta[2]
        own = gain_ref[...].astype(F32)
        width = own.shape[1]
        for b in range(D // width):
            value = own
            for k, rel in enumerate((1 + zpar, 2 - zpar, 3)):
                value = jnp.where((me ^ rel) == b, g_scr[k][:2, :width].astype(F32), value)
            gains_out[:2, b * width : (b + 1) * width] = value
    else:
        plan_start(plan, meta)
        gains_out[:2] = gain_ref[...].astype(F32)
    gains_out[2:] = jnp.zeros((6, D), F32)
    n_ref[...] = (scaled_ref[...] * gains_out[0:1, :]).astype(BF)
    plan_wait(plan, meta)
    tokens = n_ref.shape[0]
    j_scr[...] = jnp.dot(n_ref[...], w_scr[:, 896:QKV], preferred_element_type=F32)
    lane = lanes()
    cosine = cos_ref[...]
    sine = sin_ref[...]
    keys = {}
    for t in range(7, 10):
        at = 128 * (t - 7)
        tile = rope_tile(j_scr[:, at : at + 128], cosine, sine)
        for half in range(2):
            if 2 * t + half >= HEADS:
                keys[2 * t + half - HEADS] = tile if half == 0 else pltpu.roll(tile, 64, 1)
    for g in range(KV_HEADS):
        t = 10 + g // 2
        if t == 12:
            last = j_scr[:, 640:704]
            value = jnp.concatenate([last, last], axis=1)
        else:
            value = j_scr[:, 128 * (t - 7) : 128 * (t - 6)]
            if g % 2 == 0:
                value = pltpu.roll(value, 64, 1)
        both = jnp.where(lane < 64, keys[g], value).astype(BF)
        kv_ref, at = (kva_ref, g) if g < FIRST else (kvb_ref, g - FIRST)
        kv_ref[:tokens, 128 * at : 128 * (at + 1)] = both
        key = jnp.where(lane < 64, both.astype(F32), 0.0)
        top = jnp.max(jnp.sum(key * key, axis=1, keepdims=True), axis=0, keepdims=True)
        kv_ref[tokens:, 128 * at : 128 * (at + 1)] = jnp.broadcast_to(
            top * 1.02, (NORM_ROWS, 128)
        ).astype(BF)
    repeat_rows(kva_ref, kva_out, shards)


def repeat_rows(source, target, shards):
    rows = source.shape[0]
    for j in range(shards):
        target[j * rows : (j + 1) * rows] = source[...]


def kv_call(meta, scaled, gain, cosine, sine, weights, shards):
    tokens = scaled.shape[0]
    nw = len(weights)
    return pl.pallas_call(
        functools.partial(kv_body, nw, shards),
        in_specs=[SCALARS] + [WHOLE] * 4 + [ANY] * nw,
        out_specs=[WHOLE] * 4,
        out_shape=[
            jax.ShapeDtypeStruct((tokens, D), BF),
            jax.ShapeDtypeStruct((8, D), F32),
            jax.ShapeDtypeStruct((shards * (tokens + NORM_ROWS), FIRST * 128), BF),
            jax.ShapeDtypeStruct((tokens + NORM_ROWS, (KV_HEADS - FIRST) * 128), BF),
        ],
        scratch_shapes=[
            pltpu.VMEM((D, QKV), BF),
            pltpu.VMEM((tokens, QKV - 896), F32),
            pltpu.VMEM((tokens + NORM_ROWS, FIRST * 128), BF),
            pltpu.VMEM((3, 16, 256), BF),
            pltpu.SemaphoreType.DMA((8,)),
            pltpu.SemaphoreType.DMA((3,)),
        ],
        compiler_params=params(),
        cost_estimate=cost(2 * tokens * D * 704, 6 << 20),
        name="kv_project",
    )(meta, scaled, gain, cosine, sine, *weights)


def q_body(nw, shards, meta, n_ref, cos_ref, sin_ref, kvb_ref, *refs):
    w_refs = refs[:nw]
    q_ref, qn_ref, kvb_out, w_scr, j_scr, sems = refs[nw:]
    plan = qkv_plan(w_refs, w_scr, meta, sems)
    plan_start(plan, meta)
    repeat_rows(kvb_ref, kvb_out, shards)
    plan_wait(plan, meta)
    tokens = n_ref.shape[0]
    j_scr[...] = jnp.dot(n_ref[...], w_scr[:, :1024], preferred_element_type=F32)
    lane = lanes()
    cosine = cos_ref[...]
    sine = sin_ref[...]
    top_q = jnp.zeros((tokens, 1), F32)
    for t in range(8):
        tile = rope_tile(j_scr[:, 128 * t : 128 * (t + 1)], cosine, sine)
        for half in range(2):
            head = 2 * t + half
            if head >= HEADS:
                continue
            part = tile if half == 0 else pltpu.roll(tile, 64, 1)
            part = jnp.where(lane < 64, part * (LOG2E * 0.125), 0.0).astype(BF)
            q_ref[head] = part
            part = part.astype(F32)
            top_q = jnp.maximum(top_q, jnp.sum(part * part, axis=1, keepdims=True))
    qn_ref[...] = jnp.broadcast_to(jnp.max(top_q, axis=0, keepdims=True) * 1.02, (8, 128))


def q_call(meta, n1, cosine, sine, kvb, weights, shards):
    tokens = n1.shape[0]
    nw = len(weights)
    return pl.pallas_call(
        functools.partial(q_body, nw, shards),
        in_specs=[SCALARS] + [WHOLE] * 4 + [ANY] * nw,
        out_specs=[WHOLE] * 3,
        out_shape=[
            jax.ShapeDtypeStruct((HEADS, tokens, 128), BF),
            jax.ShapeDtypeStruct((8, 128), F32),
            jax.ShapeDtypeStruct((shards * kvb.shape[0], kvb.shape[1]), BF),
        ],
        scratch_shapes=[
            pltpu.VMEM((D, QKV), BF),
            pltpu.VMEM((tokens, 1024), F32),
            pltpu.SemaphoreType.DMA((8,)),
        ],
        compiler_params=params(),
        cost_estimate=cost(2 * tokens * D * 1024, 8 << 20),
        name="q_project",
    )(meta, n1, cosine, sine, kvb, *weights)


def load_rows(shards, tokens, source, kv_scr, sem, nrm_scr=None, nsem=None):
    copies = []
    for j in range(shards):
        base = j * (tokens + NORM_ROWS)
        for h in range(kv_scr.shape[0]):
            copies.append(
                pltpu.make_async_copy(
                    source.at[pl.ds(base, tokens), pl.ds(h * 128, 128)],
                    kv_scr.at[h, pl.ds(j * tokens, tokens), :],
                    sem.at[j, h],
                )
            )
        if nrm_scr is not None:
            copies.append(
                pltpu.make_async_copy(
                    source.at[pl.ds(base + tokens, NORM_ROWS), :], nrm_scr.at[j], nsem.at[j]
                )
            )
    start_all(copies)
    wait_all(copies)


def pair_range(meta, c):
    t_lo = meta[4 + 2 * c]
    t_hi = meta[5 + 2 * c]
    odd = (t_hi - t_lo) & 1
    start = jnp.where((odd == 1) & (t_lo > 0), t_lo - 1, t_lo)
    return start, (t_hi - t_lo + odd) // 2


def attend_forward_body(shards, tokens, meta, q_ref, qm_ref, qn_ref, aug_ref, *refs):
    source = refs[0]
    o_ref, q2_ref, kv_scr, acc_scr, m_scr, nrm_scr, sem, nsem = refs[-8:]
    g = pl.program_id(0)
    c = pl.program_id(1)

    @pl.when((g == 0) & (c == 0))
    def _():
        load_rows(shards, tokens, source, kv_scr, sem, nrm_scr, nsem)

    lane = lanes()
    qm = qm_ref[...]
    rows_all = GROUP * QC
    acc_scr[...] = jnp.zeros_like(acc_scr)
    q2_ref[...] = jnp.where(lane < 64, q_ref[...], qm[None])
    safe = jnp.max(qn_ref[...]) * jnp.max(nrm_scr[...].astype(F32)) < SAFE * SAFE
    start, pairs = pair_range(meta, c)

    def tiles(u):
        rows = pl.ds(pl.multiple_of((start + 2 * u) * KT, KT), 2 * KT)
        kv = kv_scr[g, rows, :]
        return (
            jnp.where(lane < 64, kv, aug_ref[rows, :]),
            jnp.where(lane < 64, jnp.ones_like(kv), kv),
        )

    @pl.when(safe)
    def _():
        def step(u, carry):
            keys, values = tiles(u)
            scores = lax.dot_general(
                q2_ref[...].reshape(rows_all, 128), keys, NT, preferred_element_type=F32
            )
            weights = jnp.exp2(scores).astype(BF)
            acc_scr[...] += jnp.dot(weights, values, preferred_element_type=F32)
            return carry

        lax.fori_loop(0, pairs, step, 0)
        m_scr[...] = jnp.zeros_like(m_scr)

    @pl.when(jnp.logical_not(safe))
    def _():
        m_scr[...] = jnp.full_like(m_scr, -1e30)

        def step(u, carry):
            keys, values = tiles(u)

            def head(h, carry):
                scores = lax.dot_general(q2_ref[h], keys, NT, preferred_element_type=F32)
                rows = pl.ds(pl.multiple_of(h * QC, QC), QC)
                old = m_scr[rows, :1]
                new = jnp.maximum(old, jnp.max(scores, axis=1, keepdims=True))
                weights = jnp.exp2(scores - new).astype(BF)
                acc_scr[rows, :] = acc_scr[rows, :] * jnp.exp2(old - new) + jnp.dot(
                    weights, values, preferred_element_type=F32
                )
                m_scr[rows, :] = jnp.broadcast_to(new, (QC, 128))
                return carry

            return lax.fori_loop(0, GROUP, head, carry)

        lax.fori_loop(0, pairs, step, 0)

    def finish(h, carry):
        rows = pl.ds(pl.multiple_of(h * QC, QC), QC)
        acc = acc_scr[rows, :]
        other = pltpu.roll(acc, 64, 1)
        o_ref[h] = jnp.where(lane < 64, 0.0, acc / jnp.where(lane < 64, 1.0, other)).astype(BF)
        total = jnp.where(lane < 64, acc, other)
        high, mid, low = split3(-(m_scr[rows, :] + jnp.log2(total)))
        with_log = jnp.where(lane == LANE_LOG + 2, low, q2_ref[h])
        with_log = jnp.where(lane == LANE_LOG + 1, mid, with_log)
        q2_ref[h] = jnp.where(lane == LANE_LOG, high, with_log)
        return carry

    lax.fori_loop(0, GROUP, finish, 0)


def attend_forward(meta, q, qm, qn, aug, kv, first, deps):
    tokens = q.shape[1]
    shards = kv.shape[0] // (tokens + NORM_ROWS)
    heads = kv.shape[1] // 128
    row = shards * tokens
    block = pl.BlockSpec((GROUP, QC, 128), lambda g, c, m: (g, c, 0))
    return pl.pallas_call(
        functools.partial(attend_forward_body, shards, tokens),
        grid_spec=pltpu.PrefetchScalarGridSpec(
            num_scalar_prefetch=1,
            grid=(heads, tokens // QC),
            in_specs=[
                pl.BlockSpec((GROUP, QC, 128), lambda g, c, m: (g + first, c, 0)),
                pl.BlockSpec((QC, 128), lambda g, c, m: (c, 0)),
                pl.BlockSpec((8, 128), lambda g, c, m: (0, 0)),
                pl.BlockSpec((row, 128), lambda g, c, m: (0, 0)),
            ]
            + [ANY] * (1 + len(deps)),
            out_specs=[block, block],
            scratch_shapes=[
                pltpu.VMEM((heads, row, 128), BF),
                pltpu.VMEM((GROUP * QC, 128), F32),
                pltpu.VMEM((GROUP * QC, 128), F32),
                pltpu.VMEM((shards, NORM_ROWS, heads * 128), BF),
                pltpu.SemaphoreType.DMA((shards, heads)),
                pltpu.SemaphoreType.DMA((shards,)),
            ],
        ),
        out_shape=[jax.ShapeDtypeStruct((GROUP * heads, tokens, 128), BF)] * 2,
        compiler_params=params(),
        cost_estimate=cost(16 * GROUP * heads * tokens * row * 128, 10 << 20),
        name="attend_forward",
    )(meta, q, qm, qn, aug, kv, *deps)


def attend_backward_body(shards, tokens, meta, qa_ref, qb_ref, do_ref, aug_ref, *refs):
    kva, kvb = refs[:2]
    dq_ref, out_ref, kv_scr, q_scr, dkv_scr, ob_scr, dq_scr, qt_scr, sem, osem = refs[-10:]
    g = pl.program_id(0)
    c = pl.program_id(1)

    @pl.when((g == 0) & (c == 0))
    def _():
        load_rows(shards, tokens, kva, kv_scr.at[pl.ds(0, FIRST)], sem.at[0])
        load_rows(shards, tokens, kvb, kv_scr.at[pl.ds(FIRST, KV_HEADS - FIRST)], sem.at[1])

    @pl.when(c == 0)
    def _():
        dkv_scr[...] = jnp.zeros_like(dkv_scr)

    lane = lanes()
    rows_all = GROUP * QC
    dq_scr[...] = jnp.zeros_like(dq_scr)
    q_scr[...] = jnp.where(g < FIRST, qa_ref[...], qb_ref[...])
    qt_scr[...] = jnp.transpose(
        jnp.where(lane < 64, q_scr[...], do_ref[...]).reshape(rows_all, 128)
    )
    start, pairs = pair_range(meta, c)

    def step(u, carry):
        tile = start + 2 * u
        rows = pl.ds(pl.multiple_of(tile * KT, KT), 2 * KT)
        kv = kv_scr[g, rows, :]
        ones = jnp.where(lane >= LANE_INNER, jnp.ones_like(kv), jnp.zeros_like(kv))
        keys = jnp.where(lane < 64, kv, aug_ref[rows, :])
        values = jnp.where(lane < 64, ones, kv)
        queries = q_scr[...].reshape(rows_all, 128)
        grads = do_ref[...].reshape(rows_all, 128)
        weights = jnp.exp2(lax.dot_general(queries, keys, NT, preferred_element_type=F32))
        inner = lax.dot_general(grads, values, NT, preferred_element_type=F32)
        grad_scores = (weights * inner).astype(BF)
        weights = weights.astype(BF)
        dq_scr[...] += jnp.dot(grad_scores, keys, preferred_element_type=F32)
        for i in range(2):
            part = slice(i * KT, (i + 1) * KT)
            dkv_scr[tile + i, :64] += jnp.dot(
                qt_scr[:64], grad_scores[:, part], preferred_element_type=F32
            )
            dkv_scr[tile + i, 64:] += jnp.dot(
                qt_scr[64:], weights[:, part], preferred_element_type=F32
            )
        return carry

    lax.fori_loop(0, pairs, step, 0)
    dq_ref[...] = dq_scr[...].reshape(GROUP, QC, 128) * 0.125

    @pl.when(c == pl.num_programs(1) - 1)
    def _():
        for t in range(shards * tokens // KT):
            both = dkv_scr[t]
            both = jnp.concatenate([both[:64] * LN2, both[64:]], axis=0)
            ob_scr[t * KT : (t + 1) * KT, :] = jnp.transpose(both).astype(BF)
        at = pl.ds(pl.multiple_of(g * 128, 128), 128)
        copy = pltpu.make_async_copy(ob_scr, out_ref.at[:, at], osem)
        copy.start()
        copy.wait()


def attend_backward(meta, qa, qb, do, aug, kva, kvb, deps):
    tokens = qa.shape[1]
    shards = kva.shape[0] // (tokens + NORM_ROWS)
    row = shards * tokens
    rows_all = GROUP * QC
    block = pl.BlockSpec((GROUP, QC, 128), lambda g, c, m: (g, c, 0))
    return pl.pallas_call(
        functools.partial(attend_backward_body, shards, tokens),
        grid_spec=pltpu.PrefetchScalarGridSpec(
            num_scalar_prefetch=1,
            grid=(KV_HEADS, tokens // QC),
            in_specs=[
                pl.BlockSpec((GROUP, QC, 128), lambda g, c, m: (jnp.minimum(g, FIRST - 1), c, 0)),
                pl.BlockSpec((GROUP, QC, 128), lambda g, c, m: (jnp.maximum(g - FIRST, 0), c, 0)),
                block,
                pl.BlockSpec((row, 128), lambda g, c, m: (0, 0)),
            ]
            + [ANY] * (2 + len(deps)),
            out_specs=[block, ANY],
            scratch_shapes=[
                pltpu.VMEM((KV_HEADS, row, 128), BF),
                pltpu.VMEM((GROUP, QC, 128), BF),
                pltpu.VMEM((row // KT, 128, KT), F32),
                pltpu.VMEM((row, 128), BF),
                pltpu.VMEM((rows_all, 128), F32),
                pltpu.VMEM((128, rows_all), BF),
                pltpu.SemaphoreType.DMA((2, shards, KV_HEADS)),
                pltpu.SemaphoreType.DMA(()),
            ],
        ),
        out_shape=[
            jax.ShapeDtypeStruct((HEADS, tokens, 128), F32),
            jax.ShapeDtypeStruct((row, KV_HEADS * 128), BF),
        ],
        compiler_params=params(),
        cost_estimate=cost(1, 1),
        name="attend_backward",
    )(meta, qa, qb, do, aug, kva, kvb, *deps)


MLP_TILE = 640


COT_ROWS = D // 2


def residual_body(nw, meta, x_ref, oa_ref, ob_ref, gain_ref, n1_ref, cot_ref, *refs):
    w_refs = refs[:nw]
    res_ref, n2_ref, mix_ref, own_ref, send_ref, proj_scr, sems = refs[nw:]
    plan = proj_plan_of(w_refs, proj_scr, meta, sems)
    plan_start(plan, meta)
    lane = lanes()
    core = meta[1]

    def o_of(head):
        return oa_ref[head] if head < GROUP * FIRST else ob_ref[head - GROUP * FIRST]

    for t in range(8):
        low = pltpu.roll(o_of(2 * t).astype(F32), 64, 1)
        if t < 7:
            tile = jnp.where(lane < 64, low, o_of(2 * t + 1).astype(F32)).astype(BF)
            mix_ref[:, 128 * t : 128 * (t + 1)] = tile
        else:
            mix_ref[:, 896:960] = low[:, :64].astype(BF)
    low, high = cot_ref[:COT_ROWS], cot_ref[COT_ROWS:]
    own_ref[:COT_ROWS] = jnp.where(core == 0, low, high)
    send_ref[:COT_ROWS] = jnp.where(core == 0, high, low)
    tokens = x_ref.shape[0]
    width = D // 4
    for b in range(4):
        rows = slice(COT_ROWS + b * tokens, COT_ROWS + (b + 1) * tokens)
        for at, ref in ((256, mix_ref), (384, n1_ref)):
            low = ref[:, b * width : b * width + PIECE]
            high = ref[:, (b + 1) * width - PIECE : (b + 1) * width]
            own_ref[rows, at : at + 128] = jnp.where(core == 0, low, high)
            send_ref[rows, at : at + 128] = jnp.where(core == 0, high, low)
    plan_wait(plan, meta)
    residual = x_ref[...].astype(F32) + jnp.dot(
        mix_ref[...], proj_scr[:, :D], preferred_element_type=F32
    )
    res_ref[...] = residual
    scale = lax.rsqrt(jnp.mean(residual * residual, axis=1, keepdims=True) + NORM_EPSILON)
    n2_ref[...] = (residual * scale * gain_ref[1:2, :]).astype(BF)
    for b in range(4):
        rows = slice(COT_ROWS + b * tokens, COT_ROWS + (b + 1) * tokens)
        block = n2_ref[:, b * width : (b + 1) * width]
        for ref in (own_ref, send_ref):
            ref[rows, 128:256] = jnp.zeros((tokens, 128), BF)
            ref[rows, :width] = block


def residual_call(meta, x, oa, ob, gains, n1, cot_t, proj):
    tokens = x.shape[0]
    nw = len(proj)
    return pl.pallas_call(
        functools.partial(residual_body, nw),
        in_specs=[SCALARS] + [WHOLE] * 6 + [ANY] * nw,
        out_specs=[WHOLE] * 5,
        out_shape=[
            jax.ShapeDtypeStruct((tokens, D), F32),
            jax.ShapeDtypeStruct((tokens, D), BF),
            jax.ShapeDtypeStruct((tokens, D), BF),
        ]
        + [jax.ShapeDtypeStruct((COT_ROWS + 4 * tokens, 512), BF)] * 2,
        scratch_shapes=[pltpu.VMEM((D, 1024), BF), pltpu.SemaphoreType.DMA((13,))],
        compiler_params=params(),
        cost_estimate=cost(2 * tokens * D * D, 10 << 20),
        name="residual",
    )(meta, x, oa, ob, gains, n1, cot_t, *proj)


def mlp_body(counts, meta, res_ref, n2_ref, cot_ref, *refs):
    n_gu, n_down = counts
    gu_refs = refs[:n_gu]
    down_refs = refs[n_gu : n_gu + n_down]
    (
        out_ref,
        dn_scr,
        act_ref,
        late_own_ref,
        late_send_ref,
        gu_scr,
        down_scr,
        acc_scr,
        act_scr,
        dgu_scr,
        gu_sems,
        down_sems,
        out_sems,
    ) = refs[n_gu + n_down :]
    down_plan = down_copies(down_refs, down_scr, meta, down_sems)
    gu_copies = gateup_copies(gu_refs, gu_scr, meta, gu_sems, MLP_TILE)
    start_all(gu_copies[0])
    start_all(down_plan)
    for one in gu_copies[1:]:
        start_all(one)
    tiles = FF // MLP_TILE
    core = meta[1]
    out_copies = []
    for f in range(tiles):
        cols = slice(f * MLP_TILE, (f + 1) * MLP_TILE)
        wait_all(gu_copies[f])
        normed = n2_ref[...]
        gate = jnp.dot(normed, gu_scr[0, :, cols], preferred_element_type=F32)
        up = jnp.dot(normed, gu_scr[1, :, cols], preferred_element_type=F32)
        if f == 0:
            wait_all(down_plan)
        grad_act = jnp.dot(cot_ref[...], down_scr[:, cols], preferred_element_type=F32)
        gated = 1.0 / (1.0 + jnp.exp(-gate))
        silu = gate * gated
        act = (silu * up).astype(BF)
        grad_gate = (grad_act * up * gated * (1.0 + gate * (1.0 - gated))).astype(BF)
        grad_up = (grad_act * silu).astype(BF)
        act_scr[f] = act
        dgu_scr[0, :, cols] = grad_gate
        dgu_scr[1, :, cols] = grad_up
        add_out = lax.dot_general(act, down_scr[:, cols], NT, preferred_element_type=F32)
        add_dn = lax.dot_general(
            grad_gate, gu_scr[0, :, cols], NT, preferred_element_type=F32
        ) + lax.dot_general(grad_up, gu_scr[1, :, cols], NT, preferred_element_type=F32)
        if f == 0:
            acc_scr[...] = add_out
            dn_scr[...] = add_dn
        else:
            acc_scr[...] += add_out
            dn_scr[...] += add_dn
        copies = [pltpu.make_async_copy(act_scr.at[f], act_ref.at[f], out_sems.at[f, 0])]
        for i, ref in enumerate((late_own_ref, late_send_ref)):
            copies.append(
                pltpu.make_async_copy(
                    dgu_scr.at[core if i == 0 else 1 - core, :, pl.ds(f * MLP_TILE, MLP_TILE)],
                    ref.at[:, pl.ds(f * MLP_TILE, MLP_TILE)],
                    out_sems.at[f, 2 + i],
                )
            )
        start_all(copies)
        out_copies += copies
    out_ref[...] = transposed_back((res_ref[...] + acc_scr[...]).astype(BF))
    wait_all(out_copies)


def norm_back_body(nw, meta, res_ref, dn_ref, cot_ref, mix_ref, gain_ref, *refs):
    proj_refs = refs[:nw]
    gres_ref, gb_ref, do_ref, gain_out_ref, proj_scr, dn_scr, sems = refs[nw:]
    proj_plan = proj_plan_of(proj_refs, proj_scr, meta, sems)
    plan_start(proj_plan, meta)
    lane = lanes()
    gain = gain_ref[1:2, :]
    residual = res_ref[...]
    scale = lax.rsqrt(jnp.mean(residual * residual, axis=1, keepdims=True) + NORM_EPSILON)
    grad = dn_ref[...]
    gain_out_ref[...] = jnp.broadcast_to(
        jnp.sum(grad * residual * scale, axis=0, keepdims=True), (8, D)
    )
    scaled = grad * gain
    mean = jnp.mean(scaled * residual, axis=1, keepdims=True)
    grad_residual = (
        cot_ref[...].astype(F32) + scale * scaled - residual * (scale * scale * scale * mean)
    )
    gres_ref[...] = grad_residual
    branch = grad_residual.astype(BF)
    gb_ref[:, :D] = branch
    gb_ref[:, D:] = jnp.zeros((branch.shape[0], 1024 - D), BF)
    plan_wait(proj_plan, meta)
    dn_scr[...] = lax.dot_general(
        gb_ref[:, :D], proj_scr[:, :D], NT, preferred_element_type=F32
    )
    ones = (
        (lax.broadcasted_iota(jnp.int32, (128, 128), 0) < 64)
        == (lax.broadcasted_iota(jnp.int32, (128, 128), 1) < 64)
    ).astype(BF)
    half_lane = lane % 64
    for t in range(8):
        if t < 7:
            gm = dn_scr[:, 128 * t : 128 * (t + 1)].astype(BF)
            mixed = mix_ref[:, 128 * t : 128 * (t + 1)]
        else:
            gm = dn_scr[:, 896:960].astype(BF)
            gm = jnp.concatenate([gm, jnp.zeros_like(gm)], axis=1)
            mixed = mix_ref[:, 896:960]
            mixed = jnp.concatenate([mixed, jnp.zeros_like(mixed)], axis=1)
        gm = gm.astype(F32)
        product = gm * mixed.astype(F32)
        high = product.astype(BF)
        low = (product - high.astype(F32)).astype(BF)
        inner = jnp.dot(high, ones, preferred_element_type=F32) + jnp.dot(
            low, ones, preferred_element_type=F32
        )
        high, mid, low = split3(-inner)
        extra = jnp.where(half_lane == LANE_INNER + 2, low.astype(F32), 0.0)
        extra = jnp.where(half_lane == LANE_INNER + 1, mid.astype(F32), extra)
        extra = jnp.where(half_lane == LANE_INNER, high.astype(F32), extra)
        do_ref[2 * t] = jnp.where(lane < 64, extra, pltpu.roll(gm, 64, 1)).astype(BF)
        if 2 * t + 1 < HEADS:
            do_ref[2 * t + 1] = jnp.where(lane < 64, pltpu.roll(extra, 64, 1), gm).astype(BF)


def norm_back_call(meta, residual, dn, cot, mixed, gains, proj):
    tokens = cot.shape[0]
    nw = len(proj)
    return pl.pallas_call(
        functools.partial(norm_back_body, nw),
        in_specs=[SCALARS] + [WHOLE] * 5 + [ANY] * nw,
        out_specs=[WHOLE] * 4,
        out_shape=[
            jax.ShapeDtypeStruct((tokens, D), F32),
            jax.ShapeDtypeStruct((tokens, 1024), BF),
            jax.ShapeDtypeStruct((HEADS, tokens, 128), BF),
            jax.ShapeDtypeStruct((8, D), F32),
        ],
        scratch_shapes=[
            pltpu.VMEM((D, 1024), BF),
            pltpu.VMEM((tokens, D), F32),
            pltpu.SemaphoreType.DMA((13,)),
        ],
        compiler_params=params(),
        cost_estimate=cost(2 * tokens * D * D, 12 << 20),
        name="norm_backward",
    )(meta, residual, dn, cot, mixed, gains, *proj)


def mlp_call(meta, residual, n2, cot, gateup, down):
    tokens = n2.shape[0]
    counts = (len(gateup), len(down))
    tiles = FF // MLP_TILE
    return pl.pallas_call(
        functools.partial(mlp_body, counts),
        in_specs=[SCALARS] + [WHOLE] * 3 + [ANY] * sum(counts),
        out_specs=[WHOLE] * 2 + [ANY] * 3,
        out_shape=[
            jax.ShapeDtypeStruct((D, tokens), BF),
            jax.ShapeDtypeStruct((tokens, D), F32),
            jax.ShapeDtypeStruct((tiles, tokens, MLP_TILE), BF),
            jax.ShapeDtypeStruct((tokens, FF), BF),
            jax.ShapeDtypeStruct((tokens, FF), BF),
        ],
        scratch_shapes=[
            pltpu.VMEM((2, D, FF), BF),
            pltpu.VMEM((D, FF), BF),
            pltpu.VMEM((tokens, D), F32),
            pltpu.VMEM((tiles, tokens, MLP_TILE), BF),
            pltpu.VMEM((2, tokens, FF), BF),
            pltpu.SemaphoreType.DMA((tiles, 8)),
            pltpu.SemaphoreType.DMA((8,)),
            pltpu.SemaphoreType.DMA((tiles, 4)),
        ],
        compiler_params=params(),
        cost_estimate=cost(2 * tokens * D * (6 * FF), 40 << 20),
        name="feed_forward",
    )(meta, residual, n2, cot, *gateup, *down)


def joined_body(
    nw, shards, meta, dq_ref, cos_ref, sin_ref, x_ref, gain_ref, gres_ref, gain_two_ref, *refs
):
    dkv_ref = refs[0]
    w_refs = refs[1 : 1 + nw]
    gj_ref, ig_ref, w_scr, g_scr, sems = refs[-5:]
    plan = qkv_plan(w_refs, w_scr, meta, sems)
    tokens = x_ref.shape[0]
    plan_start(plan, meta)
    lane = lanes()
    cosine = cos_ref[...]
    sine = -sin_ref[...]
    heads = {}

    def dkv(g):
        if g not in heads:
            at = slice(128 * g, 128 * (g + 1))
            total = dkv_ref[:tokens, at].astype(F32)
            for j in range(1, shards):
                total = total + dkv_ref[j * tokens : (j + 1) * tokens, at].astype(F32)
            heads[g] = (total, pltpu.roll(total, 64, 1))
        return heads[g]

    def dq(h):
        return dq_ref[h]

    def low_half(h):
        if h < HEADS:
            return dq(h)
        if h < HEADS + KV_HEADS:
            return dkv(h - HEADS)[0]
        return dkv(h - HEADS - KV_HEADS)[1]

    def high_half(h):
        if h < HEADS:
            return pltpu.roll(dq(h), 64, 1)
        if h < HEADS + KV_HEADS:
            return dkv(h - HEADS)[1]
        return dkv(h - HEADS - KV_HEADS)[0]

    for t in range(13):
        if t == 12:
            last = jnp.where(lane < 64, low_half(24), 0.0).astype(BF)
            gj_ref[:tokens, 1536:1664] = last
            continue
        tile = jnp.where(lane < 64, low_half(2 * t), high_half(2 * t + 1))
        if t < 10:
            tile = rope_tile(tile, cosine, sine)
        gj_ref[:tokens, 128 * t : 128 * (t + 1)] = tile.astype(BF)
    plan_wait(plan, meta)
    g_scr[...] = lax.dot_general(
        gj_ref[:tokens, :QKV], w_scr[...], NT, preferred_element_type=F32
    )
    grad = g_scr[...]
    x = x_ref[...].astype(F32)
    scale = lax.rsqrt(jnp.mean(x * x, axis=1, keepdims=True) + NORM_EPSILON)
    gj_ref[tokens:, :] = jnp.zeros((16, gj_ref.shape[1]), BF)
    gain_one = jnp.sum(grad * x * scale, axis=0, keepdims=True)
    gj_ref[tokens : tokens + 2, :D] = jnp.concatenate(
        [gain_one, gain_two_ref[:1]], axis=0
    ).astype(BF)
    scaled = grad * gain_ref[0:1, :]
    mean = jnp.mean(scaled * x, axis=1, keepdims=True)
    ig_ref[...] = transposed_back(
        gres_ref[...] + scale * scaled - x * (scale * scale * scale * mean)
    )


def joined_call(meta, dq, cosine, sine, x, gains, gres, gain_two, dkv, weights, deps):
    tokens = x.shape[0]
    nw = len(weights)
    shards = dkv.shape[0] // tokens
    return pl.pallas_call(
        functools.partial(joined_body, nw, shards),
        in_specs=[SCALARS] + [WHOLE] * 8 + [ANY] * (nw + len(deps)),
        out_specs=[WHOLE] * 2,
        out_shape=[
            jax.ShapeDtypeStruct((tokens + 16, 1664), BF),
            jax.ShapeDtypeStruct((D, tokens), F32),
        ],
        scratch_shapes=[
            pltpu.VMEM((D, QKV), BF),
            pltpu.VMEM((tokens, D), F32),
            pltpu.SemaphoreType.DMA((8,)),
        ],
        compiler_params=params(),
        cost_estimate=cost(2 * tokens * D * QKV, 16 << 20),
        name="joined_backward",
    )(meta, dq, cosine, sine, x, gains, gres, gain_two, dkv, *weights, *deps)


def block_rows(block, tokens):
    return slice(COT_ROWS + block * tokens, COT_ROWS + (block + 1) * tokens)


def gateup_grad_body(meta, own_ref, oth_ref, b_own, b_oth, *refs):
    out = refs[-1]
    tokens = b_own.shape[0]
    width = D // 4
    for j in range(4):
        rows = block_rows(j, tokens)
        total = lax.dot_general(
            own_ref[rows, 0:256], b_own[...], TN, preferred_element_type=F32
        ) + lax.dot_general(oth_ref[rows, 0:256], b_oth[...], TN, preferred_element_type=F32)
        out[j * width : (j + 1) * width] = total[:width].astype(BF)


def gateup_grad_call(meta, early_own, early_oth, late_own, late_oth, deps):
    tokens = late_own.shape[0]
    tile = 640
    whole = pl.BlockSpec(early_own.shape, lambda i, s: (0, 0))
    cols = pl.BlockSpec((tokens, tile), lambda i, s: (0, i))
    return pl.pallas_call(
        gateup_grad_body,
        grid_spec=pltpu.PrefetchScalarGridSpec(
            num_scalar_prefetch=1,
            grid=(FF // tile,),
            in_specs=[whole] * 2 + [cols] * 2 + [ANY] * len(deps),
            out_specs=pl.BlockSpec((D, tile), lambda i, s: (0, i)),
        ),
        out_shape=jax.ShapeDtypeStruct((D, FF), BF),
        compiler_params=params(),
        cost_estimate=cost(4 * tokens * D * FF, 20 << 20),
        name="gateup_gradient",
    )(meta, early_own, early_oth, late_own, late_oth, *deps)


DP_ROWS = COT_ROWS + 2 * PIECE


def down_proj_grad_body(meta, own_ref, oth_ref, act_own, act_oth, gb_own, gb_oth, *refs):
    tokens = gb_own.shape[0]
    for block in range(4):
        out = refs[-1].at[pl.ds(block * DP_ROWS, DP_ROWS)]
        total = jnp.dot(
            own_ref[:COT_ROWS], act_own[block], preferred_element_type=F32
        ) + jnp.dot(oth_ref[:COT_ROWS], act_oth[block], preferred_element_type=F32)
        out[:COT_ROWS] = total.astype(BF)
        rows = block_rows(block, tokens)
        total = lax.dot_general(
            own_ref[rows, 256:384], gb_own[...], TN, preferred_element_type=F32
        ) + lax.dot_general(oth_ref[rows, 256:384], gb_oth[...], TN, preferred_element_type=F32)
        total = total.astype(BF)
        out[COT_ROWS : COT_ROWS + PIECE] = total[:, :640]
        out[COT_ROWS + PIECE :, :384] = total[:, 640:]
        out[COT_ROWS + PIECE :, 384:] = jnp.zeros((PIECE, 256), BF)


def down_proj_grad_call(meta, early_own, early_oth, act_own, act_oth, gb_own, gb_oth, deps):
    blocks, tokens, width = act_own.shape
    return pl.pallas_call(
        down_proj_grad_body,
        in_specs=[SCALARS] + [WHOLE] * 6 + [ANY] * len(deps),
        out_specs=WHOLE,
        out_shape=jax.ShapeDtypeStruct((4 * DP_ROWS, width), BF),
        compiler_params=params(),
        cost_estimate=cost(2 * tokens * D * (FF + D), 16 << 20),
        name="down_proj_gradient",
    )(meta, early_own, early_oth, act_own, act_oth, gb_own, gb_oth, *deps)


def qkv_grad_body(meta, own_ref, oth_ref, gj_own, gj_oth, *refs):
    tokens = gj_own.shape[0] - 16
    width = D // 4
    sums = (
        gj_own[tokens : tokens + 16, :].astype(F32) + gj_oth[tokens : tokens + 16, :].astype(F32)
    ).astype(BF)
    for block in range(4):
        rows = block_rows(block, tokens)
        total = lax.dot_general(
            own_ref[rows, 384:512], gj_own[:tokens, :], TN, preferred_element_type=F32
        ) + lax.dot_general(
            oth_ref[rows, 384:512], gj_oth[:tokens, :], TN, preferred_element_type=F32
        )
        total = total[:, :QKV].astype(BF)
        part = sums[:, block * width : (block + 1) * width]
        part = jnp.concatenate([part, jnp.zeros((PIECE_ROWS - PIECE, QKV - width), BF)], axis=1)
        for j, out in enumerate(refs[-4:]):

            @pl.when((meta[0] ^ j) == block)
            def _(out=out, total=total, part=part):
                out[:PIECE] = total
                out[PIECE:] = part


def qkv_grad_call(meta, early_own, early_oth, gj_own, gj_oth, deps):
    return pl.pallas_call(
        qkv_grad_body,
        in_specs=[SCALARS] + [WHOLE] * 4 + [ANY] * len(deps),
        out_specs=[WHOLE] * 4,
        out_shape=[jax.ShapeDtypeStruct((PIECE_ROWS, QKV), BF)] * 4,
        compiler_params=params(),
        cost_estimate=cost(2 * gj_own.shape[0] * D * QKV, 8 << 20),
        name="qkv_gradient",
    )(meta, early_own, early_oth, gj_own, gj_oth, *deps)


def total_of(refs, blocks=1):
    total = None
    for ref in refs:
        rows = ref.shape[0] // blocks
        for i in range(blocks):
            term = ref[i * rows : (i + 1) * rows].astype(F32)
            total = term if total is None else total + term
    return total.astype(BF)


def cut_along(value, axis, parts):
    size = value.shape[axis] // parts
    if axis == 0:
        return [value[i * size : (i + 1) * size] for i in range(parts)]
    return [value[:, i * size : (i + 1) * size] for i in range(parts)]


def add_job(inputs, blocks=1):
    rows, columns = inputs[0].shape

    def body(meta, ins, outs):
        outs[0][...] = total_of(ins, blocks)

    return inputs, [(rows // blocks, columns)], body


def copy_job(value):
    def body(meta, ins, outs):
        outs[0][...] = ins[0][...]

    return [value], [value.shape], body


def rows_job(value, rows):
    def body(meta, ins, outs):
        at = pl.multiple_of(meta[1] * rows, 16)
        outs[0][...] = ins[0][pl.ds(at, rows), :]

    return [value], [(rows, value.shape[1])], body


def split_job(inputs, axis, at, blocks=1):
    shape = list(inputs[0].shape)
    shape[0] //= blocks
    shape[axis] //= 2

    def body(meta, ins, outs):
        low, high = cut_along(total_of(ins, blocks), axis, 2)
        bit = meta[at]
        outs[0][...] = jnp.where(bit == 0, low, high)
        outs[1][...] = jnp.where(bit == 0, high, low)

    return inputs, [tuple(shape)] * 2, body


def join_job(mine, theirs, axis, at):
    shape = list(mine.shape)
    shape[axis] *= 2

    def body(meta, ins, outs):
        bit = meta[at]
        a, b = ins[0][...], ins[1][...]
        low, high = jnp.where(bit == 0, a, b), jnp.where(bit == 0, b, a)
        size = a.shape[axis]
        if axis == 0:
            outs[0][:size] = low
            outs[0][size:] = high
        else:
            outs[0][:, :size] = low
            outs[0][:, size:] = high

    return [mine, theirs], [tuple(shape)], body


def whole_job(inputs):
    rows, columns = inputs[0].shape

    def body(meta, ins, outs):
        place = meta[2] + 2 * meta[3]
        for i in range(4):
            back = (place + 4 - i) % 4
            value = ins[3][...]
            for k in range(3):
                value = jnp.where(back == k, ins[k][...], value)
            outs[0][i * rows : (i + 1) * rows] = value

    return inputs, [(4 * rows, columns)], body


def stage_body(jobs, meta, *refs):
    outs = refs[-sum(len(job[1]) for job in jobs) :]
    at_in = at_out = 0
    for ins, shapes, body in jobs:
        body(meta, refs[at_in : at_in + len(ins)], outs[at_out : at_out + len(shapes)])
        at_in += len(ins)
        at_out += len(shapes)


def stage(name, meta, jobs, deps):
    inputs = [one for job in jobs for one in job[0]]
    shapes = [shape for job in jobs for shape in job[1]]
    results = pl.pallas_call(
        functools.partial(stage_body, jobs),
        in_specs=[SCALARS] + [WHOLE] * len(inputs) + [ANY] * len(deps),
        out_specs=[WHOLE] * len(shapes),
        out_shape=[jax.ShapeDtypeStruct(shape, BF) for shape in shapes],
        compiler_params=params(),
        cost_estimate=cost(0, 8 << 20),
        name=name,
    )(meta, *inputs, *deps)
    grouped, at = [], 0
    for job in jobs:
        grouped.append(list(results[at : at + len(job[1])]))
        at += len(job[1])
    return grouped


def adamw_step(grad_sum, master, first, second, rate, decay):
    first_new = BETA_FIRST * first + (1.0 - BETA_FIRST) * grad_sum
    second_new = BETA_SECOND * second + (1.0 - BETA_SECOND) * grad_sum * grad_sum
    corrected = (
        first_new
        / (1.0 - BETA_FIRST**STEP)
        / (jnp.sqrt(second_new / (1.0 - BETA_SECOND**STEP)) + ADAM_EPSILON)
    )
    master_new = master - rate * (corrected + decay * master)
    return (master_new, master_new.astype(jnp.bfloat16), first_new, second_new)


def pick_core(meta, half, mine, other):
    return jnp.where(meta[1] == half, mine, other).astype(F32)


def gateup_grads(meta, step, mine, other):
    return pick_core(meta, step // 4, mine[...], other[...])


def down_grads(meta, step, mine, other):
    return pick_core(meta, step // 2, mine[...], other[...])


def proj_grads(meta, step, mine, other):
    def piece(half):
        top = pick_core(meta, half, mine[COT_ROWS : COT_ROWS + PIECE], other[COT_ROWS : COT_ROWS + PIECE])
        rest = pick_core(meta, half, mine[COT_ROWS + PIECE :], other[COT_ROWS + PIECE :])
        return jnp.concatenate([top, rest], axis=1)[:, :D]

    return jnp.where(step == 0, piece(0)[:120], piece(1)[8:])


def qkv_grads(meta, step, mine, other):
    low = pick_core(meta, 0, mine[...], other[...])[:120]
    high = pick_core(meta, 1, mine[...], other[...])[8:128]
    return jnp.where(step == 0, low, high)


def adamw_body(grads_of, rate, meta, mine, other, master, first, second, *refs):
    grad_out, master_out, copy_out, first_out, second_out = refs[-5:]
    grad = grads_of(meta, pl.program_id(0), mine, other)
    grad_out[...] = grad
    new = adamw_step(grad, master[...], first[...], second[...], rate, DECAY_RATE)
    master_out[...], copy_out[...], first_out[...], second_out[...] = new


def adamw_call(meta, grads_of, pair, pair_spec, states, block, spec, steps, rate, name, deps):
    shape = states[0].shape
    own = pl.BlockSpec(block, spec)
    types = (F32, F32, BF, F32, F32)
    return pl.pallas_call(
        functools.partial(adamw_body, grads_of, rate),
        grid_spec=pltpu.PrefetchScalarGridSpec(
            num_scalar_prefetch=1,
            grid=(steps,),
            in_specs=[pair_spec] * 2 + [own] * 3 + [ANY] * len(deps),
            out_specs=[own] * 5,
        ),
        out_shape=[jax.ShapeDtypeStruct(shape, one) for one in types],
        compiler_params=params(),
        cost_estimate=cost(0, 34 * shape[0] * shape[1]),
        name=name,
    )(meta, *pair, *states, *deps)


def row_tables(doc_lengths, row, offset, tokens):
    ends = jnp.cumsum(doc_lengths, dtype=jnp.int32)
    starts = ends - doc_lengths
    blocks = (doc_lengths + BLOCK - 1) // BLOCK
    bases = jnp.cumsum(blocks, dtype=jnp.int32) - blocks
    places = jnp.arange(row, dtype=jnp.int32)
    inside = (places[:, None] >= starts[None, :]) & (places[:, None] < ends[None, :])

    def pick(values):
        return jnp.sum(jnp.where(inside, values[None, :], 0), axis=1, dtype=jnp.int32)

    doc_start, doc_end, base = pick(starts), pick(ends), pick(bases)
    position = places - doc_start
    segment = base + position // BLOCK
    reach = jnp.minimum(doc_end, doc_start + BLOCK * (position // BLOCK + 1))
    lane = jnp.arange(128, dtype=jnp.int32)
    aug = ((lane[None, :] == segment[:, None] + 64) | (lane[None, :] >= LANE_LOG)).astype(BF)

    def own(values):
        return lax.dynamic_slice_in_dim(values, offset, tokens)

    doc_start, reach, base, segment = own(doc_start), own(reach), own(base), own(segment)
    seen = (lane[None, :] >= base[:, None] + 64) & (lane[None, :] <= segment[:, None] + 64)
    open_lane = seen | (lane[None, :] >= LANE_LOG) | (lane[None, :] < 64)
    qmask = jnp.where(open_lane, 0.0, -1e30).astype(BF)
    chunks = tokens // QC
    low = jnp.min(doc_start.reshape(chunks, QC), axis=1) // KT
    high = (jnp.max(reach.reshape(chunks, QC), axis=1) + KT - 1) // KT
    ranges = jnp.stack([low, high], axis=1).reshape(-1).astype(jnp.int32)
    half = HEAD_DIM // 2
    frequency = ROPE_THETA ** (-2.0 * jnp.arange(half, dtype=F32) / HEAD_DIM)
    angles = own(position).astype(F32)[:, None] * frequency[None, :]
    cosine, sine = jnp.cos(angles), jnp.sin(angles)
    cosine = jnp.concatenate([cosine] * 4, axis=1)
    sine = jnp.concatenate([-sine, sine, -sine, sine], axis=1)
    return aug, qmask, ranges, cosine, sine


def local(
    shards,
    depth,
    tokens,
    cotangent,
    lengths,
    qkv_copy,
    qkv_master,
    qkv_first,
    qkv_second,
    proj_copy,
    proj_master,
    proj_first,
    proj_second,
    gateup_copy,
    gateup_master,
    gateup_first,
    gateup_second,
    down_copy,
    down_master,
    down_first,
    down_second,
    gain_copy,
    gain_master,
    gain_first,
    gain_second,
):
    fast = shards == 4 and depth == 4
    me = lax.axis_index("shard")
    z = lax.axis_index("deep")
    core = lax.axis_index("core")
    count = tokens.shape[0]

    def over_shard(value, flip):
        return lax.ppermute(value, "shard", [(s, s ^ flip) for s in range(shards)])

    def over_core(value):
        return lax.ppermute(value, "core", [(0, 1), (1, 0)])

    def over_deep(value, flip):
        return lax.ppermute(value, "deep", [(s, s ^ flip) for s in range(depth)])

    def all_shards(value):
        return lax.all_to_all(value, "shard", 0, 0, tiled=True)

    def over_deep_by(value, steps):
        return lax.ppermute(value, "deep", [(d, (d + steps) % depth) for d in range(depth)])

    def hop(value, flips):
        pairs = [
            (s * depth + d, (s ^ flips[d % 2]) * depth + d)
            for s in range(shards)
            for d in range(depth)
        ]
        return lax.ppermute(value, ("shard", "deep"), pairs)

    def first_hop(piece):
        return hop(piece, (1, 2))

    def second_hop(one):
        return over_deep(one, 1), hop(one, (2, 1))

    def swapped(pieces):
        return tuple(pieces) + tuple(over_core(piece) for piece in pieces)

    aug, qmask, ranges, cosine, sine = row_tables(
        lengths[0], count * shards, me * count, count
    )
    meta = jnp.concatenate([jnp.stack([me, core, z % 2, (z // 2) % 2]).astype(jnp.int32), ranges])

    tokens_t = tokens.T
    cot_t = cotangent.T
    down_t = down_copy.T
    if fast:
        pad = qkv_copy.shape[0] - PIECE
        extra = jnp.pad(gain_copy, ((0, PIECE_ROWS - PIECE - 2), (0, QKV - gain_copy.shape[1])))
        piece = jnp.concatenate(
            [lax.dynamic_slice_in_dim(qkv_copy, core * pad, PIECE), extra], axis=0
        )
        one = first_hop(piece)
        qkv_w = (qkv_copy,) + swapped((one,) + second_hop(one))
        gp_half, proj_wide = cut_call(meta, gateup_copy, proj_copy, piece)
        gp_one = first_hop(gp_half)
        gain = gain_copy
    else:
        qkv_w, proj_w, gateup_w = (
            (lax.all_gather(w, "shard", axis=0, tiled=True),)
            for w in (qkv_copy, proj_copy, gateup_copy)
        )
        proj_w = (jnp.pad(proj_w[0], ((0, 0), (0, 1024 - D))),)
        down_w = (lax.all_gather(down_t, "shard", axis=1, tiled=True),)
        gain = lax.all_gather(gain_copy, "shard", axis=1, tiled=True)

    x_rows, cot_rows, scaled = first_norm_call(tokens_t, cot_t, (cosine, sine, aug, qmask, meta))
    n1, gains, kva, kvb = kv_call(meta, scaled, gain, cosine, sine, qkv_w, shards)
    kva = all_shards(kva)
    q, qn, kvb = q_call(meta, n1, cosine, sine, kvb, qkv_w, shards)
    kvb = all_shards(kvb)
    deps = ()
    if fast:
        (gp_one,) = after((gp_one,), (q, kva))
        ((down_half,),) = stage("cut_down", meta, [rows_job(down_t, D // 2)], (gp_one,))
        deps = (down_half,)
        gp_two, gp_three = second_hop(gp_one)
        down_one = first_hop(down_half)
    oa, qa = attend_forward(meta, q, qmask, qn, aug, kva, 0, deps)
    if fast:
        (down_one,) = after((down_one,), (oa,))
        deps = (down_one,)
        down_two, down_three = second_hop(down_one)
    ob, qb = attend_forward(meta, q, qmask, qn, aug, kvb, FIRST, deps)
    if fast:
        gp_w = swapped(after((gp_one, gp_two, gp_three), (ob,)))
        gateup_w = (gateup_copy,) + gp_w
        proj_w = (proj_wide,) + gp_w
    residual, n2, mixed, early_own, early_send = residual_call(
        meta, x_rows, oa, ob, gains, n1, cot_t, proj_w
    )
    if fast:
        down_w = (down_t,) + swapped(after((down_one, down_two, down_three), (residual,)))
    output_t, dn, act, late_own, late_send = mlp_call(
        meta, residual, n2, cot_rows, gateup_w, down_w
    )
    grad_residual, grad_branch, do, gain_two = norm_back_call(
        meta, residual, dn, cot_rows, mixed, gains, proj_w
    )

    deps = ()
    if fast:
        early_oth = over_core(early_send)
        late_oth = over_core(late_send)
        act_oth = over_core(act)
        branch_oth = over_core(grad_branch)
        gp_g = gateup_grad_call(
            meta, early_own, early_oth, late_own, late_oth, (grad_branch,)
        )
        gp_parts = all_shards(gp_g)
        deps = (gp_g, act_oth, branch_oth)
    dq, dkv = attend_backward(meta, qa, qb, do, aug, kva, kvb, deps)
    deps = ()
    if fast:
        (gp_parts,) = after((gp_parts,), (dq,))
    dkv = all_shards(dkv)
    if fast:
        (gp,) = stage("gateup_over_shard", meta, [split_job([gp_parts], 1, 2, 4)], ())
        gp_recv = over_deep(gp[1], 1)
        dp_g = down_proj_grad_call(
            meta, early_own, early_oth, act, act_oth, grad_branch, branch_oth, (gp[0],)
        )
        (gp,) = stage(
            "gateup_over_near", meta, [split_job([gp[0], gp_recv], 1, 3)], (dp_g,)
        )
        gp_recv = over_deep(gp[1], 2)
        deps = (gp[0],)
    grad_joined, input_grad_t = joined_call(
        meta,
        dq,
        cosine,
        sine,
        x_rows,
        gains,
        grad_residual,
        gain_two,
        dkv,
        qkv_w,
        deps,
    )
    rates = (D ** (-0.5), max(HEAD_DIM // 16, 1) ** (-0.5), D ** (-0.5), FF ** (-0.5))
    qkv_states = (qkv_master, qkv_first, qkv_second)
    proj_states = (proj_master, proj_first, proj_second)
    gateup_states = (gateup_master, gateup_first, gateup_second)
    down_states = (down_master.T, down_first.T, down_second.T)
    if fast:
        joined_oth = over_core(grad_joined)
        (dp_g,) = after((dp_g,), (grad_joined,))
        dp_parts = all_shards(dp_g)
        ((gp,),) = stage(
            "gateup_over_far", meta, [add_job([gp[0], gp_recv])], (grad_joined,)
        )
        gp_recv = over_deep(gp, 2)
        qkv_g = qkv_grad_call(meta, early_own, early_oth, grad_joined, joined_oth, (gp,))
        qkv_parts = [qkv_g[0]] + [over_shard(qkv_g[j], j) for j in range(1, 4)]
        ((gp,),) = stage("gateup_join_far", meta, [join_job(gp, gp_recv, 1, 3)], (qkv_g[0],))
        gp_recv = over_deep(gp, 1)
        ((dp,),) = stage("down_over_shard", meta, [add_job([dp_parts], 4)], (gp,))
        dp_parts = lax.all_to_all(dp, "deep", 0, 0, tiled=True)
        ((gp,),) = stage("gateup_join_near", meta, [join_job(gp, gp_recv, 1, 2)], (dp,))
        gp_pair = (gp, over_core(gp))
        (qkv,) = stage("qkv_over_shard", meta, [split_job(qkv_parts, 0, 2)], (gp,))
        qkv_recv = over_deep(qkv[1], 1)
        ((dp,),) = stage("down_over_deep", meta, [add_job([dp_parts], 4)], (qkv[0],))
        dp_parts = [dp] + [over_deep_by(dp, k) for k in range(1, 4)]
        (qkv,) = stage("qkv_over_near", meta, [split_job([qkv[0], qkv_recv], 0, 3)], (dp,))
        qkv_recv = over_deep(qkv[1], 2)
        rows = gateup_copy.shape[0]
        gateup_new = adamw_call(
            meta,
            gateup_grads,
            gp_pair,
            pl.BlockSpec((rows, 640), lambda i, m: (0, i % 4)),
            gateup_states,
            (rows, 640),
            lambda i, m: (0, i),
            8,
            rates[2],
            "gateup_step",
            (qkv[0],),
        )
        ((qkv,),) = stage(
            "qkv_over_far", meta, [add_job([qkv[0], qkv_recv])], (gateup_new[0],)
        )
        qkv_recv = over_deep(qkv, 2)
        ((dp,),) = stage("down_join", meta, [whole_job(dp_parts)], (qkv,))
        dp_pair = (dp, over_core(dp))
        ((qkv,),) = stage("qkv_join_far", meta, [join_job(qkv, qkv_recv, 0, 3)], (dp,))
        qkv_recv = over_deep(qkv, 1)
        down_new = adamw_call(
            meta,
            down_grads,
            dp_pair,
            pl.BlockSpec((D // 4, FF // 4), lambda i, m: (i % 2, 0)),
            down_states,
            (D // 4, FF // 4),
            lambda i, m: (i, 0),
            4,
            rates[3],
            "down_step",
            (qkv,),
        )
        proj_new = adamw_call(
            meta,
            proj_grads,
            dp_pair,
            pl.BlockSpec((DP_ROWS, FF // 4), lambda i, m: (0, 0)),
            proj_states,
            (rows // 2, D),
            lambda i, m: (i, 0),
            2,
            rates[1],
            "proj_step",
            (down_new[0],),
        )
        ((qkv,),) = stage("qkv_join_near", meta, [join_job(qkv, qkv_recv, 0, 2)], (down_new[0],))
        qkv_pair = (qkv, over_core(qkv))
        qkv_new = adamw_call(
            meta,
            qkv_grads,
            qkv_pair,
            pl.BlockSpec((PIECE_ROWS, QKV), lambda i, m: (0, 0)),
            qkv_states,
            (rows // 2, QKV),
            lambda i, m: (i, 0),
            2,
            rates[0],
            "qkv_step",
            (proj_new[0],),
        )
        gain_grad = qkv[PIECE : PIECE + 2, : D // shards].astype(F32)
    else:

        def owned(left, right):
            whole = jnp.einsum("ta,tb->ab", left, right, preferred_element_type=F32)
            mine = lax.psum_scatter(whole, "shard", scatter_dimension=0, tiled=True)
            return lax.psum(mine, ("deep", "core"))

        def updated(grad, states, rate):
            return (grad,) + adamw_step(grad, *states, rate, DECAY_RATE)

        grad_gate = jnp.where(core == 0, late_own, late_send)
        grad_up = jnp.where(core == 0, late_send, late_own)
        down_grad_t = owned(act.transpose(1, 0, 2).reshape(count, FF), cotangent).T
        gateup_grad = owned(n2, jnp.concatenate([grad_gate, grad_up], axis=1))
        proj_grad = owned(mixed, grad_branch[:, :D])
        qkv_grad = owned(n1, grad_joined[:count, :QKV])
        gain_sum = lax.psum(
            grad_joined[count : count + 2, :D].astype(F32), ("shard", "deep", "core")
        )
        width = D // shards
        gain_grad = lax.dynamic_slice_in_dim(gain_sum, me * width, width, axis=1)
        qkv_new = updated(qkv_grad, qkv_states, rates[0])
        proj_new = updated(proj_grad, proj_states, rates[1])
        gateup_new = updated(gateup_grad, gateup_states, rates[2])
        down_new = updated(down_grad_t, down_states, rates[3])

    gain_new = adamw_step(gain_grad, gain_master, gain_first, gain_second, 0.5, 0.0)
    return (
        (output_t.T, input_grad_t.T)
        + tuple(qkv_new)
        + tuple(proj_new)
        + tuple(gateup_new)
        + tuple(one.T for one in down_new)
        + (gain_grad,)
        + gain_new
    )


def solution(mesh):
    shards, rep = mesh.shape["shard"], mesh.shape["rep"]
    depth = rep // 2
    fine = Mesh(mesh.devices.reshape(shards, depth, 2), ("shard", "deep", "core"))
    by_token = P(("deep", "core", "shard"), None)
    by_row = P("shard", None)
    by_column = P(None, "shard")
    return jax.shard_map(
        functools.partial(local, shards, depth),
        mesh=fine,
        in_specs=(by_token, by_token, P(("deep", "core"), None)) + (by_row,) * 16 + (by_column,) * 4,
        out_specs=(by_token,) * 2 + (by_row,) * 20 + (by_column,) * 5,
        check_vma=False,
    )
```

```python
import functools

import jax
import jax.numpy as jnp
from jax import lax
from jax.experimental import pallas as pl
from jax.experimental.pallas import tpu as pltpu
from jax.sharding import Mesh, PartitionSpec as P

D = 960
FF = 2560
HEADS = 15
KV_HEADS = 5
GROUP = 3
HEAD_DIM = 64
BLOCK = 256
STEP = 10
QKV = 1600

NORM_EPSILON = 1e-05
ROPE_THETA = 100000.0
BETA_FIRST = 0.5
BETA_SECOND = 0.6
ADAM_EPSILON = 1e-08
DECAY_RATE = 0.1

LOG2E = 1.4426950408889634
LN2 = 0.6931471805599453
QC = 256
KT = 256
NORM_ROWS = 16
SAFE = 60.0
LANE_LOG = 125
LANE_INNER = 61

F32 = jnp.float32
BF = jnp.bfloat16
NT = (((1,), (1,)), ((), ()))
TN = (((0,), (0,)), ((), ()))
VMEM_BYTES = 58 << 20
ANY = pl.BlockSpec(memory_space=pl.ANY)
WHOLE = pl.BlockSpec(memory_space=pltpu.VMEM)
SCALARS = pl.BlockSpec(memory_space=pltpu.SMEM)


def params():
    return pltpu.CompilerParams(vmem_limit_bytes=VMEM_BYTES)


def cost(flops, moved):
    del flops, moved
    return pl.CostEstimate(flops=1, bytes_accessed=1, transcendentals=0)


def after_body(*refs):
    del refs


def after(values, deps):
    values, deps = tuple(values), tuple(deps)
    return pl.pallas_call(
        after_body,
        in_specs=[ANY] * (len(values) + len(deps)),
        out_specs=[ANY] * len(values),
        out_shape=[jax.ShapeDtypeStruct(one.shape, one.dtype) for one in values],
        input_output_aliases={i: i for i in range(len(values))},
        compiler_params=params(),
        cost_estimate=cost(1, 1),
        name="after",
    )(*values, *deps)


def transposed(value):
    rows = value.shape[0]
    pad = -rows % 128
    if pad:
        value = jnp.concatenate([value, jnp.zeros((pad, value.shape[1]), value.dtype)], axis=0)
    return jnp.transpose(value)[:, :rows]


def transposed_back(value):
    columns = value.shape[1]
    pad = -columns % 128
    if pad:
        value = jnp.concatenate([value, jnp.zeros((value.shape[0], pad), value.dtype)], axis=1)
    return jnp.transpose(value)[:columns, :]


def lanes():
    return lax.broadcasted_iota(jnp.int32, (1, 128), 1)


def split3(value):
    high = value.astype(BF)
    rest = value - high.astype(F32)
    mid = rest.astype(BF)
    return high, mid, (rest - mid.astype(F32)).astype(BF)


def start_all(copies):
    for one in copies:
        one.start()


def wait_all(copies):
    for one in copies:
        one.wait()


PIECE = 128
PIECE_ROWS = 144
GP_ROWS = 304


def qkv_plan(refs, target, meta, sems):
    if len(refs) == 1:
        return [pltpu.make_async_copy(refs[0], target, sems.at[0])], [], []
    rows = refs[0].shape[0]
    me, zpar = meta[0], meta[2]
    first = rows - PIECE
    own = target.at[pl.ds(pl.multiple_of(me * rows, 16), rows), :]
    common = [pltpu.make_async_copy(refs[0], own, sems.at[0])]
    by_core = ([], [])
    for k, rel in enumerate((1 + zpar, 2 - zpar, 3)):
        base = (me ^ rel) * rows
        low = target.at[pl.ds(pl.multiple_of(base, 16), first), :]
        high = target.at[pl.ds(pl.multiple_of(base + first, 16), PIECE), :]
        mine, other = refs[1 + k], refs[4 + k]
        for c in range(2):
            low_src, high_src = (mine, other) if c == 0 else (other, mine)
            by_core[c].append(
                pltpu.make_async_copy(low_src.at[pl.ds(0, first), :], low, sems.at[1 + k])
            )
            by_core[c].append(
                pltpu.make_async_copy(high_src.at[pl.ds(0, PIECE), :], high, sems.at[4 + k])
            )
    return common, by_core[0], by_core[1]


def proj_plan_of(refs, target, meta, sems):
    if len(refs) == 1:
        return [pltpu.make_async_copy(refs[0], target, sems.at[0])], [], []
    rows = refs[0].shape[0]
    me, zpar = meta[0], meta[2]
    first = rows - PIECE
    own = target.at[pl.ds(pl.multiple_of(me * rows, 16), rows), :]
    common = [pltpu.make_async_copy(refs[0], own, sems.at[0])]
    by_core = ([], [])
    top = GP_ROWS - 64
    for k, rel in enumerate((1 + zpar, 2 - zpar, 3)):
        base = (me ^ rel) * rows
        mine, other = refs[1 + k], refs[4 + k]
        for c in range(2):
            low_src, high_src = (mine, other) if c == 0 else (other, mine)
            jobs = (
                (low_src, 0, 64, 0),
                (low_src, 1, first - 64, 64),
                (high_src, 0, 64, first),
                (high_src, 1, 64, first + 64),
            )
            for n, (src, side, count, at) in enumerate(jobs):
                by_core[c].append(
                    pltpu.make_async_copy(
                        src.at[pl.ds(top, count), pl.ds(side * 1024, 1024)],
                        target.at[pl.ds(pl.multiple_of(base + at, 16), count), :],
                        sems.at[1 + 4 * k + n],
                    )
                )
    return common, by_core[0], by_core[1]


def plan_start(plan, meta):
    common, zero, one = plan
    start_all(common)
    if zero:
        pl.when(meta[1] == 0)(lambda: start_all(zero))
        pl.when(meta[1] == 1)(lambda: start_all(one))


def plan_wait(plan, meta):
    common, zero, one = plan
    wait_all(common)
    if zero:
        pl.when(meta[1] == 0)(lambda: wait_all(zero))
        pl.when(meta[1] == 1)(lambda: wait_all(one))


def gateup_copies(refs, target, meta, sems, tile):
    me, core, zpar = meta[0], meta[1], meta[2]
    rows = refs[0].shape[0]
    out = []
    for f in range(FF // tile):
        cols = pl.ds(f * tile, tile)
        own_rows = pl.ds(pl.multiple_of(me * rows, 16), rows)
        if len(refs) == 1:
            own_rows = pl.ds(0, rows)
        copies = [
            pltpu.make_async_copy(
                refs[0].at[:, pl.ds(i * FF + f * tile, tile)],
                target.at[i, own_rows, cols],
                sems.at[f, i],
            )
            for i in range(2)
        ]
        if len(refs) > 1:
            for k, rel in enumerate((1 + zpar, 2 - zpar, 3)):
                at = pl.ds(pl.multiple_of((me ^ rel) * rows, 16), rows)
                for n, (half, ref) in enumerate(((core, refs[1 + k]), (1 - core, refs[4 + k]))):
                    copies.append(
                        pltpu.make_async_copy(
                            ref.at[pl.ds(0, rows), cols],
                            target.at[half, at, cols],
                            sems.at[f, 2 + 2 * k + n],
                        )
                    )
        out.append(copies)
    return out


def down_copies(refs, target, meta, sems):
    if len(refs) == 1:
        return [pltpu.make_async_copy(refs[0], target, sems.at[0])]
    me, core, zpar = meta[0], meta[1], meta[2]
    width = refs[0].shape[1]
    rows = refs[1].shape[0]

    def columns(rel):
        return pl.ds(pl.multiple_of((me ^ rel) * width, 128), width)

    out = [pltpu.make_async_copy(refs[0], target.at[:, columns(0)], sems.at[6])]
    for k, rel in enumerate((1 + zpar, 2 - zpar, 3)):
        for which, ref in ((core, refs[1 + k]), (1 - core, refs[4 + k])):
            at = pl.ds(pl.multiple_of(which * rows, 16), rows)
            out.append(
                pltpu.make_async_copy(ref, target.at[at, columns(rel)], sems.at[len(out) - 1])
            )
    return out


def cut_body(meta, gateup_ref, proj_ref, dep_ref, gp_out, proj_out):
    rows = gateup_ref.shape[0]
    gp_out[:rows] = gateup_ref[...]
    gp_out[rows:] = jnp.zeros((GP_ROWS - rows, FF), BF)
    half = proj_ref[pl.ds(pl.multiple_of(meta[1] * (rows - PIECE), 16), PIECE), :]
    gp_out[rows:, :D] = half[:64]
    gp_out[rows:, 1024 : 1024 + D] = half[64:]
    proj_out[:, 896:] = jnp.zeros((rows, 128), BF)
    proj_out[:, :D] = proj_ref[...]


def cut_call(meta, gateup, proj, dep):
    rows = gateup.shape[0]
    return pl.pallas_call(
        cut_body,
        grid_spec=pltpu.PrefetchScalarGridSpec(
            num_scalar_prefetch=1,
            grid=(1,),
            in_specs=[
                pl.BlockSpec((rows, FF), lambda i, m: (0, m[1])),
                pl.BlockSpec(proj.shape, lambda i, m: (0, 0)),
                ANY,
            ],
            out_specs=[
                pl.BlockSpec((GP_ROWS, FF), lambda i, m: (0, 0)),
                pl.BlockSpec((rows, 1024), lambda i, m: (0, 0)),
            ],
        ),
        out_shape=[
            jax.ShapeDtypeStruct((GP_ROWS, FF), BF),
            jax.ShapeDtypeStruct((rows, 1024), BF),
        ],
        compiler_params=params(),
        cost_estimate=cost(0, 8 << 20),
        name="cut_weights",
    )(meta, gateup, proj, dep)


def rope_tile(tile, cosine, sine):
    low = (lanes() % 64) < 32
    swapped = jnp.where(low, pltpu.roll(tile, 96, 1), pltpu.roll(tile, 32, 1))
    return tile * cosine + swapped * sine


def first_norm_body(x_ref, cot_ref, *refs):
    x_out, cot_out, scaled_ref = refs[-3:]
    x = transposed(x_ref[...])
    x_out[...] = x
    cot_out[...] = transposed(cot_ref[...])
    x = x.astype(F32)
    scale = lax.rsqrt(jnp.mean(x * x, axis=1, keepdims=True) + NORM_EPSILON)
    scaled_ref[...] = x * scale


def first_norm_call(x, cot, deps):
    tokens = x.shape[1]
    return pl.pallas_call(
        first_norm_body,
        in_specs=[WHOLE] * 2 + [ANY] * len(deps),
        out_specs=[WHOLE] * 3,
        out_shape=[jax.ShapeDtypeStruct((tokens, D), BF)] * 2
        + [jax.ShapeDtypeStruct((tokens, D), F32)],
        compiler_params=params(),
        cost_estimate=cost(0, 5 << 20),
        name="first_norm",
    )(x, cot, *deps)


def kv_body(nw, meta, scaled_ref, gain_ref, cos_ref, sin_ref, *refs):
    w_refs = refs[:nw]
    n_ref, gains_out, kv_ref, w_scr, j_scr, g_scr, sems, gsems = refs[nw:]
    plan = qkv_plan(w_refs, w_scr, meta, sems)
    if nw > 1:
        gain_copies = [
            pltpu.make_async_copy(
                w_refs[1 + k].at[pl.ds(PIECE, 16), pl.ds(0, 256)], g_scr.at[k], gsems.at[k]
            )
            for k in range(3)
        ]
        start_all(gain_copies)
        plan_start(plan, meta)
        wait_all(gain_copies)
        me, zpar = meta[0], meta[2]
        own = gain_ref[...].astype(F32)
        width = own.shape[1]
        for b in range(D // width):
            value = own
            for k, rel in enumerate((1 + zpar, 2 - zpar, 3)):
                value = jnp.where((me ^ rel) == b, g_scr[k][:2, :width].astype(F32), value)
            gains_out[:2, b * width : (b + 1) * width] = value
    else:
        plan_start(plan, meta)
        gains_out[:2] = gain_ref[...].astype(F32)
    gains_out[2:] = jnp.zeros((6, D), F32)
    n_ref[...] = (scaled_ref[...] * gains_out[0:1, :]).astype(BF)
    plan_wait(plan, meta)
    tokens = n_ref.shape[0]
    j_scr[...] = jnp.dot(n_ref[...], w_scr[:, 896:QKV], preferred_element_type=F32)
    lane = lanes()
    cosine = cos_ref[...]
    sine = sin_ref[...]
    keys = {}
    for t in range(7, 10):
        at = 128 * (t - 7)
        tile = rope_tile(j_scr[:, at : at + 128], cosine, sine)
        for half in range(2):
            if 2 * t + half >= HEADS:
                keys[2 * t + half - HEADS] = tile if half == 0 else pltpu.roll(tile, 64, 1)
    for g in range(KV_HEADS):
        t = 10 + g // 2
        if t == 12:
            last = j_scr[:, 640:704]
            value = jnp.concatenate([last, last], axis=1)
        else:
            value = j_scr[:, 128 * (t - 7) : 128 * (t - 6)]
            if g % 2 == 0:
                value = pltpu.roll(value, 64, 1)
        both = jnp.where(lane < 64, keys[g], value).astype(BF)
        kv_ref[:tokens, 128 * g : 128 * (g + 1)] = both
        key = jnp.where(lane < 64, both.astype(F32), 0.0)
        top = jnp.max(jnp.sum(key * key, axis=1, keepdims=True), axis=0, keepdims=True)
        kv_ref[tokens:, 128 * g : 128 * (g + 1)] = jnp.broadcast_to(
            top * 1.02, (NORM_ROWS, 128)
        ).astype(BF)


def kv_call(meta, scaled, gain, cosine, sine, weights):
    tokens = scaled.shape[0]
    nw = len(weights)
    return pl.pallas_call(
        functools.partial(kv_body, nw),
        in_specs=[SCALARS] + [WHOLE] * 4 + [ANY] * nw,
        out_specs=[WHOLE] * 3,
        out_shape=[
            jax.ShapeDtypeStruct((tokens, D), BF),
            jax.ShapeDtypeStruct((8, D), F32),
            jax.ShapeDtypeStruct((tokens + NORM_ROWS, KV_HEADS * 128), BF),
        ],
        scratch_shapes=[
            pltpu.VMEM((D, QKV), BF),
            pltpu.VMEM((tokens, QKV - 896), F32),
            pltpu.VMEM((3, 16, 256), BF),
            pltpu.SemaphoreType.DMA((8,)),
            pltpu.SemaphoreType.DMA((3,)),
        ],
        compiler_params=params(),
        cost_estimate=cost(2 * tokens * D * 704, 6 << 20),
        name="kv_project",
    )(meta, scaled, gain, cosine, sine, *weights)


def q_body(nw, meta, n_ref, cos_ref, sin_ref, *refs):
    w_refs = refs[:nw]
    q_ref, qn_ref, w_scr, j_scr, sems = refs[nw:]
    plan = qkv_plan(w_refs, w_scr, meta, sems)
    plan_start(plan, meta)
    plan_wait(plan, meta)
    tokens = n_ref.shape[0]
    j_scr[...] = jnp.dot(n_ref[...], w_scr[:, :1024], preferred_element_type=F32)
    lane = lanes()
    cosine = cos_ref[...]
    sine = sin_ref[...]
    top_q = jnp.zeros((tokens, 1), F32)
    for t in range(8):
        tile = rope_tile(j_scr[:, 128 * t : 128 * (t + 1)], cosine, sine)
        for half in range(2):
            head = 2 * t + half
            if head >= HEADS:
                continue
            part = tile if half == 0 else pltpu.roll(tile, 64, 1)
            part = jnp.where(lane < 64, part * (LOG2E * 0.125), 0.0).astype(BF)
            q_ref[head] = part
            part = part.astype(F32)
            top_q = jnp.maximum(top_q, jnp.sum(part * part, axis=1, keepdims=True))
    qn_ref[...] = jnp.broadcast_to(jnp.max(top_q, axis=0, keepdims=True) * 1.02, (8, 128))


def q_call(meta, n1, cosine, sine, weights):
    tokens = n1.shape[0]
    nw = len(weights)
    return pl.pallas_call(
        functools.partial(q_body, nw),
        in_specs=[SCALARS] + [WHOLE] * 3 + [ANY] * nw,
        out_specs=[WHOLE] * 2,
        out_shape=[
            jax.ShapeDtypeStruct((HEADS, tokens, 128), BF),
            jax.ShapeDtypeStruct((8, 128), F32),
        ],
        scratch_shapes=[
            pltpu.VMEM((D, QKV), BF),
            pltpu.VMEM((tokens, 1024), F32),
            pltpu.SemaphoreType.DMA((8,)),
        ],
        compiler_params=params(),
        cost_estimate=cost(2 * tokens * D * 1024, 8 << 20),
        name="q_project",
    )(meta, n1, cosine, sine, *weights)


def load_rows(shards, tokens, me, pieces, kv_scr, sem, nrm_scr=None, nsem=None):
    copies = []
    for j in range(shards):
        row = pl.multiple_of((me ^ j) * tokens, tokens)
        for h in range(KV_HEADS):
            copies.append(
                pltpu.make_async_copy(
                    pieces[j].at[pl.ds(0, tokens), pl.ds(h * 128, 128)],
                    kv_scr.at[h, pl.ds(row, tokens), :],
                    sem.at[j, h],
                )
            )
        if nrm_scr is not None:
            copies.append(
                pltpu.make_async_copy(
                    pieces[j].at[pl.ds(tokens, NORM_ROWS), :], nrm_scr.at[j], nsem.at[j]
                )
            )
    start_all(copies)
    wait_all(copies)


def pair_range(meta, c):
    t_lo = meta[4 + 2 * c]
    t_hi = meta[5 + 2 * c]
    odd = (t_hi - t_lo) & 1
    start = jnp.where((odd == 1) & (t_lo > 0), t_lo - 1, t_lo)
    return start, (t_hi - t_lo + odd) // 2


def attend_forward_body(shards, tokens, meta, q_ref, qm_ref, qn_ref, aug_ref, *refs):
    o_ref, q2_ref, kv_scr, acc_scr, m_scr, nrm_scr, sem, nsem = refs[-8:]
    g = pl.program_id(0)
    c = pl.program_id(1)

    @pl.when((g == 0) & (c == 0))
    def _():
        load_rows(shards, tokens, meta[0], refs[:shards], kv_scr, sem, nrm_scr, nsem)

    lane = lanes()
    qm = qm_ref[...]
    rows_all = GROUP * QC
    acc_scr[...] = jnp.zeros_like(acc_scr)
    q2_ref[...] = jnp.where(lane < 64, q_ref[...], qm[None])
    safe = jnp.max(qn_ref[...]) * jnp.max(nrm_scr[...].astype(F32)) < SAFE * SAFE
    start, pairs = pair_range(meta, c)

    def tiles(u):
        rows = pl.ds(pl.multiple_of((start + 2 * u) * KT, KT), 2 * KT)
        kv = kv_scr[g, rows, :]
        return (
            jnp.where(lane < 64, kv, aug_ref[rows, :]),
            jnp.where(lane < 64, jnp.ones_like(kv), kv),
        )

    @pl.when(safe)
    def _():
        def step(u, carry):
            keys, values = tiles(u)
            scores = lax.dot_general(
                q2_ref[...].reshape(rows_all, 128), keys, NT, preferred_element_type=F32
            )
            weights = jnp.exp2(scores).astype(BF)
            acc_scr[...] += jnp.dot(weights, values, preferred_element_type=F32)
            return carry

        lax.fori_loop(0, pairs, step, 0)
        m_scr[...] = jnp.zeros_like(m_scr)

    @pl.when(jnp.logical_not(safe))
    def _():
        m_scr[...] = jnp.full_like(m_scr, -1e30)

        def step(u, carry):
            keys, values = tiles(u)

            def head(h, carry):
                scores = lax.dot_general(q2_ref[h], keys, NT, preferred_element_type=F32)
                rows = pl.ds(pl.multiple_of(h * QC, QC), QC)
                old = m_scr[rows, :1]
                new = jnp.maximum(old, jnp.max(scores, axis=1, keepdims=True))
                weights = jnp.exp2(scores - new).astype(BF)
                acc_scr[rows, :] = acc_scr[rows, :] * jnp.exp2(old - new) + jnp.dot(
                    weights, values, preferred_element_type=F32
                )
                m_scr[rows, :] = jnp.broadcast_to(new, (QC, 128))
                return carry

            return lax.fori_loop(0, GROUP, head, carry)

        lax.fori_loop(0, pairs, step, 0)

    def finish(h, carry):
        rows = pl.ds(pl.multiple_of(h * QC, QC), QC)
        acc = acc_scr[rows, :]
        other = pltpu.roll(acc, 64, 1)
        o_ref[h] = jnp.where(lane < 64, 0.0, acc / jnp.where(lane < 64, 1.0, other)).astype(BF)
        total = jnp.where(lane < 64, acc, other)
        high, mid, low = split3(-(m_scr[rows, :] + jnp.log2(total)))
        with_log = jnp.where(lane == LANE_LOG + 2, low, q2_ref[h])
        with_log = jnp.where(lane == LANE_LOG + 1, mid, with_log)
        q2_ref[h] = jnp.where(lane == LANE_LOG, high, with_log)
        return carry

    lax.fori_loop(0, GROUP, finish, 0)


def attend_forward(meta, q, qm, qn, aug, kv, deps):
    tokens = q.shape[1]
    shards = len(kv)
    heads = KV_HEADS
    row = shards * tokens
    block = pl.BlockSpec((GROUP, QC, 128), lambda g, c, m: (g, c, 0))
    return pl.pallas_call(
        functools.partial(attend_forward_body, shards, tokens),
        grid_spec=pltpu.PrefetchScalarGridSpec(
            num_scalar_prefetch=1,
            grid=(heads, tokens // QC),
            in_specs=[
                pl.BlockSpec((GROUP, QC, 128), lambda g, c, m: (g, c, 0)),
                pl.BlockSpec((QC, 128), lambda g, c, m: (c, 0)),
                pl.BlockSpec((8, 128), lambda g, c, m: (0, 0)),
                pl.BlockSpec((row, 128), lambda g, c, m: (0, 0)),
            ]
            + [ANY] * (shards + len(deps)),
            out_specs=[block, block],
            scratch_shapes=[
                pltpu.VMEM((heads, row, 128), BF),
                pltpu.VMEM((GROUP * QC, 128), F32),
                pltpu.VMEM((GROUP * QC, 128), F32),
                pltpu.VMEM((shards, NORM_ROWS, heads * 128), BF),
                pltpu.SemaphoreType.DMA((shards, heads)),
                pltpu.SemaphoreType.DMA((shards,)),
            ],
        ),
        out_shape=[jax.ShapeDtypeStruct((GROUP * heads, tokens, 128), BF)] * 2,
        compiler_params=params(),
        cost_estimate=cost(16 * GROUP * heads * tokens * row * 128, 10 << 20),
        name="attend_forward",
    )(meta, q, qm, qn, aug, *kv, *deps)


def attend_backward_body(shards, tokens, meta, q_ref, do_ref, aug_ref, *refs):
    dq_ref, out_ref, kv_scr, dkv_scr, ob_scr, dq_scr, qt_scr, sem, osem = refs[-9:]
    g = pl.program_id(0)
    c = pl.program_id(1)

    @pl.when((g == 0) & (c == 0))
    def _():
        load_rows(shards, tokens, meta[0], refs[:shards], kv_scr, sem)

    @pl.when(c == 0)
    def _():
        dkv_scr[...] = jnp.zeros_like(dkv_scr)

    lane = lanes()
    rows_all = GROUP * QC
    dq_scr[...] = jnp.zeros_like(dq_scr)
    qt_scr[...] = jnp.transpose(
        jnp.where(lane < 64, q_ref[...], do_ref[...]).reshape(rows_all, 128)
    )
    start, pairs = pair_range(meta, c)

    def step(u, carry):
        tile = start + 2 * u
        rows = pl.ds(pl.multiple_of(tile * KT, KT), 2 * KT)
        kv = kv_scr[g, rows, :]
        ones = jnp.where(lane >= LANE_INNER, jnp.ones_like(kv), jnp.zeros_like(kv))
        keys = jnp.where(lane < 64, kv, aug_ref[rows, :])
        values = jnp.where(lane < 64, ones, kv)
        queries = q_ref[...].reshape(rows_all, 128)
        grads = do_ref[...].reshape(rows_all, 128)
        weights = jnp.exp2(lax.dot_general(queries, keys, NT, preferred_element_type=F32))
        inner = lax.dot_general(grads, values, NT, preferred_element_type=F32)
        grad_scores = (weights * inner).astype(BF)
        weights = weights.astype(BF)
        dq_scr[...] += jnp.dot(grad_scores, keys, preferred_element_type=F32)
        for i in range(2):
            part = slice(i * KT, (i + 1) * KT)
            dkv_scr[tile + i, :64] += jnp.dot(
                qt_scr[:64], grad_scores[:, part], preferred_element_type=F32
            )
            dkv_scr[tile + i, 64:] += jnp.dot(
                qt_scr[64:], weights[:, part], preferred_element_type=F32
            )
        return carry

    lax.fori_loop(0, pairs, step, 0)
    dq_ref[...] = dq_scr[...].reshape(GROUP, QC, 128) * 0.125

    def out_copy(group):
        at = pl.ds(pl.multiple_of(group * 128, 128), 128)
        return pltpu.make_async_copy(ob_scr, out_ref.at[:, at], osem)

    @pl.when(c == pl.num_programs(1) - 1)
    def _():
        pl.when(g > 0)(lambda: out_copy(g - 1).wait())
        for t in range(shards * tokens // KT):
            both = dkv_scr[t]
            both = jnp.concatenate([both[:64] * LN2, both[64:]], axis=0)
            ob_scr[t * KT : (t + 1) * KT, :] = jnp.transpose(both).astype(BF)
        out_copy(g).start()
        pl.when(g == KV_HEADS - 1)(lambda: out_copy(g).wait())


def attend_backward(meta, q2, do, aug, kv, deps):
    tokens = q2.shape[1]
    shards = len(kv)
    row = shards * tokens
    rows_all = GROUP * QC
    block = pl.BlockSpec((GROUP, QC, 128), lambda g, c, m: (g, c, 0))
    return pl.pallas_call(
        functools.partial(attend_backward_body, shards, tokens),
        grid_spec=pltpu.PrefetchScalarGridSpec(
            num_scalar_prefetch=1,
            grid=(KV_HEADS, tokens // QC),
            in_specs=[
                block,
                block,
                pl.BlockSpec((row, 128), lambda g, c, m: (0, 0)),
            ]
            + [ANY] * (shards + len(deps)),
            out_specs=[block, ANY],
            scratch_shapes=[
                pltpu.VMEM((KV_HEADS, row, 128), BF),
                pltpu.VMEM((row // KT, 128, KT), F32),
                pltpu.VMEM((row, 128), BF),
                pltpu.VMEM((rows_all, 128), F32),
                pltpu.VMEM((128, rows_all), BF),
                pltpu.SemaphoreType.DMA((shards, KV_HEADS)),
                pltpu.SemaphoreType.DMA(()),
            ],
        ),
        out_shape=[
            jax.ShapeDtypeStruct((HEADS, tokens, 128), F32),
            jax.ShapeDtypeStruct((row, KV_HEADS * 128), BF),
        ],
        compiler_params=params(),
        cost_estimate=cost(1, 1),
        name="attend_backward",
    )(meta, q2, do, aug, *kv, *deps)


MLP_TILE = 640


COT_ROWS = D // 2


def mix_body(meta, o_ref, n1_ref, cot_ref, mix_ref, own_ref, send_ref):
    lane = lanes()
    core = meta[1]
    for t in range(8):
        low = pltpu.roll(o_ref[2 * t].astype(F32), 64, 1)
        if t < 7:
            tile = jnp.where(lane < 64, low, o_ref[2 * t + 1].astype(F32)).astype(BF)
            mix_ref[:, 128 * t : 128 * (t + 1)] = tile
        else:
            mix_ref[:, 896:960] = low[:, :64].astype(BF)
    for n in range(2):
        rows = slice(n * COT_ROWS, (n + 1) * COT_ROWS)
        at = slice(n * 256, (n + 1) * 256)
        low, high = cot_ref[:COT_ROWS, at], cot_ref[COT_ROWS:, at]
        own_ref[rows] = jnp.where(core == 0, low, high)
        send_ref[rows] = jnp.where(core == 0, high, low)
    tokens = mix_ref.shape[0]
    width = D // 4
    for b in range(4):
        rows = block_rows(b, tokens)
        for at, ref in ((0, mix_ref), (128, n1_ref)):
            low = ref[:, b * width : b * width + PIECE]
            high = ref[:, (b + 1) * width - PIECE : (b + 1) * width]
            own_ref[rows, at : at + 128] = jnp.where(core == 0, low, high)
            send_ref[rows, at : at + 128] = jnp.where(core == 0, high, low)


def mix_call(meta, o, n1, cot_t):
    tokens = n1.shape[0]
    return pl.pallas_call(
        mix_body,
        in_specs=[SCALARS] + [WHOLE] * 3,
        out_specs=[WHOLE] * 3,
        out_shape=[jax.ShapeDtypeStruct((tokens, D), BF)]
        + [jax.ShapeDtypeStruct((2 * COT_ROWS + 4 * tokens, 256), BF)] * 2,
        compiler_params=params(),
        cost_estimate=cost(1, 1),
        name="mix_heads",
    )(meta, o, n1, cot_t)


def residual_body(nw, meta, x_ref, mix_ref, gain_ref, *refs):
    w_refs = refs[:nw]
    res_ref, n2_ref, n2b_ref, proj_scr, sems = refs[nw:]
    plan = proj_plan_of(w_refs, proj_scr, meta, sems)
    plan_start(plan, meta)
    plan_wait(plan, meta)
    residual = x_ref[...].astype(F32) + jnp.dot(
        mix_ref[...], proj_scr[:, :D], preferred_element_type=F32
    )
    res_ref[...] = residual
    scale = lax.rsqrt(jnp.mean(residual * residual, axis=1, keepdims=True) + NORM_EPSILON)
    n2_ref[...] = (residual * scale * gain_ref[1:2, :]).astype(BF)
    tokens = x_ref.shape[0]
    width = D // 4
    for b in range(4):
        rows = slice(b * tokens, (b + 1) * tokens)
        n2b_ref[rows, 128:256] = jnp.zeros((tokens, 128), BF)
        n2b_ref[rows, :width] = n2_ref[:, b * width : (b + 1) * width]


def residual_call(meta, x, mixed, gains, proj):
    tokens = x.shape[0]
    nw = len(proj)
    return pl.pallas_call(
        functools.partial(residual_body, nw),
        in_specs=[SCALARS] + [WHOLE] * 3 + [ANY] * nw,
        out_specs=[WHOLE] * 3,
        out_shape=[
            jax.ShapeDtypeStruct((tokens, D), F32),
            jax.ShapeDtypeStruct((tokens, D), BF),
            jax.ShapeDtypeStruct((4 * tokens, 256), BF),
        ],
        scratch_shapes=[pltpu.VMEM((D, 1024), BF), pltpu.SemaphoreType.DMA((13,))],
        compiler_params=params(),
        cost_estimate=cost(1, 1),
        name="residual",
    )(meta, x, mixed, gains, *proj)


def mlp_body(counts, meta, res_ref, n2_ref, cot_ref, *refs):
    n_gu, n_down = counts
    gu_refs = refs[:n_gu]
    down_refs = refs[n_gu : n_gu + n_down]
    (
        out_ref,
        dn_scr,
        act_ref,
        late_own_ref,
        late_send_ref,
        gu_scr,
        down_scr,
        acc_scr,
        act_scr,
        dgu_scr,
        gu_sems,
        down_sems,
        out_sems,
    ) = refs[n_gu + n_down :]
    down_plan = down_copies(down_refs, down_scr, meta, down_sems)
    gu_copies = gateup_copies(gu_refs, gu_scr, meta, gu_sems, MLP_TILE)
    start_all(gu_copies[0])
    start_all(down_plan)
    for one in gu_copies[1:]:
        start_all(one)
    tiles = FF // MLP_TILE
    core = meta[1]
    out_copies = []
    for f in range(tiles):
        cols = slice(f * MLP_TILE, (f + 1) * MLP_TILE)
        wait_all(gu_copies[f])
        normed = n2_ref[...]
        gate = jnp.dot(normed, gu_scr[0, :, cols], preferred_element_type=F32)
        up = jnp.dot(normed, gu_scr[1, :, cols], preferred_element_type=F32)
        if f == 0:
            wait_all(down_plan)
        grad_act = jnp.dot(cot_ref[...], down_scr[:, cols], preferred_element_type=F32)
        gated = 1.0 / (1.0 + jnp.exp(-gate))
        silu = gate * gated
        act = (silu * up).astype(BF)
        grad_gate = (grad_act * up * gated * (1.0 + gate * (1.0 - gated))).astype(BF)
        grad_up = (grad_act * silu).astype(BF)
        act_scr[f] = act
        dgu_scr[0, :, cols] = grad_gate
        dgu_scr[1, :, cols] = grad_up
        add_out = lax.dot_general(act, down_scr[:, cols], NT, preferred_element_type=F32)
        add_dn = lax.dot_general(
            grad_gate, gu_scr[0, :, cols], NT, preferred_element_type=F32
        ) + lax.dot_general(grad_up, gu_scr[1, :, cols], NT, preferred_element_type=F32)
        if f == 0:
            acc_scr[...] = add_out
            dn_scr[...] = add_dn
        else:
            acc_scr[...] += add_out
            dn_scr[...] += add_dn
        copies = [pltpu.make_async_copy(act_scr.at[f], act_ref.at[f], out_sems.at[f, 0])]
        for i, ref in enumerate((late_own_ref, late_send_ref)):
            copies.append(
                pltpu.make_async_copy(
                    dgu_scr.at[core if i == 0 else 1 - core, :, pl.ds(f * MLP_TILE, MLP_TILE)],
                    ref.at[:, pl.ds(f * MLP_TILE, MLP_TILE)],
                    out_sems.at[f, 2 + i],
                )
            )
        start_all(copies)
        out_copies += copies
    out_ref[...] = transposed_back((res_ref[...] + acc_scr[...]).astype(BF))
    wait_all(out_copies)


def norm_back_body(nw, meta, res_ref, dn_ref, cot_ref, mix_ref, gain_ref, *refs):
    proj_refs = refs[:nw]
    gres_ref, gb_ref, do_ref, gain_out_ref, proj_scr, dn_scr, sems = refs[nw:]
    proj_plan = proj_plan_of(proj_refs, proj_scr, meta, sems)
    plan_start(proj_plan, meta)
    lane = lanes()
    gain = gain_ref[1:2, :]
    residual = res_ref[...]
    scale = lax.rsqrt(jnp.mean(residual * residual, axis=1, keepdims=True) + NORM_EPSILON)
    grad = dn_ref[...]
    gain_out_ref[...] = jnp.broadcast_to(
        jnp.sum(grad * residual * scale, axis=0, keepdims=True), (8, D)
    )
    scaled = grad * gain
    mean = jnp.mean(scaled * residual, axis=1, keepdims=True)
    grad_residual = (
        cot_ref[...].astype(F32) + scale * scaled - residual * (scale * scale * scale * mean)
    )
    gres_ref[...] = grad_residual
    branch = grad_residual.astype(BF)
    gb_ref[:, :D] = branch
    gb_ref[:, D:] = jnp.zeros((branch.shape[0], 1024 - D), BF)
    plan_wait(proj_plan, meta)
    dn_scr[...] = lax.dot_general(
        gb_ref[:, :D], proj_scr[:, :D], NT, preferred_element_type=F32
    )
    ones = (
        (lax.broadcasted_iota(jnp.int32, (128, 128), 0) < 64)
        == (lax.broadcasted_iota(jnp.int32, (128, 128), 1) < 64)
    ).astype(BF)
    half_lane = lane % 64
    for t in range(8):
        if t < 7:
            gm = dn_scr[:, 128 * t : 128 * (t + 1)].astype(BF)
            mixed = mix_ref[:, 128 * t : 128 * (t + 1)]
        else:
            gm = dn_scr[:, 896:960].astype(BF)
            gm = jnp.concatenate([gm, jnp.zeros_like(gm)], axis=1)
            mixed = mix_ref[:, 896:960]
            mixed = jnp.concatenate([mixed, jnp.zeros_like(mixed)], axis=1)
        gm = gm.astype(F32)
        product = gm * mixed.astype(F32)
        high = product.astype(BF)
        low = (product - high.astype(F32)).astype(BF)
        inner = jnp.dot(high, ones, preferred_element_type=F32) + jnp.dot(
            low, ones, preferred_element_type=F32
        )
        high, mid, low = split3(-inner)
        extra = jnp.where(half_lane == LANE_INNER + 2, low.astype(F32), 0.0)
        extra = jnp.where(half_lane == LANE_INNER + 1, mid.astype(F32), extra)
        extra = jnp.where(half_lane == LANE_INNER, high.astype(F32), extra)
        do_ref[2 * t] = jnp.where(lane < 64, extra, pltpu.roll(gm, 64, 1)).astype(BF)
        if 2 * t + 1 < HEADS:
            do_ref[2 * t + 1] = jnp.where(lane < 64, pltpu.roll(extra, 64, 1), gm).astype(BF)


def norm_back_call(meta, residual, dn, cot, mixed, gains, proj):
    tokens = cot.shape[0]
    nw = len(proj)
    return pl.pallas_call(
        functools.partial(norm_back_body, nw),
        in_specs=[SCALARS] + [WHOLE] * 5 + [ANY] * nw,
        out_specs=[WHOLE] * 4,
        out_shape=[
            jax.ShapeDtypeStruct((tokens, D), F32),
            jax.ShapeDtypeStruct((tokens, 1024), BF),
            jax.ShapeDtypeStruct((HEADS, tokens, 128), BF),
            jax.ShapeDtypeStruct((8, D), F32),
        ],
        scratch_shapes=[
            pltpu.VMEM((D, 1024), BF),
            pltpu.VMEM((tokens, D), F32),
            pltpu.SemaphoreType.DMA((13,)),
        ],
        compiler_params=params(),
        cost_estimate=cost(2 * tokens * D * D, 12 << 20),
        name="norm_backward",
    )(meta, residual, dn, cot, mixed, gains, *proj)


def mlp_call(meta, residual, n2, cot, gateup, down):
    tokens = n2.shape[0]
    counts = (len(gateup), len(down))
    tiles = FF // MLP_TILE
    return pl.pallas_call(
        functools.partial(mlp_body, counts),
        in_specs=[SCALARS] + [WHOLE] * 3 + [ANY] * sum(counts),
        out_specs=[WHOLE] * 2 + [ANY] * 3,
        out_shape=[
            jax.ShapeDtypeStruct((D, tokens), BF),
            jax.ShapeDtypeStruct((tokens, D), F32),
            jax.ShapeDtypeStruct((tiles, tokens, MLP_TILE), BF),
            jax.ShapeDtypeStruct((tokens, FF), BF),
            jax.ShapeDtypeStruct((tokens, FF), BF),
        ],
        scratch_shapes=[
            pltpu.VMEM((2, D, FF), BF),
            pltpu.VMEM((D, FF), BF),
            pltpu.VMEM((tokens, D), F32),
            pltpu.VMEM((tiles, tokens, MLP_TILE), BF),
            pltpu.VMEM((2, tokens, FF), BF),
            pltpu.SemaphoreType.DMA((tiles, 8)),
            pltpu.SemaphoreType.DMA((8,)),
            pltpu.SemaphoreType.DMA((tiles, 4)),
        ],
        compiler_params=params(),
        cost_estimate=cost(2 * tokens * D * (6 * FF), 40 << 20),
        name="feed_forward",
    )(meta, residual, n2, cot, *gateup, *down)


def joined_body(
    nw, shards, meta, dq_ref, cos_ref, sin_ref, x_ref, gain_ref, gres_ref, gain_two_ref, *refs
):
    dkv_ref = refs[0]
    w_refs = refs[1 : 1 + nw]
    gj_ref, ig_ref, w_scr, g_scr, sems = refs[-5:]
    plan = qkv_plan(w_refs, w_scr, meta, sems)
    tokens = x_ref.shape[0]
    plan_start(plan, meta)
    lane = lanes()
    cosine = cos_ref[...]
    sine = -sin_ref[...]
    heads = {}

    def dkv(g):
        if g not in heads:
            at = slice(128 * g, 128 * (g + 1))
            total = dkv_ref[:tokens, at].astype(F32)
            for j in range(1, shards):
                total = total + dkv_ref[j * tokens : (j + 1) * tokens, at].astype(F32)
            heads[g] = (total, pltpu.roll(total, 64, 1))
        return heads[g]

    def dq(h):
        return dq_ref[h]

    def low_half(h):
        if h < HEADS:
            return dq(h)
        if h < HEADS + KV_HEADS:
            return dkv(h - HEADS)[0]
        return dkv(h - HEADS - KV_HEADS)[1]

    def high_half(h):
        if h < HEADS:
            return pltpu.roll(dq(h), 64, 1)
        if h < HEADS + KV_HEADS:
            return dkv(h - HEADS)[1]
        return dkv(h - HEADS - KV_HEADS)[0]

    for t in range(13):
        if t == 12:
            last = jnp.where(lane < 64, low_half(24), 0.0).astype(BF)
            gj_ref[:tokens, 1536:1664] = last
            continue
        tile = jnp.where(lane < 64, low_half(2 * t), high_half(2 * t + 1))
        if t < 10:
            tile = rope_tile(tile, cosine, sine)
        gj_ref[:tokens, 128 * t : 128 * (t + 1)] = tile.astype(BF)
    plan_wait(plan, meta)
    g_scr[...] = lax.dot_general(
        gj_ref[:tokens, :QKV], w_scr[...], NT, preferred_element_type=F32
    )
    grad = g_scr[...]
    x = x_ref[...].astype(F32)
    scale = lax.rsqrt(jnp.mean(x * x, axis=1, keepdims=True) + NORM_EPSILON)
    gj_ref[tokens:, :] = jnp.zeros((16, gj_ref.shape[1]), BF)
    gain_one = jnp.sum(grad * x * scale, axis=0, keepdims=True)
    gj_ref[tokens : tokens + 2, :D] = jnp.concatenate(
        [gain_one, gain_two_ref[:1]], axis=0
    ).astype(BF)
    scaled = grad * gain_ref[0:1, :]
    mean = jnp.mean(scaled * x, axis=1, keepdims=True)
    ig_ref[...] = transposed_back(
        gres_ref[...] + scale * scaled - x * (scale * scale * scale * mean)
    )


def joined_call(meta, dq, cosine, sine, x, gains, gres, gain_two, dkv, weights, deps):
    tokens = x.shape[0]
    nw = len(weights)
    shards = dkv.shape[0] // tokens
    return pl.pallas_call(
        functools.partial(joined_body, nw, shards),
        in_specs=[SCALARS] + [WHOLE] * 8 + [ANY] * (nw + len(deps)),
        out_specs=[WHOLE] * 2,
        out_shape=[
            jax.ShapeDtypeStruct((tokens + 16, 1664), BF),
            jax.ShapeDtypeStruct((D, tokens), F32),
        ],
        scratch_shapes=[
            pltpu.VMEM((D, QKV), BF),
            pltpu.VMEM((tokens, D), F32),
            pltpu.SemaphoreType.DMA((8,)),
        ],
        compiler_params=params(),
        cost_estimate=cost(2 * tokens * D * QKV, 16 << 20),
        name="joined_backward",
    )(meta, dq, cosine, sine, x, gains, gres, gain_two, dkv, *weights, *deps)


def block_rows(block, tokens):
    return slice(2 * COT_ROWS + block * tokens, 2 * COT_ROWS + (block + 1) * tokens)


def gateup_grad_body(meta, own_ref, oth_ref, b_own, b_oth, *refs):
    out = refs[-1]
    tokens = b_own.shape[0]
    width = D // 4
    for j in range(4):
        rows = slice(j * tokens, (j + 1) * tokens)
        total = lax.dot_general(
            own_ref[rows, 0:256], b_own[...], TN, preferred_element_type=F32
        ) + lax.dot_general(oth_ref[rows, 0:256], b_oth[...], TN, preferred_element_type=F32)
        out[j * width : (j + 1) * width] = total[:width].astype(BF)


def gateup_grad_call(meta, n2_own, n2_oth, late_own, late_oth, deps):
    tokens = late_own.shape[0]
    tile = 640
    whole = pl.BlockSpec(n2_own.shape, lambda i, s: (0, 0))
    cols = pl.BlockSpec((tokens, tile), lambda i, s: (0, i))
    return pl.pallas_call(
        gateup_grad_body,
        grid_spec=pltpu.PrefetchScalarGridSpec(
            num_scalar_prefetch=1,
            grid=(FF // tile,),
            in_specs=[whole] * 2 + [cols] * 2 + [ANY] * len(deps),
            out_specs=pl.BlockSpec((D, tile), lambda i, s: (0, i)),
        ),
        out_shape=jax.ShapeDtypeStruct((D, FF), BF),
        compiler_params=params(),
        cost_estimate=cost(4 * tokens * D * FF, 20 << 20),
        name="gateup_gradient",
    )(meta, n2_own, n2_oth, late_own, late_oth, *deps)


DP_ROWS = COT_ROWS + 2 * PIECE


def down_proj_grad_body(meta, own_ref, oth_ref, act_own, act_oth, gb_own, gb_oth, *refs):
    tokens = gb_own.shape[0]
    for block in range(4):
        out = refs[-1].at[pl.ds(block * DP_ROWS, DP_ROWS)]
        total = None
        for cot_rows, act_ref in ((own_ref, act_own), (oth_ref, act_oth)):
            for n in range(2):
                term = jnp.dot(
                    cot_rows[n * COT_ROWS : (n + 1) * COT_ROWS],
                    act_ref[block, n * 256 : (n + 1) * 256],
                    preferred_element_type=F32,
                )
                total = term if total is None else total + term
        out[:COT_ROWS] = total.astype(BF)
        rows = block_rows(block, tokens)
        total = lax.dot_general(
            own_ref[rows, 0:128], gb_own[...], TN, preferred_element_type=F32
        ) + lax.dot_general(oth_ref[rows, 0:128], gb_oth[...], TN, preferred_element_type=F32)
        total = total.astype(BF)
        out[COT_ROWS : COT_ROWS + PIECE] = total[:, :640]
        out[COT_ROWS + PIECE :, :384] = total[:, 640:]
        out[COT_ROWS + PIECE :, 384:] = jnp.zeros((PIECE, 256), BF)


def down_proj_grad_call(meta, early_own, early_oth, act_own, act_oth, gb_own, gb_oth, deps):
    blocks, tokens, width = act_own.shape
    return pl.pallas_call(
        down_proj_grad_body,
        in_specs=[SCALARS] + [WHOLE] * 6 + [ANY] * len(deps),
        out_specs=WHOLE,
        out_shape=jax.ShapeDtypeStruct((4 * DP_ROWS, width), BF),
        compiler_params=params(),
        cost_estimate=cost(2 * tokens * D * (FF + D), 16 << 20),
        name="down_proj_gradient",
    )(meta, early_own, early_oth, act_own, act_oth, gb_own, gb_oth, *deps)


def qkv_grad_body(meta, own_ref, oth_ref, gj_own, gj_oth, *refs):
    tokens = gj_own.shape[0] - 16
    width = D // 4
    sums = (
        gj_own[tokens : tokens + 16, :].astype(F32) + gj_oth[tokens : tokens + 16, :].astype(F32)
    ).astype(BF)
    for block in range(4):
        rows = block_rows(block, tokens)
        total = lax.dot_general(
            own_ref[rows, 128:256], gj_own[:tokens, :], TN, preferred_element_type=F32
        ) + lax.dot_general(
            oth_ref[rows, 128:256], gj_oth[:tokens, :], TN, preferred_element_type=F32
        )
        total = total[:, :QKV].astype(BF)
        part = sums[:, block * width : (block + 1) * width]
        part = jnp.concatenate([part, jnp.zeros((PIECE_ROWS - PIECE, QKV - width), BF)], axis=1)
        for j, out in enumerate(refs[-4:]):

            @pl.when((meta[0] ^ j) == block)
            def _(out=out, total=total, part=part):
                out[:PIECE] = total
                out[PIECE:] = part


def qkv_grad_call(meta, early_own, early_oth, gj_own, gj_oth, deps):
    return pl.pallas_call(
        qkv_grad_body,
        in_specs=[SCALARS] + [WHOLE] * 4 + [ANY] * len(deps),
        out_specs=[WHOLE] * 4,
        out_shape=[jax.ShapeDtypeStruct((PIECE_ROWS, QKV), BF)] * 4,
        compiler_params=params(),
        cost_estimate=cost(2 * gj_own.shape[0] * D * QKV, 8 << 20),
        name="qkv_gradient",
    )(meta, early_own, early_oth, gj_own, gj_oth, *deps)


def total_of(refs, blocks=1):
    total = None
    for ref in refs:
        rows = ref.shape[0] // blocks
        for i in range(blocks):
            term = ref[i * rows : (i + 1) * rows].astype(F32)
            total = term if total is None else total + term
    return total.astype(BF)


def cut_along(value, axis, parts):
    size = value.shape[axis] // parts
    if axis == 0:
        return [value[i * size : (i + 1) * size] for i in range(parts)]
    return [value[:, i * size : (i + 1) * size] for i in range(parts)]


def add_job(inputs, blocks=1):
    rows, columns = inputs[0].shape

    def body(meta, ins, outs):
        outs[0][...] = total_of(ins, blocks)

    return inputs, [(rows // blocks, columns)], body


def copy_job(value):
    def body(meta, ins, outs):
        outs[0][...] = ins[0][...]

    return [value], [value.shape], body


def rows_job(value, rows):
    def body(meta, ins, outs):
        at = pl.multiple_of(meta[1] * rows, 16)
        outs[0][...] = ins[0][pl.ds(at, rows), :]

    return [value], [(rows, value.shape[1])], body


def split_job(inputs, axis, at, blocks=1):
    shape = list(inputs[0].shape)
    shape[0] //= blocks
    shape[axis] //= 2

    def body(meta, ins, outs):
        low, high = cut_along(total_of(ins, blocks), axis, 2)
        bit = meta[at]
        outs[0][...] = jnp.where(bit == 0, low, high)
        outs[1][...] = jnp.where(bit == 0, high, low)

    return inputs, [tuple(shape)] * 2, body


def join_job(mine, theirs, axis, at):
    shape = list(mine.shape)
    shape[axis] *= 2

    def body(meta, ins, outs):
        bit = meta[at]
        a, b = ins[0][...], ins[1][...]
        low, high = jnp.where(bit == 0, a, b), jnp.where(bit == 0, b, a)
        size = a.shape[axis]
        if axis == 0:
            outs[0][:size] = low
            outs[0][size:] = high
        else:
            outs[0][:, :size] = low
            outs[0][:, size:] = high

    return [mine, theirs], [tuple(shape)], body


def whole_job(inputs):
    rows, columns = inputs[0].shape

    def body(meta, ins, outs):
        place = meta[2] + 2 * meta[3]
        for i in range(4):
            back = (place + 4 - i) % 4
            value = ins[3][...]
            for k in range(3):
                value = jnp.where(back == k, ins[k][...], value)
            outs[0][i * rows : (i + 1) * rows] = value

    return inputs, [(4 * rows, columns)], body


def stage_body(jobs, meta, *refs):
    outs = refs[-sum(len(job[1]) for job in jobs) :]
    at_in = at_out = 0
    for ins, shapes, body in jobs:
        body(meta, refs[at_in : at_in + len(ins)], outs[at_out : at_out + len(shapes)])
        at_in += len(ins)
        at_out += len(shapes)


def stage(name, meta, jobs, deps):
    inputs = [one for job in jobs for one in job[0]]
    shapes = [shape for job in jobs for shape in job[1]]
    results = pl.pallas_call(
        functools.partial(stage_body, jobs),
        in_specs=[SCALARS] + [WHOLE] * len(inputs) + [ANY] * len(deps),
        out_specs=[WHOLE] * len(shapes),
        out_shape=[jax.ShapeDtypeStruct(shape, BF) for shape in shapes],
        compiler_params=params(),
        cost_estimate=cost(0, 8 << 20),
        name=name,
    )(meta, *inputs, *deps)
    grouped, at = [], 0
    for job in jobs:
        grouped.append(list(results[at : at + len(job[1])]))
        at += len(job[1])
    return grouped


def adamw_step(grad_sum, master, first, second, rate, decay):
    first_new = BETA_FIRST * first + (1.0 - BETA_FIRST) * grad_sum
    second_new = BETA_SECOND * second + (1.0 - BETA_SECOND) * grad_sum * grad_sum
    corrected = (
        first_new
        / (1.0 - BETA_FIRST**STEP)
        / (jnp.sqrt(second_new / (1.0 - BETA_SECOND**STEP)) + ADAM_EPSILON)
    )
    master_new = master - rate * (corrected + decay * master)
    return (master_new, master_new.astype(jnp.bfloat16), first_new, second_new)


def pick_core(meta, half, mine, other):
    return jnp.where(meta[1] == half, mine, other).astype(F32)


def gateup_grads(meta, step, mine, other):
    halves = [pick_core(meta, half, mine[...], other[...]) for half in range(2)]
    return jnp.concatenate(halves, axis=1)


def down_grads(meta, step, mine, other):
    return pick_core(meta, step // 2, mine[...], other[...])


def proj_grads(meta, step, mine, other):
    def piece(half):
        top = pick_core(meta, half, mine[COT_ROWS : COT_ROWS + PIECE], other[COT_ROWS : COT_ROWS + PIECE])
        rest = pick_core(meta, half, mine[COT_ROWS + PIECE :], other[COT_ROWS + PIECE :])
        return jnp.concatenate([top, rest], axis=1)[:, :D]

    return jnp.where(step == 0, piece(0)[:120], piece(1)[8:])


def qkv_grads(meta, step, mine, other):
    low = pick_core(meta, 0, mine[...], other[...])[:120]
    high = pick_core(meta, 1, mine[...], other[...])[8:128]
    return jnp.where(step == 0, low, high)


def adamw_body(grads_of, rate, meta, mine, other, master, first, second, *refs):
    grad_out, master_out, copy_out, first_out, second_out = refs[-5:]
    grad = grads_of(meta, pl.program_id(0), mine, other)
    grad_out[...] = grad
    new = adamw_step(grad, master[...], first[...], second[...], rate, DECAY_RATE)
    master_out[...], copy_out[...], first_out[...], second_out[...] = new


def adamw_call(meta, grads_of, pair, pair_spec, states, block, spec, steps, rate, name, deps):
    shape = states[0].shape
    own = pl.BlockSpec(block, spec)
    types = (F32, F32, BF, F32, F32)
    return pl.pallas_call(
        functools.partial(adamw_body, grads_of, rate),
        grid_spec=pltpu.PrefetchScalarGridSpec(
            num_scalar_prefetch=1,
            grid=(steps,),
            in_specs=[pair_spec] * 2 + [own] * 3 + [ANY] * len(deps),
            out_specs=[own] * 5,
        ),
        out_shape=[jax.ShapeDtypeStruct(shape, one) for one in types],
        compiler_params=params(),
        cost_estimate=cost(0, 34 * shape[0] * shape[1]),
        name=name,
    )(meta, *pair, *states, *deps)


def row_tables(doc_lengths, row, offset, tokens):
    ends = jnp.cumsum(doc_lengths, dtype=jnp.int32)
    starts = ends - doc_lengths
    blocks = (doc_lengths + BLOCK - 1) // BLOCK
    bases = jnp.cumsum(blocks, dtype=jnp.int32) - blocks
    places = jnp.arange(row, dtype=jnp.int32)
    inside = (places[:, None] >= starts[None, :]) & (places[:, None] < ends[None, :])

    def pick(values):
        return jnp.sum(jnp.where(inside, values[None, :], 0), axis=1, dtype=jnp.int32)

    doc_start, doc_end, base = pick(starts), pick(ends), pick(bases)
    position = places - doc_start
    segment = base + position // BLOCK
    reach = jnp.minimum(doc_end, doc_start + BLOCK * (position // BLOCK + 1))
    lane = jnp.arange(128, dtype=jnp.int32)
    aug = ((lane[None, :] == segment[:, None] + 64) | (lane[None, :] >= LANE_LOG)).astype(BF)

    def own(values):
        return lax.dynamic_slice_in_dim(values, offset, tokens)

    doc_start, reach, base, segment = own(doc_start), own(reach), own(base), own(segment)
    seen = (lane[None, :] >= base[:, None] + 64) & (lane[None, :] <= segment[:, None] + 64)
    open_lane = seen | (lane[None, :] >= LANE_LOG) | (lane[None, :] < 64)
    qmask = jnp.where(open_lane, 0.0, -1e30).astype(BF)
    chunks = tokens // QC
    low = jnp.min(doc_start.reshape(chunks, QC), axis=1) // KT
    high = (jnp.max(reach.reshape(chunks, QC), axis=1) + KT - 1) // KT
    ranges = jnp.stack([low, high], axis=1).reshape(-1).astype(jnp.int32)
    half = HEAD_DIM // 2
    frequency = ROPE_THETA ** (-2.0 * jnp.arange(half, dtype=F32) / HEAD_DIM)
    angles = own(position).astype(F32)[:, None] * frequency[None, :]
    cosine, sine = jnp.cos(angles), jnp.sin(angles)
    cosine = jnp.concatenate([cosine] * 4, axis=1)
    sine = jnp.concatenate([-sine, sine, -sine, sine], axis=1)
    return aug, qmask, ranges, cosine, sine


def local(
    shards,
    depth,
    tokens,
    cotangent,
    lengths,
    qkv_copy,
    qkv_master,
    qkv_first,
    qkv_second,
    proj_copy,
    proj_master,
    proj_first,
    proj_second,
    gateup_copy,
    gateup_master,
    gateup_first,
    gateup_second,
    down_copy,
    down_master,
    down_first,
    down_second,
    gain_copy,
    gain_master,
    gain_first,
    gain_second,
):
    fast = shards == 4 and depth == 4
    me = lax.axis_index("shard")
    z = lax.axis_index("deep")
    core = lax.axis_index("core")
    count = tokens.shape[0]

    def over_shard(value, flip):
        return lax.ppermute(value, "shard", [(s, s ^ flip) for s in range(shards)])

    def over_core(value):
        return lax.ppermute(value, "core", [(0, 1), (1, 0)])

    def over_deep(value, flip):
        return lax.ppermute(value, "deep", [(s, s ^ flip) for s in range(depth)])

    def all_shards(value):
        return lax.all_to_all(value, "shard", 0, 0, tiled=True)

    def over_deep_by(value, steps):
        return lax.ppermute(value, "deep", [(d, (d + steps) % depth) for d in range(depth)])

    def deep_start(name, parts, axis):
        (kept,) = stage(name + "_over_shard", meta, [split_job([parts], axis, 2, 4)], ())
        return kept[0], over_deep(kept[1], 1)

    def deep_end(name, pair, axis):
        (kept,) = stage(name + "_over_near", meta, [split_job(list(pair), axis, 3)], ())
        far = over_deep(kept[1], 2)
        ((kept,),) = stage(name + "_over_far", meta, [add_job([kept[0], far])], ())
        far = over_deep(kept, 2)
        ((kept,),) = stage(name + "_join_far", meta, [join_job(kept, far, axis, 3)], ())
        near = over_deep(kept, 1)
        ((kept,),) = stage(name + "_join_near", meta, [join_job(kept, near, axis, 2)], ())
        return kept

    def hop(value, flips):
        pairs = [
            (s * depth + d, (s ^ flips[d % 2]) * depth + d)
            for s in range(shards)
            for d in range(depth)
        ]
        return lax.ppermute(value, ("shard", "deep"), pairs)

    def first_hop(piece):
        return hop(piece, (1, 2))

    def second_hop(one):
        return over_deep(one, 1), hop(one, (2, 1))

    def swapped(pieces):
        return tuple(pieces) + tuple(over_core(piece) for piece in pieces)

    aug, qmask, ranges, cosine, sine = row_tables(
        lengths[0], count * shards, me * count, count
    )
    meta = jnp.concatenate([jnp.stack([me, core, z % 2, (z // 2) % 2]).astype(jnp.int32), ranges])

    tokens_t = tokens.T
    cot_t = cotangent.T
    down_t = down_copy.T
    if fast:
        pad = qkv_copy.shape[0] - PIECE
        extra = jnp.pad(gain_copy, ((0, PIECE_ROWS - PIECE - 2), (0, QKV - gain_copy.shape[1])))
        piece = jnp.concatenate(
            [lax.dynamic_slice_in_dim(qkv_copy, core * pad, PIECE), extra], axis=0
        )
        one = first_hop(piece)
        qkv_w = (qkv_copy,) + swapped((one,) + second_hop(one))
        gp_half, proj_wide = cut_call(meta, gateup_copy, proj_copy, piece)
        gp_one = first_hop(gp_half)
        gain = gain_copy
        early = (cosine, sine, aug, qmask, meta, gp_half)
    else:
        qkv_w, proj_w, gateup_w = (
            (lax.all_gather(w, "shard", axis=0, tiled=True),)
            for w in (qkv_copy, proj_copy, gateup_copy)
        )
        proj_w = (jnp.pad(proj_w[0], ((0, 0), (0, 1024 - D))),)
        down_w = (lax.all_gather(down_t, "shard", axis=1, tiled=True),)
        gain = lax.all_gather(gain_copy, "shard", axis=1, tiled=True)
        early = ()

    x_rows, cot_rows, scaled = first_norm_call(tokens_t, cot_t, early)
    n1, gains, kv = kv_call(meta, scaled, gain, cosine, sine, qkv_w)
    kv = [kv] + [over_shard(kv, j) for j in range(1, shards)]
    q, qn = q_call(meta, n1, cosine, sine, qkv_w)
    deps = ()
    if fast:
        (gp_one,) = after((gp_one,), (q, *kv))
        ((down_half,),) = stage("cut_down", meta, [rows_job(down_t, D // 2)], (gp_one,))
        deps = (down_half,)
        gp_two, gp_three = second_hop(gp_one)
        gp_one_oth = over_core(gp_one)
        down_one = first_hop(down_half)
    o, q2 = attend_forward(meta, q, qmask, qn, aug, kv, deps)
    if fast:
        gp_two, gp_three, down_one = after((gp_two, gp_three, down_one), (o,))
        gp_w = (gp_one, gp_two, gp_three, gp_one_oth, over_core(gp_two), over_core(gp_three))
        gateup_w = (gateup_copy,) + gp_w
        proj_w = (proj_wide,) + gp_w
        down_two, down_three = second_hop(down_one)
    mixed, early_own, early_send = mix_call(meta, o, n1, cot_t)
    residual, n2, n2_blocks = residual_call(meta, x_rows, mixed, gains, proj_w)
    if fast:
        down_w = (down_t,) + swapped(after((down_one, down_two, down_three), (residual,)))
    output_t, dn, act, late_own, late_send = mlp_call(
        meta, residual, n2, cot_rows, gateup_w, down_w
    )
    grad_residual, grad_branch, do, gain_two = norm_back_call(
        meta, residual, dn, cot_rows, mixed, gains, proj_w
    )

    deps = ()
    if fast:
        early_oth = over_core(early_send)
        n2_oth = over_core(n2_blocks)
        late_oth = over_core(late_send)
        act_oth = over_core(act)
        branch_oth = over_core(grad_branch)
        gp_g = gateup_grad_call(
            meta, n2_blocks, n2_oth, late_own, late_oth, (grad_branch,)
        )
        gp_parts = all_shards(gp_g)
        deps = (gp_g,)
    dq, dkv = attend_backward(meta, q2, do, aug, kv, deps)
    deps = ()
    if fast:
        (gp_parts,) = after((gp_parts,), (dq,))
    dkv = all_shards(dkv)
    if fast:
        (gp,) = stage("gateup_over_shard", meta, [split_job([gp_parts], 1, 2, 4)], ())
        gp_recv = over_deep(gp[1], 1)
        dp_g = down_proj_grad_call(
            meta, early_own, early_oth, act, act_oth, grad_branch, branch_oth, (gp[0],)
        )
        (gp,) = stage(
            "gateup_over_near", meta, [split_job([gp[0], gp_recv], 1, 3)], (dp_g,)
        )
        gp_recv = over_deep(gp[1], 2)
        deps = (gp[0],)
    grad_joined, input_grad_t = joined_call(
        meta,
        dq,
        cosine,
        sine,
        x_rows,
        gains,
        grad_residual,
        gain_two,
        dkv,
        qkv_w,
        deps,
    )
    rates = (D ** (-0.5), max(HEAD_DIM // 16, 1) ** (-0.5), D ** (-0.5), FF ** (-0.5))
    qkv_states = (qkv_master, qkv_first, qkv_second)
    proj_states = (proj_master, proj_first, proj_second)
    gateup_states = (gateup_master, gateup_first, gateup_second)
    down_states = (down_master.T, down_first.T, down_second.T)
    if fast:
        joined_oth = over_core(grad_joined)
        (dp_g,) = after((dp_g,), (grad_joined,))
        dp_parts = all_shards(dp_g)
        qkv_g = qkv_grad_call(meta, early_own, early_oth, grad_joined, joined_oth, ())
        qkv_parts = [qkv_g[0]] + [over_shard(qkv_g[j], j) for j in range(1, 4)]
        ((gp,),) = stage("gateup_over_far", meta, [add_job([gp[0], gp_recv])], (qkv_g[0],))
        gp_recv = over_deep(gp, 2)
        ((gp,),) = stage("gateup_join_far", meta, [join_job(gp, gp_recv, 1, 3)], ())
        gp_recv = over_deep(gp, 1)
        ((dp,),) = stage("down_over_shard", meta, [add_job([dp_parts], 4)], (gp,))
        dp_parts = lax.all_to_all(dp, "deep", 0, 0, tiled=True)
        (qkv,) = stage("qkv_over_shard", meta, [split_job(qkv_parts, 0, 2)], (dp,))
        qkv_recv = over_deep(qkv[1], 1)
        ((gp,),) = stage("gateup_join_near", meta, [join_job(gp, gp_recv, 1, 2)], (qkv[0],))
        gp_pair = (gp, over_core(gp))
        ((dp,),) = stage("down_over_deep", meta, [add_job([dp_parts], 4)], (gp,))
        dp_parts = [dp] + [over_deep_by(dp, k) for k in range(1, 4)]
        (qkv,) = stage("qkv_over_near", meta, [split_job([qkv[0], qkv_recv], 0, 3)], (dp,))
        qkv_recv = over_deep(qkv[1], 2)
        rows = gateup_copy.shape[0]
        gateup_new = adamw_call(
            meta,
            gateup_grads,
            gp_pair,
            pl.BlockSpec((48, FF), lambda i, m: (i, 0)),
            gateup_states,
            (48, 2 * FF),
            lambda i, m: (i, 0),
            rows // 48,
            rates[2],
            "gateup_step",
            (qkv[0],),
        )
        ((qkv,),) = stage(
            "qkv_over_far", meta, [add_job([qkv[0], qkv_recv])], (gateup_new[0],)
        )
        qkv_recv = over_deep(qkv, 2)
        ((dp,),) = stage("down_join", meta, [whole_job(dp_parts)], (qkv,))
        dp_pair = (dp, over_core(dp))
        ((qkv,),) = stage("qkv_join_far", meta, [join_job(qkv, qkv_recv, 0, 3)], (dp,))
        qkv_recv = over_deep(qkv, 1)
        down_new = adamw_call(
            meta,
            down_grads,
            dp_pair,
            pl.BlockSpec((D // 4, FF // 4), lambda i, m: (i % 2, 0)),
            down_states,
            (D // 4, FF // 4),
            lambda i, m: (i, 0),
            4,
            rates[3],
            "down_step",
            (qkv,),
        )
        proj_new = adamw_call(
            meta,
            proj_grads,
            dp_pair,
            pl.BlockSpec((DP_ROWS, FF // 4), lambda i, m: (0, 0)),
            proj_states,
            (rows // 2, D),
            lambda i, m: (i, 0),
            2,
            rates[1],
            "proj_step",
            (down_new[0],),
        )
        ((qkv,),) = stage(
            "qkv_join_near", meta, [join_job(qkv, qkv_recv, 0, 2)], (down_new[0],)
        )
        qkv_pair = (qkv, over_core(qkv))
        qkv_new = adamw_call(
            meta,
            qkv_grads,
            qkv_pair,
            pl.BlockSpec((PIECE_ROWS, QKV), lambda i, m: (0, 0)),
            qkv_states,
            (rows // 2, QKV),
            lambda i, m: (i, 0),
            2,
            rates[0],
            "qkv_step",
            (),
        )
        gain_grad = qkv[PIECE : PIECE + 2, : D // shards].astype(F32)
    else:

        def owned(left, right):
            whole = jnp.einsum("ta,tb->ab", left, right, preferred_element_type=F32)
            mine = lax.psum_scatter(whole, "shard", scatter_dimension=0, tiled=True)
            return lax.psum(mine, ("deep", "core"))

        def updated(grad, states, rate):
            return (grad,) + adamw_step(grad, *states, rate, DECAY_RATE)

        grad_gate = jnp.where(core == 0, late_own, late_send)
        grad_up = jnp.where(core == 0, late_send, late_own)
        down_grad_t = owned(act.transpose(1, 0, 2).reshape(count, FF), cotangent).T
        gateup_grad = owned(n2, jnp.concatenate([grad_gate, grad_up], axis=1))
        proj_grad = owned(mixed, grad_branch[:, :D])
        qkv_grad = owned(n1, grad_joined[:count, :QKV])
        gain_sum = lax.psum(
            grad_joined[count : count + 2, :D].astype(F32), ("shard", "deep", "core")
        )
        width = D // shards
        gain_grad = lax.dynamic_slice_in_dim(gain_sum, me * width, width, axis=1)
        qkv_new = updated(qkv_grad, qkv_states, rates[0])
        proj_new = updated(proj_grad, proj_states, rates[1])
        gateup_new = updated(gateup_grad, gateup_states, rates[2])
        down_new = updated(down_grad_t, down_states, rates[3])

    gain_new = adamw_step(gain_grad, gain_master, gain_first, gain_second, 0.5, 0.0)
    return (
        (output_t.T, input_grad_t.T)
        + tuple(qkv_new)
        + tuple(proj_new)
        + tuple(gateup_new)
        + tuple(one.T for one in down_new)
        + (gain_grad,)
        + gain_new
    )


def solution(mesh):
    shards, rep = mesh.shape["shard"], mesh.shape["rep"]
    depth = rep // 2
    fine = Mesh(mesh.devices.reshape(shards, depth, 2), ("shard", "deep", "core"))
    by_token = P(("deep", "core", "shard"), None)
    by_row = P("shard", None)
    by_column = P(None, "shard")
    return jax.shard_map(
        functools.partial(local, shards, depth),
        mesh=fine,
        in_specs=(by_token, by_token, P(("deep", "core"), None)) + (by_row,) * 16 + (by_column,) * 4,
        out_specs=(by_token,) * 2 + (by_row,) * 20 + (by_column,) * 5,
        check_vma=False,
    )
```

```python
import functools

import jax
import jax.numpy as jnp
from jax import lax
from jax.experimental import pallas as pl
from jax.experimental.pallas import tpu as pltpu
from jax.sharding import Mesh, PartitionSpec as P

D = 960
FF = 2560
HEADS = 15
KV_HEADS = 5
GROUP = 3
HEAD_DIM = 64
BLOCK = 256
STEP = 10
QKV = 1600

NORM_EPSILON = 1e-05
ROPE_THETA = 100000.0
BETA_FIRST = 0.5
BETA_SECOND = 0.6
ADAM_EPSILON = 1e-08
DECAY_RATE = 0.1

LOG2E = 1.4426950408889634
LN2 = 0.6931471805599453
QC = 256
KT = 256
NORM_ROWS = 16
SAFE = 60.0
LANE_LOG = 125
LANE_INNER = 61

F32 = jnp.float32
BF = jnp.bfloat16
NT = (((1,), (1,)), ((), ()))
TN = (((0,), (0,)), ((), ()))
VMEM_BYTES = 58 << 20
ANY = pl.BlockSpec(memory_space=pl.ANY)
WHOLE = pl.BlockSpec(memory_space=pltpu.VMEM)
SCALARS = pl.BlockSpec(memory_space=pltpu.SMEM)


def params():
    return pltpu.CompilerParams(vmem_limit_bytes=VMEM_BYTES)


def cost(flops, moved):
    del flops, moved
    return pl.CostEstimate(flops=1, bytes_accessed=1, transcendentals=0)


def after_body(*refs):
    del refs


def after(values, deps):
    values, deps = tuple(values), tuple(deps)
    return pl.pallas_call(
        after_body,
        in_specs=[ANY] * (len(values) + len(deps)),
        out_specs=[ANY] * len(values),
        out_shape=[jax.ShapeDtypeStruct(one.shape, one.dtype) for one in values],
        input_output_aliases={i: i for i in range(len(values))},
        compiler_params=params(),
        cost_estimate=cost(1, 1),
        name="after",
    )(*values, *deps)


def transposed(value):
    rows = value.shape[0]
    pad = -rows % 128
    if pad:
        value = jnp.concatenate([value, jnp.zeros((pad, value.shape[1]), value.dtype)], axis=0)
    return jnp.transpose(value)[:, :rows]


def transposed_back(value):
    columns = value.shape[1]
    pad = -columns % 128
    if pad:
        value = jnp.concatenate([value, jnp.zeros((value.shape[0], pad), value.dtype)], axis=1)
    return jnp.transpose(value)[:columns, :]


def lanes():
    return lax.broadcasted_iota(jnp.int32, (1, 128), 1)


def split3(value):
    high = value.astype(BF)
    rest = value - high.astype(F32)
    mid = rest.astype(BF)
    return high, mid, (rest - mid.astype(F32)).astype(BF)


def start_all(copies):
    for one in copies:
        one.start()


def wait_all(copies):
    for one in copies:
        one.wait()


PIECE = 128
PIECE_ROWS = 144
GRAD_ROWS = 128
GP_ROWS = 304


def qkv_plan(refs, target, meta, sems):
    if len(refs) == 1:
        return [pltpu.make_async_copy(refs[0], target, sems.at[0])], [], []
    rows = refs[0].shape[0]
    me, zpar = meta[0], meta[2]
    first = rows - PIECE
    own = target.at[pl.ds(pl.multiple_of(me * rows, 16), rows), :]
    common = [pltpu.make_async_copy(refs[0], own, sems.at[0])]
    by_core = ([], [])
    for k, rel in enumerate((1 + zpar, 2 - zpar, 3)):
        base = (me ^ rel) * rows
        low = target.at[pl.ds(pl.multiple_of(base, 16), first), :]
        high = target.at[pl.ds(pl.multiple_of(base + first, 16), PIECE), :]
        mine, other = refs[1 + k], refs[4 + k]
        for c in range(2):
            low_src, high_src = (mine, other) if c == 0 else (other, mine)
            by_core[c].append(
                pltpu.make_async_copy(low_src.at[pl.ds(0, first), :], low, sems.at[1 + k])
            )
            by_core[c].append(
                pltpu.make_async_copy(high_src.at[pl.ds(0, PIECE), :], high, sems.at[4 + k])
            )
    return common, by_core[0], by_core[1]


def proj_plan_of(refs, target, meta, sems):
    if len(refs) == 1:
        return [pltpu.make_async_copy(refs[0], target, sems.at[0])], [], []
    rows = refs[0].shape[0]
    me, zpar = meta[0], meta[2]
    first = rows - PIECE
    own = target.at[pl.ds(pl.multiple_of(me * rows, 16), rows), :]
    common = [pltpu.make_async_copy(refs[0], own, sems.at[0])]
    by_core = ([], [])
    top = GP_ROWS - 64
    for k, rel in enumerate((1 + zpar, 2 - zpar, 3)):
        base = (me ^ rel) * rows
        mine, other = refs[1 + k], refs[4 + k]
        for c in range(2):
            low_src, high_src = (mine, other) if c == 0 else (other, mine)
            jobs = (
                (low_src, 0, 64, 0),
                (low_src, 1, first - 64, 64),
                (high_src, 0, 64, first),
                (high_src, 1, 64, first + 64),
            )
            for n, (src, side, count, at) in enumerate(jobs):
                by_core[c].append(
                    pltpu.make_async_copy(
                        src.at[pl.ds(top, count), pl.ds(side * 1024, 1024)],
                        target.at[pl.ds(pl.multiple_of(base + at, 16), count), :],
                        sems.at[1 + 4 * k + n],
                    )
                )
    return common, by_core[0], by_core[1]


def plan_start(plan, meta):
    common, zero, one = plan
    start_all(common)
    if zero:
        pl.when(meta[1] == 0)(lambda: start_all(zero))
        pl.when(meta[1] == 1)(lambda: start_all(one))


def plan_wait(plan, meta):
    common, zero, one = plan
    wait_all(common)
    if zero:
        pl.when(meta[1] == 0)(lambda: wait_all(zero))
        pl.when(meta[1] == 1)(lambda: wait_all(one))


def gateup_copies(refs, target, meta, sems, tile):
    me, core, zpar = meta[0], meta[1], meta[2]
    rows = refs[0].shape[0]
    out = []
    for f in range(FF // tile):
        cols = pl.ds(f * tile, tile)
        own_rows = pl.ds(pl.multiple_of(me * rows, 16), rows)
        if len(refs) == 1:
            own_rows = pl.ds(0, rows)
        copies = [
            pltpu.make_async_copy(
                refs[0].at[:, pl.ds(i * FF + f * tile, tile)],
                target.at[i, own_rows, cols],
                sems.at[f, i],
            )
            for i in range(2)
        ]
        if len(refs) > 1:
            for k, rel in enumerate((1 + zpar, 2 - zpar, 3)):
                at = pl.ds(pl.multiple_of((me ^ rel) * rows, 16), rows)
                for n, (half, ref) in enumerate(((core, refs[1 + k]), (1 - core, refs[4 + k]))):
                    copies.append(
                        pltpu.make_async_copy(
                            ref.at[pl.ds(0, rows), cols],
                            target.at[half, at, cols],
                            sems.at[f, 2 + 2 * k + n],
                        )
                    )
        out.append(copies)
    return out


def down_copies(refs, target, meta, sems):
    if len(refs) == 1:
        return [pltpu.make_async_copy(refs[0], target, sems.at[0])]
    me, core, zpar = meta[0], meta[1], meta[2]
    width = refs[0].shape[1]
    rows = refs[1].shape[0]

    def columns(rel):
        return pl.ds(pl.multiple_of((me ^ rel) * width, 128), width)

    out = [pltpu.make_async_copy(refs[0], target.at[:, columns(0)], sems.at[6])]
    for k, rel in enumerate((1 + zpar, 2 - zpar, 3)):
        for which, ref in ((core, refs[1 + k]), (1 - core, refs[4 + k])):
            at = pl.ds(pl.multiple_of(which * rows, 16), rows)
            out.append(
                pltpu.make_async_copy(ref, target.at[at, columns(rel)], sems.at[len(out) - 1])
            )
    return out


def cut_body(meta, gateup_ref, proj_ref, dep_ref, gp_out, proj_out):
    rows = gateup_ref.shape[0]
    gp_out[:rows] = gateup_ref[...]
    gp_out[rows:] = jnp.zeros((GP_ROWS - rows, FF), BF)
    half = proj_ref[pl.ds(pl.multiple_of(meta[1] * (rows - PIECE), 16), PIECE), :]
    gp_out[rows:, :D] = half[:64]
    gp_out[rows:, 1024 : 1024 + D] = half[64:]
    proj_out[:, 896:] = jnp.zeros((rows, 128), BF)
    proj_out[:, :D] = proj_ref[...]


def cut_call(meta, gateup, proj, dep):
    rows = gateup.shape[0]
    return pl.pallas_call(
        cut_body,
        grid_spec=pltpu.PrefetchScalarGridSpec(
            num_scalar_prefetch=1,
            grid=(1,),
            in_specs=[
                pl.BlockSpec((rows, FF), lambda i, m: (0, m[1])),
                pl.BlockSpec(proj.shape, lambda i, m: (0, 0)),
                ANY,
            ],
            out_specs=[
                pl.BlockSpec((GP_ROWS, FF), lambda i, m: (0, 0)),
                pl.BlockSpec((rows, 1024), lambda i, m: (0, 0)),
            ],
        ),
        out_shape=[
            jax.ShapeDtypeStruct((GP_ROWS, FF), BF),
            jax.ShapeDtypeStruct((rows, 1024), BF),
        ],
        compiler_params=params(),
        cost_estimate=cost(0, 8 << 20),
        name="cut_weights",
    )(meta, gateup, proj, dep)


def rope_tile(tile, cosine, sine):
    low = (lanes() % 64) < 32
    swapped = jnp.where(low, pltpu.roll(tile, 96, 1), pltpu.roll(tile, 32, 1))
    return tile * cosine + swapped * sine


def first_norm_body(x_ref, cot_ref, *refs):
    x_out, cot_out, scaled_ref = refs[-3:]
    x = transposed(x_ref[...])
    x_out[...] = x
    cot_out[...] = transposed(cot_ref[...])
    x = x.astype(F32)
    scale = lax.rsqrt(jnp.mean(x * x, axis=1, keepdims=True) + NORM_EPSILON)
    scaled_ref[...] = x * scale


def first_norm_call(x, cot, deps):
    tokens = x.shape[1]
    return pl.pallas_call(
        first_norm_body,
        in_specs=[WHOLE] * 2 + [ANY] * len(deps),
        out_specs=[WHOLE] * 3,
        out_shape=[jax.ShapeDtypeStruct((tokens, D), BF)] * 2
        + [jax.ShapeDtypeStruct((tokens, D), F32)],
        compiler_params=params(),
        cost_estimate=cost(0, 5 << 20),
        name="first_norm",
    )(x, cot, *deps)


def kv_body(nw, meta, scaled_ref, gain_ref, cos_ref, sin_ref, *refs):
    w_refs = refs[:nw]
    n_ref, gains_out, kv_ref, w_scr, j_scr, g_scr, sems, gsems = refs[nw:]
    plan = qkv_plan(w_refs, w_scr, meta, sems)
    if nw > 1:
        gain_copies = [
            pltpu.make_async_copy(
                w_refs[1 + k].at[pl.ds(PIECE, 16), pl.ds(0, 256)], g_scr.at[k], gsems.at[k]
            )
            for k in range(3)
        ]
        start_all(gain_copies)
        plan_start(plan, meta)
        wait_all(gain_copies)
        me, zpar = meta[0], meta[2]
        own = gain_ref[...].astype(F32)
        width = own.shape[1]
        for b in range(D // width):
            value = own
            for k, rel in enumerate((1 + zpar, 2 - zpar, 3)):
                value = jnp.where((me ^ rel) == b, g_scr[k][:2, :width].astype(F32), value)
            gains_out[:2, b * width : (b + 1) * width] = value
    else:
        plan_start(plan, meta)
        gains_out[:2] = gain_ref[...].astype(F32)
    gains_out[2:] = jnp.zeros((6, D), F32)
    n_ref[...] = (scaled_ref[...] * gains_out[0:1, :]).astype(BF)
    plan_wait(plan, meta)
    tokens = n_ref.shape[0]
    j_scr[...] = jnp.dot(n_ref[...], w_scr[:, 896:QKV], preferred_element_type=F32)
    lane = lanes()
    cosine = cos_ref[...]
    sine = sin_ref[...]
    keys = {}
    for t in range(7, 10):
        at = 128 * (t - 7)
        tile = rope_tile(j_scr[:, at : at + 128], cosine, sine)
        for half in range(2):
            if 2 * t + half >= HEADS:
                keys[2 * t + half - HEADS] = tile if half == 0 else pltpu.roll(tile, 64, 1)
    for g in range(KV_HEADS):
        t = 10 + g // 2
        if t == 12:
            last = j_scr[:, 640:704]
            value = jnp.concatenate([last, last], axis=1)
        else:
            value = j_scr[:, 128 * (t - 7) : 128 * (t - 6)]
            if g % 2 == 0:
                value = pltpu.roll(value, 64, 1)
        both = jnp.where(lane < 64, keys[g], value).astype(BF)
        kv_ref[:tokens, 128 * g : 128 * (g + 1)] = both
        key = jnp.where(lane < 64, both.astype(F32), 0.0)
        top = jnp.max(jnp.sum(key * key, axis=1, keepdims=True), axis=0, keepdims=True)
        kv_ref[tokens:, 128 * g : 128 * (g + 1)] = jnp.broadcast_to(
            top * 1.02, (NORM_ROWS, 128)
        ).astype(BF)


def kv_call(meta, scaled, gain, cosine, sine, weights):
    tokens = scaled.shape[0]
    nw = len(weights)
    return pl.pallas_call(
        functools.partial(kv_body, nw),
        in_specs=[SCALARS] + [WHOLE] * 4 + [ANY] * nw,
        out_specs=[WHOLE] * 3,
        out_shape=[
            jax.ShapeDtypeStruct((tokens, D), BF),
            jax.ShapeDtypeStruct((8, D), F32),
            jax.ShapeDtypeStruct((tokens + NORM_ROWS, KV_HEADS * 128), BF),
        ],
        scratch_shapes=[
            pltpu.VMEM((D, QKV), BF),
            pltpu.VMEM((tokens, QKV - 896), F32),
            pltpu.VMEM((3, 16, 256), BF),
            pltpu.SemaphoreType.DMA((8,)),
            pltpu.SemaphoreType.DMA((3,)),
        ],
        compiler_params=params(),
        cost_estimate=cost(2 * tokens * D * 704, 6 << 20),
        name="kv_project",
    )(meta, scaled, gain, cosine, sine, *weights)


def q_body(nw, meta, n_ref, cos_ref, sin_ref, *refs):
    w_refs = refs[:nw]
    q_ref, qn_ref, w_scr, j_scr, sems = refs[nw:]
    plan = qkv_plan(w_refs, w_scr, meta, sems)
    plan_start(plan, meta)
    plan_wait(plan, meta)
    tokens = n_ref.shape[0]
    j_scr[...] = jnp.dot(n_ref[...], w_scr[:, :1024], preferred_element_type=F32)
    lane = lanes()
    cosine = cos_ref[...]
    sine = sin_ref[...]
    top_q = jnp.zeros((tokens, 1), F32)
    for t in range(8):
        tile = rope_tile(j_scr[:, 128 * t : 128 * (t + 1)], cosine, sine)
        for half in range(2):
            head = 2 * t + half
            if head >= HEADS:
                continue
            part = tile if half == 0 else pltpu.roll(tile, 64, 1)
            part = jnp.where(lane < 64, part * (LOG2E * 0.125), 0.0).astype(BF)
            q_ref[head] = part
            part = part.astype(F32)
            top_q = jnp.maximum(top_q, jnp.sum(part * part, axis=1, keepdims=True))
    qn_ref[...] = jnp.broadcast_to(jnp.max(top_q, axis=0, keepdims=True) * 1.02, (8, 128))


def q_call(meta, n1, cosine, sine, weights):
    tokens = n1.shape[0]
    nw = len(weights)
    return pl.pallas_call(
        functools.partial(q_body, nw),
        in_specs=[SCALARS] + [WHOLE] * 3 + [ANY] * nw,
        out_specs=[WHOLE] * 2,
        out_shape=[
            jax.ShapeDtypeStruct((HEADS, tokens, 128), BF),
            jax.ShapeDtypeStruct((8, 128), F32),
        ],
        scratch_shapes=[
            pltpu.VMEM((D, QKV), BF),
            pltpu.VMEM((tokens, 1024), F32),
            pltpu.SemaphoreType.DMA((8,)),
        ],
        compiler_params=params(),
        cost_estimate=cost(2 * tokens * D * 1024, 8 << 20),
        name="q_project",
    )(meta, n1, cosine, sine, *weights)


def load_rows(shards, tokens, me, pieces, kv_scr, sem, nrm_scr=None, nsem=None):
    copies = []
    for j in range(shards):
        row = pl.multiple_of((me ^ j) * tokens, tokens)
        for h in range(KV_HEADS):
            copies.append(
                pltpu.make_async_copy(
                    pieces[j].at[pl.ds(0, tokens), pl.ds(h * 128, 128)],
                    kv_scr.at[h, pl.ds(row, tokens), :],
                    sem.at[j, h],
                )
            )
        if nrm_scr is not None:
            copies.append(
                pltpu.make_async_copy(
                    pieces[j].at[pl.ds(tokens, NORM_ROWS), :], nrm_scr.at[j], nsem.at[j]
                )
            )
    start_all(copies)
    wait_all(copies)


def pair_range(meta, c):
    t_lo = meta[4 + 2 * c]
    t_hi = meta[5 + 2 * c]
    odd = (t_hi - t_lo) & 1
    start = jnp.where((odd == 1) & (t_lo > 0), t_lo - 1, t_lo)
    return start, (t_hi - t_lo + odd) // 2


def attend_forward_body(shards, tokens, meta, q_ref, qm_ref, qn_ref, aug_ref, *refs):
    o_ref, q2_ref, kv_scr, acc_scr, m_scr, nrm_scr, sem, nsem = refs[-8:]
    g = pl.program_id(0)
    c = pl.program_id(1)

    @pl.when((g == 0) & (c == 0))
    def _():
        load_rows(shards, tokens, meta[0], refs[:shards], kv_scr, sem, nrm_scr, nsem)

    lane = lanes()
    qm = qm_ref[...]
    rows_all = GROUP * QC
    acc_scr[...] = jnp.zeros_like(acc_scr)
    q2_ref[...] = jnp.where(lane < 64, q_ref[...], qm[None])
    safe = jnp.max(qn_ref[...]) * jnp.max(nrm_scr[...].astype(F32)) < SAFE * SAFE
    start, pairs = pair_range(meta, c)

    def tiles(u):
        rows = pl.ds(pl.multiple_of((start + 2 * u) * KT, KT), 2 * KT)
        kv = kv_scr[g, rows, :]
        return (
            jnp.where(lane < 64, kv, aug_ref[rows, :]),
            jnp.where(lane < 64, jnp.ones_like(kv), kv),
        )

    @pl.when(safe)
    def _():
        def step(u, carry):
            keys, values = tiles(u)
            scores = lax.dot_general(
                q2_ref[...].reshape(rows_all, 128), keys, NT, preferred_element_type=F32
            )
            weights = jnp.exp2(scores).astype(BF)
            acc_scr[...] += jnp.dot(weights, values, preferred_element_type=F32)
            return carry

        lax.fori_loop(0, pairs, step, 0)
        m_scr[...] = jnp.zeros_like(m_scr)

    @pl.when(jnp.logical_not(safe))
    def _():
        m_scr[...] = jnp.full_like(m_scr, -1e30)

        def step(u, carry):
            keys, values = tiles(u)

            def head(h, carry):
                scores = lax.dot_general(q2_ref[h], keys, NT, preferred_element_type=F32)
                rows = pl.ds(pl.multiple_of(h * QC, QC), QC)
                old = m_scr[rows, :1]
                new = jnp.maximum(old, jnp.max(scores, axis=1, keepdims=True))
                weights = jnp.exp2(scores - new).astype(BF)
                acc_scr[rows, :] = acc_scr[rows, :] * jnp.exp2(old - new) + jnp.dot(
                    weights, values, preferred_element_type=F32
                )
                m_scr[rows, :] = jnp.broadcast_to(new, (QC, 128))
                return carry

            return lax.fori_loop(0, GROUP, head, carry)

        lax.fori_loop(0, pairs, step, 0)

    def finish(h, carry):
        rows = pl.ds(pl.multiple_of(h * QC, QC), QC)
        acc = acc_scr[rows, :]
        other = pltpu.roll(acc, 64, 1)
        o_ref[h] = jnp.where(lane < 64, 0.0, acc / jnp.where(lane < 64, 1.0, other)).astype(BF)
        total = jnp.where(lane < 64, acc, other)
        high, mid, low = split3(-(m_scr[rows, :] + jnp.log2(total)))
        with_log = jnp.where(lane == LANE_LOG + 2, low, q2_ref[h])
        with_log = jnp.where(lane == LANE_LOG + 1, mid, with_log)
        q2_ref[h] = jnp.where(lane == LANE_LOG, high, with_log)
        return carry

    lax.fori_loop(0, GROUP, finish, 0)


def attend_forward(meta, q, qm, qn, aug, kv, deps):
    tokens = q.shape[1]
    shards = len(kv)
    heads = KV_HEADS
    row = shards * tokens
    block = pl.BlockSpec((GROUP, QC, 128), lambda g, c, m: (g, c, 0))
    return pl.pallas_call(
        functools.partial(attend_forward_body, shards, tokens),
        grid_spec=pltpu.PrefetchScalarGridSpec(
            num_scalar_prefetch=1,
            grid=(heads, tokens // QC),
            in_specs=[
                pl.BlockSpec((GROUP, QC, 128), lambda g, c, m: (g, c, 0)),
                pl.BlockSpec((QC, 128), lambda g, c, m: (c, 0)),
                pl.BlockSpec((8, 128), lambda g, c, m: (0, 0)),
                pl.BlockSpec((row, 128), lambda g, c, m: (0, 0)),
            ]
            + [ANY] * (shards + len(deps)),
            out_specs=[block, block],
            scratch_shapes=[
                pltpu.VMEM((heads, row, 128), BF),
                pltpu.VMEM((GROUP * QC, 128), F32),
                pltpu.VMEM((GROUP * QC, 128), F32),
                pltpu.VMEM((shards, NORM_ROWS, heads * 128), BF),
                pltpu.SemaphoreType.DMA((shards, heads)),
                pltpu.SemaphoreType.DMA((shards,)),
            ],
        ),
        out_shape=[jax.ShapeDtypeStruct((GROUP * heads, tokens, 128), BF)] * 2,
        compiler_params=params(),
        cost_estimate=cost(16 * GROUP * heads * tokens * row * 128, 10 << 20),
        name="attend_forward",
    )(meta, q, qm, qn, aug, *kv, *deps)


def attend_backward_body(shards, tokens, meta, q_ref, do_ref, aug_ref, *refs):
    dq_ref, out_ref, kv_scr, dkv_scr, ob_scr, dq_scr, qt_scr, sem, osem = refs[-9:]
    g = pl.program_id(0)
    c = pl.program_id(1)

    @pl.when((g == 0) & (c == 0))
    def _():
        load_rows(shards, tokens, meta[0], refs[:shards], kv_scr, sem)

    @pl.when(c == 0)
    def _():
        dkv_scr[...] = jnp.zeros_like(dkv_scr)

    lane = lanes()
    rows_all = GROUP * QC
    dq_scr[...] = jnp.zeros_like(dq_scr)
    qt_scr[...] = jnp.transpose(
        jnp.where(lane < 64, q_ref[...], do_ref[...]).reshape(rows_all, 128)
    )
    start, pairs = pair_range(meta, c)

    def step(u, carry):
        tile = start + 2 * u
        rows = pl.ds(pl.multiple_of(tile * KT, KT), 2 * KT)
        kv = kv_scr[g, rows, :]
        ones = jnp.where(lane >= LANE_INNER, jnp.ones_like(kv), jnp.zeros_like(kv))
        keys = jnp.where(lane < 64, kv, aug_ref[rows, :])
        values = jnp.where(lane < 64, ones, kv)
        queries = q_ref[...].reshape(rows_all, 128)
        grads = do_ref[...].reshape(rows_all, 128)
        weights = jnp.exp2(lax.dot_general(queries, keys, NT, preferred_element_type=F32))
        inner = lax.dot_general(grads, values, NT, preferred_element_type=F32)
        grad_scores = (weights * inner).astype(BF)
        weights = weights.astype(BF)
        dq_scr[...] += jnp.dot(grad_scores, keys, preferred_element_type=F32)
        for i in range(2):
            part = slice(i * KT, (i + 1) * KT)
            dkv_scr[tile + i, :64] += jnp.dot(
                qt_scr[:64], grad_scores[:, part], preferred_element_type=F32
            )
            dkv_scr[tile + i, 64:] += jnp.dot(
                qt_scr[64:], weights[:, part], preferred_element_type=F32
            )
        return carry

    lax.fori_loop(0, pairs, step, 0)
    dq_ref[...] = dq_scr[...].reshape(GROUP, QC, 128) * 0.125

    def out_copy(group):
        at = pl.ds(pl.multiple_of(group * 128, 128), 128)
        return pltpu.make_async_copy(ob_scr, out_ref.at[:, at], osem)

    @pl.when(c == pl.num_programs(1) - 1)
    def _():
        pl.when(g > 0)(lambda: out_copy(g - 1).wait())
        for t in range(shards * tokens // KT):
            both = dkv_scr[t]
            both = jnp.concatenate([both[:64] * LN2, both[64:]], axis=0)
            ob_scr[t * KT : (t + 1) * KT, :] = jnp.transpose(both).astype(BF)
        out_copy(g).start()
        pl.when(g == KV_HEADS - 1)(lambda: out_copy(g).wait())


def attend_backward(meta, q2, do, aug, kv, deps):
    tokens = q2.shape[1]
    shards = len(kv)
    row = shards * tokens
    rows_all = GROUP * QC
    block = pl.BlockSpec((GROUP, QC, 128), lambda g, c, m: (g, c, 0))
    return pl.pallas_call(
        functools.partial(attend_backward_body, shards, tokens),
        grid_spec=pltpu.PrefetchScalarGridSpec(
            num_scalar_prefetch=1,
            grid=(KV_HEADS, tokens // QC),
            in_specs=[
                block,
                block,
                pl.BlockSpec((row, 128), lambda g, c, m: (0, 0)),
            ]
            + [ANY] * (shards + len(deps)),
            out_specs=[block, ANY],
            scratch_shapes=[
                pltpu.VMEM((KV_HEADS, row, 128), BF),
                pltpu.VMEM((row // KT, 128, KT), F32),
                pltpu.VMEM((row, 128), BF),
                pltpu.VMEM((rows_all, 128), F32),
                pltpu.VMEM((128, rows_all), BF),
                pltpu.SemaphoreType.DMA((shards, KV_HEADS)),
                pltpu.SemaphoreType.DMA(()),
            ],
        ),
        out_shape=[
            jax.ShapeDtypeStruct((HEADS, tokens, 128), F32),
            jax.ShapeDtypeStruct((row, KV_HEADS * 128), BF),
        ],
        compiler_params=params(),
        cost_estimate=cost(1, 1),
        name="attend_backward",
    )(meta, q2, do, aug, *kv, *deps)


MLP_TILE = 640


COT_ROWS = D // 2


def mix_body(meta, o_ref, n1_ref, cot_ref, mix_ref, own_ref, send_ref):
    lane = lanes()
    core = meta[1]
    for t in range(8):
        low = pltpu.roll(o_ref[2 * t].astype(F32), 64, 1)
        if t < 7:
            tile = jnp.where(lane < 64, low, o_ref[2 * t + 1].astype(F32)).astype(BF)
            mix_ref[:, 128 * t : 128 * (t + 1)] = tile
        else:
            mix_ref[:, 896:960] = low[:, :64].astype(BF)
    for n in range(2):
        rows = slice(n * COT_ROWS, (n + 1) * COT_ROWS)
        at = slice(n * 256, (n + 1) * 256)
        low, high = cot_ref[:COT_ROWS, at], cot_ref[COT_ROWS:, at]
        own_ref[rows] = jnp.where(core == 0, low, high)
        send_ref[rows] = jnp.where(core == 0, high, low)
    tokens = mix_ref.shape[0]
    width = D // 4
    for b in range(4):
        rows = block_rows(b, tokens)
        for at, ref in ((0, mix_ref), (128, n1_ref)):
            low = ref[:, b * width : b * width + PIECE]
            high = ref[:, (b + 1) * width - PIECE : (b + 1) * width]
            own_ref[rows, at : at + 128] = jnp.where(core == 0, low, high)
            send_ref[rows, at : at + 128] = jnp.where(core == 0, high, low)


def mix_call(meta, o, n1, cot_t):
    tokens = n1.shape[0]
    return pl.pallas_call(
        mix_body,
        in_specs=[SCALARS] + [WHOLE] * 3,
        out_specs=[WHOLE] * 3,
        out_shape=[jax.ShapeDtypeStruct((tokens, D), BF)]
        + [jax.ShapeDtypeStruct((2 * COT_ROWS + 4 * tokens, 256), BF)] * 2,
        compiler_params=params(),
        cost_estimate=cost(1, 1),
        name="mix_heads",
    )(meta, o, n1, cot_t)


def residual_body(nw, meta, x_ref, mix_ref, gain_ref, *refs):
    w_refs = refs[:nw]
    res_ref, n2_ref, n2b_ref, proj_scr, sems = refs[nw:]
    plan = proj_plan_of(w_refs, proj_scr, meta, sems)
    plan_start(plan, meta)
    plan_wait(plan, meta)
    residual = x_ref[...].astype(F32) + jnp.dot(
        mix_ref[...], proj_scr[:, :D], preferred_element_type=F32
    )
    res_ref[...] = residual
    scale = lax.rsqrt(jnp.mean(residual * residual, axis=1, keepdims=True) + NORM_EPSILON)
    n2_ref[...] = (residual * scale * gain_ref[1:2, :]).astype(BF)
    tokens = x_ref.shape[0]
    width = D // 4
    for b in range(4):
        rows = slice(b * tokens, (b + 1) * tokens)
        n2b_ref[rows, 128:256] = jnp.zeros((tokens, 128), BF)
        n2b_ref[rows, :width] = n2_ref[:, b * width : (b + 1) * width]


def residual_call(meta, x, mixed, gains, proj):
    tokens = x.shape[0]
    nw = len(proj)
    return pl.pallas_call(
        functools.partial(residual_body, nw),
        in_specs=[SCALARS] + [WHOLE] * 3 + [ANY] * nw,
        out_specs=[WHOLE] * 3,
        out_shape=[
            jax.ShapeDtypeStruct((tokens, D), F32),
            jax.ShapeDtypeStruct((tokens, D), BF),
            jax.ShapeDtypeStruct((4 * tokens, 256), BF),
        ],
        scratch_shapes=[pltpu.VMEM((D, 1024), BF), pltpu.SemaphoreType.DMA((13,))],
        compiler_params=params(),
        cost_estimate=cost(1, 1),
        name="residual",
    )(meta, x, mixed, gains, *proj)


def mlp_body(counts, meta, res_ref, n2_ref, cot_ref, *refs):
    n_gu, n_down = counts
    gu_refs = refs[:n_gu]
    down_refs = refs[n_gu : n_gu + n_down]
    (
        out_ref,
        dn_scr,
        act_ref,
        late_own_ref,
        late_send_ref,
        gu_scr,
        down_scr,
        acc_scr,
        act_scr,
        dgu_scr,
        gu_sems,
        down_sems,
        out_sems,
    ) = refs[n_gu + n_down :]
    down_plan = down_copies(down_refs, down_scr, meta, down_sems)
    gu_copies = gateup_copies(gu_refs, gu_scr, meta, gu_sems, MLP_TILE)
    start_all(gu_copies[0])
    start_all(down_plan)
    for one in gu_copies[1:]:
        start_all(one)
    tiles = FF // MLP_TILE
    core = meta[1]
    out_copies = []
    for f in range(tiles):
        cols = slice(f * MLP_TILE, (f + 1) * MLP_TILE)
        wait_all(gu_copies[f])
        normed = n2_ref[...]
        gate = jnp.dot(normed, gu_scr[0, :, cols], preferred_element_type=F32)
        up = jnp.dot(normed, gu_scr[1, :, cols], preferred_element_type=F32)
        if f == 0:
            wait_all(down_plan)
        grad_act = jnp.dot(cot_ref[...], down_scr[:, cols], preferred_element_type=F32)
        gated = 1.0 / (1.0 + jnp.exp(-gate))
        silu = gate * gated
        act = (silu * up).astype(BF)
        grad_gate = (grad_act * up * gated * (1.0 + gate * (1.0 - gated))).astype(BF)
        grad_up = (grad_act * silu).astype(BF)
        act_scr[f] = act
        dgu_scr[0, :, cols] = grad_gate
        dgu_scr[1, :, cols] = grad_up
        add_out = lax.dot_general(act, down_scr[:, cols], NT, preferred_element_type=F32)
        add_dn = lax.dot_general(
            grad_gate, gu_scr[0, :, cols], NT, preferred_element_type=F32
        ) + lax.dot_general(grad_up, gu_scr[1, :, cols], NT, preferred_element_type=F32)
        if f == 0:
            acc_scr[...] = add_out
            dn_scr[...] = add_dn
        else:
            acc_scr[...] += add_out
            dn_scr[...] += add_dn
        copies = [pltpu.make_async_copy(act_scr.at[f], act_ref.at[f], out_sems.at[f, 0])]
        for i, ref in enumerate((late_own_ref, late_send_ref)):
            copies.append(
                pltpu.make_async_copy(
                    dgu_scr.at[core if i == 0 else 1 - core, :, pl.ds(f * MLP_TILE, MLP_TILE)],
                    ref.at[:, pl.ds(f * MLP_TILE, MLP_TILE)],
                    out_sems.at[f, 2 + i],
                )
            )
        start_all(copies)
        out_copies += copies
    out_ref[...] = transposed_back((res_ref[...] + acc_scr[...]).astype(BF))
    wait_all(out_copies)


def norm_back_body(nw, meta, res_ref, dn_ref, cot_ref, mix_ref, gain_ref, *refs):
    proj_refs = refs[:nw]
    gres_ref, gb_ref, do_ref, gain_out_ref, proj_scr, dn_scr, sems = refs[-7:]
    proj_plan = proj_plan_of(proj_refs, proj_scr, meta, sems)
    plan_start(proj_plan, meta)
    lane = lanes()
    gain = gain_ref[1:2, :]
    residual = res_ref[...]
    scale = lax.rsqrt(jnp.mean(residual * residual, axis=1, keepdims=True) + NORM_EPSILON)
    grad = dn_ref[...]
    gain_out_ref[...] = jnp.broadcast_to(
        jnp.sum(grad * residual * scale, axis=0, keepdims=True), (8, D)
    )
    scaled = grad * gain
    mean = jnp.mean(scaled * residual, axis=1, keepdims=True)
    grad_residual = (
        cot_ref[...].astype(F32) + scale * scaled - residual * (scale * scale * scale * mean)
    )
    gres_ref[...] = grad_residual
    branch = grad_residual.astype(BF)
    gb_ref[:, :D] = branch
    gb_ref[:, D:] = jnp.zeros((branch.shape[0], 1024 - D), BF)
    plan_wait(proj_plan, meta)
    dn_scr[...] = lax.dot_general(
        gb_ref[:, :D], proj_scr[:, :D], NT, preferred_element_type=F32
    )
    ones = (
        (lax.broadcasted_iota(jnp.int32, (128, 128), 0) < 64)
        == (lax.broadcasted_iota(jnp.int32, (128, 128), 1) < 64)
    ).astype(BF)
    half_lane = lane % 64
    for t in range(8):
        if t < 7:
            gm = dn_scr[:, 128 * t : 128 * (t + 1)].astype(BF)
            mixed = mix_ref[:, 128 * t : 128 * (t + 1)]
        else:
            gm = dn_scr[:, 896:960].astype(BF)
            gm = jnp.concatenate([gm, jnp.zeros_like(gm)], axis=1)
            mixed = mix_ref[:, 896:960]
            mixed = jnp.concatenate([mixed, jnp.zeros_like(mixed)], axis=1)
        gm = gm.astype(F32)
        product = gm * mixed.astype(F32)
        high = product.astype(BF)
        low = (product - high.astype(F32)).astype(BF)
        inner = jnp.dot(high, ones, preferred_element_type=F32) + jnp.dot(
            low, ones, preferred_element_type=F32
        )
        high, mid, low = split3(-inner)
        extra = jnp.where(half_lane == LANE_INNER + 2, low.astype(F32), 0.0)
        extra = jnp.where(half_lane == LANE_INNER + 1, mid.astype(F32), extra)
        extra = jnp.where(half_lane == LANE_INNER, high.astype(F32), extra)
        do_ref[2 * t] = jnp.where(lane < 64, extra, pltpu.roll(gm, 64, 1)).astype(BF)
        if 2 * t + 1 < HEADS:
            do_ref[2 * t + 1] = jnp.where(lane < 64, pltpu.roll(extra, 64, 1), gm).astype(BF)


def norm_back_call(meta, residual, dn, cot, mixed, gains, proj, deps):
    tokens = cot.shape[0]
    nw = len(proj)
    return pl.pallas_call(
        functools.partial(norm_back_body, nw),
        in_specs=[SCALARS] + [WHOLE] * 5 + [ANY] * (nw + len(deps)),
        out_specs=[WHOLE] * 4,
        out_shape=[
            jax.ShapeDtypeStruct((tokens, D), F32),
            jax.ShapeDtypeStruct((tokens, 1024), BF),
            jax.ShapeDtypeStruct((HEADS, tokens, 128), BF),
            jax.ShapeDtypeStruct((8, D), F32),
        ],
        scratch_shapes=[
            pltpu.VMEM((D, 1024), BF),
            pltpu.VMEM((tokens, D), F32),
            pltpu.SemaphoreType.DMA((13,)),
        ],
        compiler_params=params(),
        cost_estimate=cost(2 * tokens * D * D, 12 << 20),
        name="norm_backward",
    )(meta, residual, dn, cot, mixed, gains, *proj, *deps)


def mlp_call(meta, residual, n2, cot, gateup, down):
    tokens = n2.shape[0]
    counts = (len(gateup), len(down))
    tiles = FF // MLP_TILE
    return pl.pallas_call(
        functools.partial(mlp_body, counts),
        in_specs=[SCALARS] + [WHOLE] * 3 + [ANY] * sum(counts),
        out_specs=[WHOLE] * 2 + [ANY] * 3,
        out_shape=[
            jax.ShapeDtypeStruct((D, tokens), BF),
            jax.ShapeDtypeStruct((tokens, D), F32),
            jax.ShapeDtypeStruct((tiles, tokens, MLP_TILE), BF),
            jax.ShapeDtypeStruct((tokens, FF), BF),
            jax.ShapeDtypeStruct((tokens, FF), BF),
        ],
        scratch_shapes=[
            pltpu.VMEM((2, D, FF), BF),
            pltpu.VMEM((D, FF), BF),
            pltpu.VMEM((tokens, D), F32),
            pltpu.VMEM((tiles, tokens, MLP_TILE), BF),
            pltpu.VMEM((2, tokens, FF), BF),
            pltpu.SemaphoreType.DMA((tiles, 8)),
            pltpu.SemaphoreType.DMA((8,)),
            pltpu.SemaphoreType.DMA((tiles, 4)),
        ],
        compiler_params=params(),
        cost_estimate=cost(2 * tokens * D * (6 * FF), 40 << 20),
        name="feed_forward",
    )(meta, residual, n2, cot, *gateup, *down)


def joined_body(
    nw, shards, meta, dq_ref, cos_ref, sin_ref, x_ref, gain_ref, gres_ref, gain_two_ref, *refs
):
    dkv_ref = refs[0]
    w_refs = refs[1 : 1 + nw]
    gj_ref, ig_ref, w_scr, g_scr, sems = refs[-5:]
    plan = qkv_plan(w_refs, w_scr, meta, sems)
    tokens = x_ref.shape[0]
    plan_start(plan, meta)
    lane = lanes()
    cosine = cos_ref[...]
    sine = -sin_ref[...]
    heads = {}

    def dkv(g):
        if g not in heads:
            at = slice(128 * g, 128 * (g + 1))
            total = dkv_ref[:tokens, at].astype(F32)
            for j in range(1, shards):
                total = total + dkv_ref[j * tokens : (j + 1) * tokens, at].astype(F32)
            heads[g] = (total, pltpu.roll(total, 64, 1))
        return heads[g]

    def dq(h):
        return dq_ref[h]

    def low_half(h):
        if h < HEADS:
            return dq(h)
        if h < HEADS + KV_HEADS:
            return dkv(h - HEADS)[0]
        return dkv(h - HEADS - KV_HEADS)[1]

    def high_half(h):
        if h < HEADS:
            return pltpu.roll(dq(h), 64, 1)
        if h < HEADS + KV_HEADS:
            return dkv(h - HEADS)[1]
        return dkv(h - HEADS - KV_HEADS)[0]

    for t in range(13):
        if t == 12:
            last = jnp.where(lane < 64, low_half(24), 0.0).astype(BF)
            gj_ref[:tokens, 1536:1664] = last
            continue
        tile = jnp.where(lane < 64, low_half(2 * t), high_half(2 * t + 1))
        if t < 10:
            tile = rope_tile(tile, cosine, sine)
        gj_ref[:tokens, 128 * t : 128 * (t + 1)] = tile.astype(BF)
    plan_wait(plan, meta)
    g_scr[...] = lax.dot_general(
        gj_ref[:tokens, :QKV], w_scr[...], NT, preferred_element_type=F32
    )
    grad = g_scr[...]
    x = x_ref[...].astype(F32)
    scale = lax.rsqrt(jnp.mean(x * x, axis=1, keepdims=True) + NORM_EPSILON)
    gj_ref[tokens:, :] = jnp.zeros((16, gj_ref.shape[1]), BF)
    gain_one = jnp.sum(grad * x * scale, axis=0, keepdims=True)
    gj_ref[tokens : tokens + 2, :D] = jnp.concatenate(
        [gain_one, gain_two_ref[:1]], axis=0
    ).astype(BF)
    scaled = grad * gain_ref[0:1, :]
    mean = jnp.mean(scaled * x, axis=1, keepdims=True)
    ig_ref[...] = transposed_back(
        gres_ref[...] + scale * scaled - x * (scale * scale * scale * mean)
    )


def joined_call(meta, dq, cosine, sine, x, gains, gres, gain_two, dkv, weights, deps):
    tokens = x.shape[0]
    nw = len(weights)
    shards = dkv.shape[0] // tokens
    return pl.pallas_call(
        functools.partial(joined_body, nw, shards),
        in_specs=[SCALARS] + [WHOLE] * 8 + [ANY] * (nw + len(deps)),
        out_specs=[WHOLE] * 2,
        out_shape=[
            jax.ShapeDtypeStruct((tokens + 16, 1664), BF),
            jax.ShapeDtypeStruct((D, tokens), F32),
        ],
        scratch_shapes=[
            pltpu.VMEM((D, QKV), BF),
            pltpu.VMEM((tokens, D), F32),
            pltpu.SemaphoreType.DMA((8,)),
        ],
        compiler_params=params(),
        cost_estimate=cost(2 * tokens * D * QKV, 16 << 20),
        name="joined_backward",
    )(meta, dq, cosine, sine, x, gains, gres, gain_two, dkv, *weights, *deps)


def block_rows(block, tokens):
    return slice(2 * COT_ROWS + block * tokens, 2 * COT_ROWS + (block + 1) * tokens)


def gateup_grad_body(meta, own_ref, oth_ref, b_own, b_oth, *refs):
    out = refs[-1]
    tokens = b_own.shape[0]
    width = D // 4
    for j in range(4):
        rows = slice(j * tokens, (j + 1) * tokens)
        total = lax.dot_general(
            own_ref[rows, 0:256], b_own[...], TN, preferred_element_type=F32
        ) + lax.dot_general(oth_ref[rows, 0:256], b_oth[...], TN, preferred_element_type=F32)
        out[j * width : (j + 1) * width] = total[:width].astype(BF)


def gateup_grad_call(meta, n2_own, n2_oth, late_own, late_oth, deps):
    tokens = late_own.shape[0]
    tile = 640
    whole = pl.BlockSpec(n2_own.shape, lambda i, s: (0, 0))
    cols = pl.BlockSpec((tokens, tile), lambda i, s: (0, i))
    return pl.pallas_call(
        gateup_grad_body,
        grid_spec=pltpu.PrefetchScalarGridSpec(
            num_scalar_prefetch=1,
            grid=(FF // tile,),
            in_specs=[whole] * 2 + [cols] * 2 + [ANY] * len(deps),
            out_specs=pl.BlockSpec((D, tile), lambda i, s: (0, i)),
        ),
        out_shape=jax.ShapeDtypeStruct((D, FF), BF),
        compiler_params=params(),
        cost_estimate=cost(4 * tokens * D * FF, 20 << 20),
        name="gateup_gradient",
    )(meta, n2_own, n2_oth, late_own, late_oth, *deps)


DP_ROWS = COT_ROWS + 2 * PIECE


def down_proj_grad_body(meta, own_ref, oth_ref, act_own, act_oth, gb_own, gb_oth, *refs):
    tokens = gb_own.shape[0]
    for block in range(4):
        out = refs[-1].at[pl.ds(block * DP_ROWS, DP_ROWS)]
        total = None
        for cot_rows, act_ref in ((own_ref, act_own), (oth_ref, act_oth)):
            for n in range(2):
                term = jnp.dot(
                    cot_rows[n * COT_ROWS : (n + 1) * COT_ROWS],
                    act_ref[block, n * 256 : (n + 1) * 256],
                    preferred_element_type=F32,
                )
                total = term if total is None else total + term
        out[:COT_ROWS] = total.astype(BF)
        rows = block_rows(block, tokens)
        total = lax.dot_general(
            own_ref[rows, 0:128], gb_own[...], TN, preferred_element_type=F32
        ) + lax.dot_general(oth_ref[rows, 0:128], gb_oth[...], TN, preferred_element_type=F32)
        total = total.astype(BF)
        out[COT_ROWS : COT_ROWS + PIECE] = total[:, :640]
        out[COT_ROWS + PIECE :, :384] = total[:, 640:]
        out[COT_ROWS + PIECE :, 384:] = jnp.zeros((PIECE, 256), BF)


def down_proj_grad_call(meta, early_own, early_oth, act_own, act_oth, gb_own, gb_oth, deps):
    blocks, tokens, width = act_own.shape
    return pl.pallas_call(
        down_proj_grad_body,
        in_specs=[SCALARS] + [WHOLE] * 6 + [ANY] * len(deps),
        out_specs=WHOLE,
        out_shape=jax.ShapeDtypeStruct((4 * DP_ROWS, width), BF),
        compiler_params=params(),
        cost_estimate=cost(2 * tokens * D * (FF + D), 16 << 20),
        name="down_proj_gradient",
    )(meta, early_own, early_oth, act_own, act_oth, gb_own, gb_oth, *deps)


def qkv_grad_body(meta, own_ref, oth_ref, gj_own, gj_oth, *refs):
    tokens = gj_own.shape[0] - 16
    width = D // 4
    sums = (
        gj_own[tokens : tokens + 16, :].astype(F32) + gj_oth[tokens : tokens + 16, :].astype(F32)
    ).astype(BF)
    for block in range(4):
        rows = block_rows(block, tokens)
        total = lax.dot_general(
            own_ref[rows, 128:256], gj_own[:tokens, :], TN, preferred_element_type=F32
        ) + lax.dot_general(
            oth_ref[rows, 128:256], gj_oth[:tokens, :], TN, preferred_element_type=F32
        )
        total = total[:, :QKV]
        part = sums[:, block * width : (block + 1) * width]
        total = jnp.where(meta[1] == 0, total[:120], total[8:])
        part = jnp.concatenate([part[:8], jnp.zeros((8, QKV - width), BF)], axis=1)
        for j, out in enumerate(refs[-4:]):

            @pl.when((meta[0] ^ j) == block)
            def _(out=out, total=total, part=part):
                out[:120] = total.astype(BF)
                out[120:] = part


def qkv_grad_call(meta, early_own, early_oth, gj_own, gj_oth, deps):
    return pl.pallas_call(
        qkv_grad_body,
        in_specs=[SCALARS] + [WHOLE] * 4 + [ANY] * len(deps),
        out_specs=[WHOLE] * 4,
        out_shape=[jax.ShapeDtypeStruct((GRAD_ROWS, QKV), BF)] * 4,
        compiler_params=params(),
        cost_estimate=cost(2 * gj_own.shape[0] * D * QKV, 8 << 20),
        name="qkv_gradient",
    )(meta, early_own, early_oth, gj_own, gj_oth, *deps)


def total_of(refs, blocks=1):
    total = None
    for ref in refs:
        rows = ref.shape[0] // blocks
        for i in range(blocks):
            term = ref[i * rows : (i + 1) * rows].astype(F32)
            total = term if total is None else total + term
    return total.astype(BF)


def cut_along(value, axis, parts):
    size = value.shape[axis] // parts
    if axis == 0:
        return [value[i * size : (i + 1) * size] for i in range(parts)]
    return [value[:, i * size : (i + 1) * size] for i in range(parts)]


def add_job(inputs, blocks=1):
    rows, columns = inputs[0].shape

    def body(meta, ins, outs):
        outs[0][...] = total_of(ins, blocks)

    return inputs, [(rows // blocks, columns)], body


def copy_job(value):
    def body(meta, ins, outs):
        outs[0][...] = ins[0][...]

    return [value], [value.shape], body


def rows_job(value, rows):
    def body(meta, ins, outs):
        at = pl.multiple_of(meta[1] * rows, 16)
        outs[0][...] = ins[0][pl.ds(at, rows), :]

    return [value], [(rows, value.shape[1])], body


def split_job(inputs, axis, at, blocks=1):
    shape = list(inputs[0].shape)
    shape[0] //= blocks
    shape[axis] //= 2

    def body(meta, ins, outs):
        low, high = cut_along(total_of(ins, blocks), axis, 2)
        bit = meta[at]
        outs[0][...] = jnp.where(bit == 0, low, high)
        outs[1][...] = jnp.where(bit == 0, high, low)

    return inputs, [tuple(shape)] * 2, body


def join_job(mine, theirs, axis, at):
    shape = list(mine.shape)
    shape[axis] *= 2

    def body(meta, ins, outs):
        bit = meta[at]
        a, b = ins[0][...], ins[1][...]
        low, high = jnp.where(bit == 0, a, b), jnp.where(bit == 0, b, a)
        size = a.shape[axis]
        if axis == 0:
            outs[0][:size] = low
            outs[0][size:] = high
        else:
            outs[0][:, :size] = low
            outs[0][:, size:] = high

    return [mine, theirs], [tuple(shape)], body


def whole_job(inputs):
    rows, columns = inputs[0].shape

    def body(meta, ins, outs):
        place = meta[2] + 2 * meta[3]
        for i in range(4):
            back = (place + 4 - i) % 4
            value = ins[3][...]
            for k in range(3):
                value = jnp.where(back == k, ins[k][...], value)
            outs[0][i * rows : (i + 1) * rows] = value

    return inputs, [(4 * rows, columns)], body


def stage_body(jobs, meta, *refs):
    outs = refs[-sum(len(job[1]) for job in jobs) :]
    at_in = at_out = 0
    for ins, shapes, body in jobs:
        body(meta, refs[at_in : at_in + len(ins)], outs[at_out : at_out + len(shapes)])
        at_in += len(ins)
        at_out += len(shapes)


def stage(name, meta, jobs, deps):
    inputs = [one for job in jobs for one in job[0]]
    shapes = [shape for job in jobs for shape in job[1]]
    results = pl.pallas_call(
        functools.partial(stage_body, jobs),
        in_specs=[SCALARS] + [WHOLE] * len(inputs) + [ANY] * len(deps),
        out_specs=[WHOLE] * len(shapes),
        out_shape=[jax.ShapeDtypeStruct(shape, BF) for shape in shapes],
        compiler_params=params(),
        cost_estimate=cost(0, 8 << 20),
        name=name,
    )(meta, *inputs, *deps)
    grouped, at = [], 0
    for job in jobs:
        grouped.append(list(results[at : at + len(job[1])]))
        at += len(job[1])
    return grouped


def adamw_step(grad_sum, master, first, second, rate, decay):
    first_new = BETA_FIRST * first + (1.0 - BETA_FIRST) * grad_sum
    second_new = BETA_SECOND * second + (1.0 - BETA_SECOND) * grad_sum * grad_sum
    corrected = (
        first_new
        / (1.0 - BETA_FIRST**STEP)
        / (jnp.sqrt(second_new / (1.0 - BETA_SECOND**STEP)) + ADAM_EPSILON)
    )
    master_new = master - rate * (corrected + decay * master)
    return (master_new, master_new.astype(jnp.bfloat16), first_new, second_new)


def pick_core(meta, half, mine, other):
    return jnp.where(meta[1] == half, mine, other).astype(F32)


def gateup_grads(meta, step, mine, other):
    halves = [pick_core(meta, half, mine[...], other[...]) for half in range(2)]
    return jnp.concatenate(halves, axis=1)


def down_grads(meta, step, mine, other):
    return pick_core(meta, step // 2, mine[...], other[...])


def proj_grads(meta, step, mine, other):
    def piece(half):
        top = pick_core(meta, half, mine[COT_ROWS : COT_ROWS + PIECE], other[COT_ROWS : COT_ROWS + PIECE])
        rest = pick_core(meta, half, mine[COT_ROWS + PIECE :], other[COT_ROWS + PIECE :])
        return jnp.concatenate([top, rest], axis=1)[:, :D]

    return jnp.where(step == 0, piece(0)[:120], piece(1)[8:])


def qkv_grads(meta, step, mine, other):
    low = pick_core(meta, 0, mine[...], other[...])[:120]
    high = pick_core(meta, 1, mine[...], other[...])[:120]
    return jnp.where(step == 0, low, high)


def adamw_body(grads_of, rate, meta, mine, other, master, first, second, *refs):
    grad_out, master_out, copy_out, first_out, second_out = refs[-5:]
    grad = grads_of(meta, pl.program_id(0), mine, other)
    grad_out[...] = grad
    new = adamw_step(grad, master[...], first[...], second[...], rate, DECAY_RATE)
    master_out[...], copy_out[...], first_out[...], second_out[...] = new


def adamw_call(meta, grads_of, pair, pair_spec, states, block, spec, steps, rate, name, deps):
    shape = states[0].shape
    own = pl.BlockSpec(block, spec)
    types = (F32, F32, BF, F32, F32)
    return pl.pallas_call(
        functools.partial(adamw_body, grads_of, rate),
        grid_spec=pltpu.PrefetchScalarGridSpec(
            num_scalar_prefetch=1,
            grid=(steps,),
            in_specs=[pair_spec] * 2 + [own] * 3 + [ANY] * len(deps),
            out_specs=[own] * 5,
        ),
        out_shape=[jax.ShapeDtypeStruct(shape, one) for one in types],
        compiler_params=params(),
        cost_estimate=cost(0, 34 * shape[0] * shape[1]),
        name=name,
    )(meta, *pair, *states, *deps)


def row_tables(doc_lengths, row, offset, tokens):
    ends = jnp.cumsum(doc_lengths, dtype=jnp.int32)
    starts = ends - doc_lengths
    blocks = (doc_lengths + BLOCK - 1) // BLOCK
    bases = jnp.cumsum(blocks, dtype=jnp.int32) - blocks
    places = jnp.arange(row, dtype=jnp.int32)
    inside = (places[:, None] >= starts[None, :]) & (places[:, None] < ends[None, :])

    def pick(values):
        return jnp.sum(jnp.where(inside, values[None, :], 0), axis=1, dtype=jnp.int32)

    doc_start, doc_end, base = pick(starts), pick(ends), pick(bases)
    position = places - doc_start
    segment = base + position // BLOCK
    reach = jnp.minimum(doc_end, doc_start + BLOCK * (position // BLOCK + 1))
    lane = jnp.arange(128, dtype=jnp.int32)
    aug = ((lane[None, :] == segment[:, None] + 64) | (lane[None, :] >= LANE_LOG)).astype(BF)

    def own(values):
        return lax.dynamic_slice_in_dim(values, offset, tokens)

    doc_start, reach, base, segment = own(doc_start), own(reach), own(base), own(segment)
    seen = (lane[None, :] >= base[:, None] + 64) & (lane[None, :] <= segment[:, None] + 64)
    open_lane = seen | (lane[None, :] >= LANE_LOG) | (lane[None, :] < 64)
    qmask = jnp.where(open_lane, 0.0, -1e30).astype(BF)
    chunks = tokens // QC
    low = jnp.min(doc_start.reshape(chunks, QC), axis=1) // KT
    high = (jnp.max(reach.reshape(chunks, QC), axis=1) + KT - 1) // KT
    ranges = jnp.stack([low, high], axis=1).reshape(-1).astype(jnp.int32)
    half = HEAD_DIM // 2
    frequency = ROPE_THETA ** (-2.0 * jnp.arange(half, dtype=F32) / HEAD_DIM)
    angles = own(position).astype(F32)[:, None] * frequency[None, :]
    cosine, sine = jnp.cos(angles), jnp.sin(angles)
    cosine = jnp.concatenate([cosine] * 4, axis=1)
    sine = jnp.concatenate([-sine, sine, -sine, sine], axis=1)
    return aug, qmask, ranges, cosine, sine


def local(
    shards,
    depth,
    tokens,
    cotangent,
    lengths,
    qkv_copy,
    qkv_master,
    qkv_first,
    qkv_second,
    proj_copy,
    proj_master,
    proj_first,
    proj_second,
    gateup_copy,
    gateup_master,
    gateup_first,
    gateup_second,
    down_copy,
    down_master,
    down_first,
    down_second,
    gain_copy,
    gain_master,
    gain_first,
    gain_second,
):
    fast = shards == 4 and depth == 4
    me = lax.axis_index("shard")
    z = lax.axis_index("deep")
    core = lax.axis_index("core")
    count = tokens.shape[0]

    def over_shard(value, flip):
        return lax.ppermute(value, "shard", [(s, s ^ flip) for s in range(shards)])

    def over_core(value):
        return lax.ppermute(value, "core", [(0, 1), (1, 0)])

    def over_deep(value, flip):
        return lax.ppermute(value, "deep", [(s, s ^ flip) for s in range(depth)])

    def all_shards(value):
        return lax.all_to_all(value, "shard", 0, 0, tiled=True)

    def over_deep_by(value, steps):
        return lax.ppermute(value, "deep", [(d, (d + steps) % depth) for d in range(depth)])

    def deep_start(name, parts, axis):
        (kept,) = stage(name + "_over_shard", meta, [split_job([parts], axis, 2, 4)], ())
        return kept[0], over_deep(kept[1], 1)

    def deep_end(name, pair, axis):
        (kept,) = stage(name + "_over_near", meta, [split_job(list(pair), axis, 3)], ())
        far = over_deep(kept[1], 2)
        ((kept,),) = stage(name + "_over_far", meta, [add_job([kept[0], far])], ())
        far = over_deep(kept, 2)
        ((kept,),) = stage(name + "_join_far", meta, [join_job(kept, far, axis, 3)], ())
        near = over_deep(kept, 1)
        ((kept,),) = stage(name + "_join_near", meta, [join_job(kept, near, axis, 2)], ())
        return kept

    def hop(value, flips):
        pairs = [
            (s * depth + d, (s ^ flips[d % 2]) * depth + d)
            for s in range(shards)
            for d in range(depth)
        ]
        return lax.ppermute(value, ("shard", "deep"), pairs)

    def first_hop(piece):
        return hop(piece, (1, 2))

    def second_hop(one):
        return over_deep(one, 1), hop(one, (2, 1))

    def swapped(pieces):
        return tuple(pieces) + tuple(over_core(piece) for piece in pieces)

    aug, qmask, ranges, cosine, sine = row_tables(
        lengths[0], count * shards, me * count, count
    )
    meta = jnp.concatenate([jnp.stack([me, core, z % 2, (z // 2) % 2]).astype(jnp.int32), ranges])

    tokens_t = tokens.T
    cot_t = cotangent.T
    down_t = down_copy.T
    if fast:
        pad = qkv_copy.shape[0] - PIECE
        extra = jnp.pad(gain_copy, ((0, PIECE_ROWS - PIECE - 2), (0, QKV - gain_copy.shape[1])))
        piece = jnp.concatenate(
            [lax.dynamic_slice_in_dim(qkv_copy, core * pad, PIECE), extra], axis=0
        )
        one = first_hop(piece)
        qkv_w = (qkv_copy,) + swapped((one,) + second_hop(one))
        gp_half, proj_wide = cut_call(meta, gateup_copy, proj_copy, piece)
        gp_one = first_hop(gp_half)
        gain = gain_copy
        early = (cosine, sine, aug, qmask, meta, gp_half)
    else:
        qkv_w, proj_w, gateup_w = (
            (lax.all_gather(w, "shard", axis=0, tiled=True),)
            for w in (qkv_copy, proj_copy, gateup_copy)
        )
        proj_w = (jnp.pad(proj_w[0], ((0, 0), (0, 1024 - D))),)
        down_w = (lax.all_gather(down_t, "shard", axis=1, tiled=True),)
        gain = lax.all_gather(gain_copy, "shard", axis=1, tiled=True)
        early = ()

    x_rows, cot_rows, scaled = first_norm_call(tokens_t, cot_t, early)
    n1, gains, kv = kv_call(meta, scaled, gain, cosine, sine, qkv_w)
    kv = [kv] + [over_shard(kv, j) for j in range(1, shards)]
    q, qn = q_call(meta, n1, cosine, sine, qkv_w)
    deps = ()
    if fast:
        (gp_one,) = after((gp_one,), (q, *kv))
        ((down_half,),) = stage("cut_down", meta, [rows_job(down_t, D // 2)], (gp_one,))
        deps = (down_half,)
        gp_two, gp_three = second_hop(gp_one)
        gp_one_oth = over_core(gp_one)
        down_one = first_hop(down_half)
    o, q2 = attend_forward(meta, q, qmask, qn, aug, kv, deps)
    if fast:
        gp_two, gp_three, down_one = after((gp_two, gp_three, down_one), (o,))
        gp_w = (gp_one, gp_two, gp_three, gp_one_oth, over_core(gp_two), over_core(gp_three))
        gateup_w = (gateup_copy,) + gp_w
        proj_w = (proj_wide,) + gp_w
        down_two, down_three = second_hop(down_one)
    mixed, early_own, early_send = mix_call(meta, o, n1, cot_t)
    residual, n2, n2_blocks = residual_call(meta, x_rows, mixed, gains, proj_w)
    if fast:
        down_w = (down_t,) + swapped(after((down_one, down_two, down_three), (residual,)))
    output_t, dn, act, late_own, late_send = mlp_call(
        meta, residual, n2, cot_rows, gateup_w, down_w
    )
    deps = ()
    if fast:
        early_oth = over_core(early_send)
        n2_oth = over_core(n2_blocks)
        late_oth = over_core(late_send)
        act_oth = over_core(act)
        gp_g = gateup_grad_call(meta, n2_blocks, n2_oth, late_own, late_oth, ())
        deps = (gp_g,)
    grad_residual, grad_branch, do, gain_two = norm_back_call(
        meta, residual, dn, cot_rows, mixed, gains, proj_w, deps
    )
    if fast:
        branch_oth = over_core(grad_branch)
        gp_parts = all_shards(gp_g)
        deps = (gp_g,)
    dq, dkv = attend_backward(meta, q2, do, aug, kv, deps)
    deps = ()
    if fast:
        (gp_parts,) = after((gp_parts,), (dq,))
    dkv = all_shards(dkv)
    if fast:
        (gp,) = stage("gateup_over_shard", meta, [split_job([gp_parts], 1, 2, 4)], ())
        gp_recv = over_deep(gp[1], 1)
        dp_g = down_proj_grad_call(
            meta, early_own, early_oth, act, act_oth, grad_branch, branch_oth, (gp[0],)
        )
        (gp,) = stage(
            "gateup_over_near", meta, [split_job([gp[0], gp_recv], 1, 3)], (dp_g,)
        )
        gp_recv = over_deep(gp[1], 2)
        (dp_g,) = after((dp_g,), (dkv, gp[0]))
        dp_parts = all_shards(dp_g)
        deps = (dp_g,)
    grad_joined, input_grad_t = joined_call(
        meta,
        dq,
        cosine,
        sine,
        x_rows,
        gains,
        grad_residual,
        gain_two,
        dkv,
        qkv_w,
        deps,
    )
    rates = (D ** (-0.5), max(HEAD_DIM // 16, 1) ** (-0.5), D ** (-0.5), FF ** (-0.5))
    qkv_states = (qkv_master, qkv_first, qkv_second)
    proj_states = (proj_master, proj_first, proj_second)
    gateup_states = (gateup_master, gateup_first, gateup_second)
    down_states = (down_master.T, down_first.T, down_second.T)
    if fast:
        joined_oth = over_core(grad_joined)
        qkv_g = qkv_grad_call(meta, early_own, early_oth, grad_joined, joined_oth, ())
        qkv_parts = [qkv_g[0]] + [over_shard(qkv_g[j], j) for j in range(1, 4)]
        ((gp,),) = stage("gateup_over_far", meta, [add_job([gp[0], gp_recv])], (qkv_g[0],))
        gp_recv = over_deep(gp, 2)
        ((dp,),) = stage("down_over_shard", meta, [add_job([dp_parts], 4)], (gp,))
        dp_parts = lax.all_to_all(dp, "deep", 0, 0, tiled=True)
        ((gp,),) = stage("gateup_join_far", meta, [join_job(gp, gp_recv, 1, 3)], (dp,))
        gp_recv = over_deep(gp, 1)
        (qkv,) = stage("qkv_over_shard", meta, [split_job(qkv_parts, 0, 2)], (gp,))
        qkv_recv = over_deep(qkv[1], 1)
        ((gp,),) = stage("gateup_join_near", meta, [join_job(gp, gp_recv, 1, 2)], (qkv[0],))
        gp_pair = (gp, over_core(gp))
        ((dp,),) = stage("down_over_deep", meta, [add_job([dp_parts], 4)], (gp,))
        dp_parts = [dp] + [over_deep_by(dp, k) for k in range(1, 4)]
        (qkv,) = stage("qkv_over_near", meta, [split_job([qkv[0], qkv_recv], 0, 3)], (dp,))
        qkv_recv = over_deep(qkv[1], 2)
        rows = gateup_copy.shape[0]
        gateup_new = adamw_call(
            meta,
            gateup_grads,
            gp_pair,
            pl.BlockSpec((48, FF), lambda i, m: (i, 0)),
            gateup_states,
            (48, 2 * FF),
            lambda i, m: (i, 0),
            rows // 48,
            rates[2],
            "gateup_step",
            (qkv[0],),
        )
        ((qkv,),) = stage(
            "qkv_over_far", meta, [add_job([qkv[0], qkv_recv])], (gateup_new[0],)
        )
        qkv_recv = over_deep(qkv, 2)
        ((dp,),) = stage("down_join", meta, [whole_job(dp_parts)], (qkv,))
        dp_pair = (dp, over_core(dp))
        ((qkv,),) = stage("qkv_join_far", meta, [join_job(qkv, qkv_recv, 0, 3)], (dp,))
        qkv_recv = over_deep(qkv, 1)
        down_new = adamw_call(
            meta,
            down_grads,
            dp_pair,
            pl.BlockSpec((D // 4, FF // 4), lambda i, m: (i % 2, 0)),
            down_states,
            (D // 4, FF // 4),
            lambda i, m: (i, 0),
            4,
            rates[3],
            "down_step",
            (qkv,),
        )
        proj_new = adamw_call(
            meta,
            proj_grads,
            dp_pair,
            pl.BlockSpec((DP_ROWS, FF // 4), lambda i, m: (0, 0)),
            proj_states,
            (rows // 2, D),
            lambda i, m: (i, 0),
            2,
            rates[1],
            "proj_step",
            (down_new[0],),
        )
        ((qkv,),) = stage(
            "qkv_join_near", meta, [join_job(qkv, qkv_recv, 0, 2)], (down_new[0],)
        )
        qkv_pair = (qkv, over_core(qkv))
        qkv_new = adamw_call(
            meta,
            qkv_grads,
            qkv_pair,
            pl.BlockSpec((GRAD_ROWS, QKV), lambda i, m: (0, 0)),
            qkv_states,
            (rows // 2, QKV),
            lambda i, m: (i, 0),
            2,
            rates[0],
            "qkv_step",
            (),
        )
        gain_grad = qkv[120:122, : D // shards].astype(F32)
    else:

        def owned(left, right):
            whole = jnp.einsum("ta,tb->ab", left, right, preferred_element_type=F32)
            mine = lax.psum_scatter(whole, "shard", scatter_dimension=0, tiled=True)
            return lax.psum(mine, ("deep", "core"))

        def updated(grad, states, rate):
            return (grad,) + adamw_step(grad, *states, rate, DECAY_RATE)

        grad_gate = jnp.where(core == 0, late_own, late_send)
        grad_up = jnp.where(core == 0, late_send, late_own)
        down_grad_t = owned(act.transpose(1, 0, 2).reshape(count, FF), cotangent).T
        gateup_grad = owned(n2, jnp.concatenate([grad_gate, grad_up], axis=1))
        proj_grad = owned(mixed, grad_branch[:, :D])
        qkv_grad = owned(n1, grad_joined[:count, :QKV])
        gain_sum = lax.psum(
            grad_joined[count : count + 2, :D].astype(F32), ("shard", "deep", "core")
        )
        width = D // shards
        gain_grad = lax.dynamic_slice_in_dim(gain_sum, me * width, width, axis=1)
        qkv_new = updated(qkv_grad, qkv_states, rates[0])
        proj_new = updated(proj_grad, proj_states, rates[1])
        gateup_new = updated(gateup_grad, gateup_states, rates[2])
        down_new = updated(down_grad_t, down_states, rates[3])

    gain_new = adamw_step(gain_grad, gain_master, gain_first, gain_second, 0.5, 0.0)
    return (
        (output_t.T, input_grad_t.T)
        + tuple(qkv_new)
        + tuple(proj_new)
        + tuple(gateup_new)
        + tuple(one.T for one in down_new)
        + (gain_grad,)
        + gain_new
    )


def solution(mesh):
    shards, rep = mesh.shape["shard"], mesh.shape["rep"]
    depth = rep // 2
    fine = Mesh(mesh.devices.reshape(shards, depth, 2), ("shard", "deep", "core"))
    by_token = P(("deep", "core", "shard"), None)
    by_row = P("shard", None)
    by_column = P(None, "shard")
    return jax.shard_map(
        functools.partial(local, shards, depth),
        mesh=fine,
        in_specs=(by_token, by_token, P(("deep", "core"), None)) + (by_row,) * 16 + (by_column,) * 4,
        out_specs=(by_token,) * 2 + (by_row,) * 20 + (by_column,) * 5,
        check_vma=False,
    )
```
